128 devices in a mesh: dp: 4 (over z_hi, core), fsdp: 32 (over z_lo, x, y).
Axes of the slice: x: 4, y: 4, z: 4 (z_hi: 2, z_lo: 2; z = z_hi * 2 + z_lo), core: 2. Of those that a mesh axis runs over, the one named last changes fastest.
Arguments:
- tokens: bfloat16 [2, 128, 128, 896], P(None, ('dp', 'fsdp')), may hold values from -6 to 6
- segments: int32 [2, 128, 128], P(None, ('dp', 'fsdp')), may hold values from 0 to 3, never falling along the last dimension, each value on 1 to 64 neighbouring positions
- w_query: bfloat16 [896, 896], P(('dp', 'fsdp')), may hold values from -0.1875 to 0.1875
- w_key: bfloat16 [896, 128], P(('dp', 'fsdp')), may hold values from -0.1875 to 0.1875
- w_value: bfloat16 [896, 128], P(('dp', 'fsdp')), may hold values from -0.1875 to 0.1875
- w_out: bfloat16 [896, 896], P(('dp', 'fsdp')), may hold values from -0.5 to 0.5
- w_gate: bfloat16 [896, 4864], P(('dp', 'fsdp')), may hold values from -0.1875 to 0.1875
- w_up: bfloat16 [896, 4864], P(('dp', 'fsdp')), may hold values from -0.1875 to 0.1875
- w_down: bfloat16 [4864, 896], P(('dp', 'fsdp')), may hold values from -0.078125 to 0.078125
- gains: bfloat16 [896, 2], P(('dp', 'fsdp')), may hold values from 0.099609375 to 1.8984375
- biases: bfloat16 [1152], P(('dp', 'fsdp')), may hold values from -3 to 3
- cotangent: bfloat16 [2, 128, 128, 896], P(None, ('dp', 'fsdp')), may hold values from -6 to 6
Outputs:
- block_out: bfloat16 [2, 128, 128, 896], P(None, ('dp', 'fsdp'))
- grad_tokens: bfloat16 [2, 128, 128, 896], P(None, ('dp', 'fsdp'))
- grad_query: float32 [896, 896], P(('dp', 'fsdp'))
- grad_key: float32 [896, 128], P(('dp', 'fsdp'))
- grad_value: float32 [896, 128], P(('dp', 'fsdp'))
- grad_outproj: float32 [896, 896], P(('dp', 'fsdp'))
- grad_gate: float32 [896, 4864], P(('dp', 'fsdp'))
- grad_up: float32 [896, 4864], P(('dp', 'fsdp'))
- grad_down: float32 [4864, 896], P(('dp', 'fsdp'))
- grad_gains: float32 [896, 2], P(('dp', 'fsdp'))
- grad_biases: float32 [1152], P(('dp', 'fsdp'))
The draws below stay inside these ranges and needn't reach their ends.
Inputs may be any that keep to these rules, and one draw needn't show every extreme that they name: `segments`: within each sequence the document numbers never fall; each of the 4 documents holds 1 to half of 128 tokens.
All inputs are finite; a program needn't handle non-finite values.
Results may differ from the reference program's by a relative error of at most 0.017.
Values may be sent and summed in bfloat16 or wider, within the bound.
A program may use at most 256 MiB of HBM per device.

```python
import math
import jax
import jax.numpy as jnp
import numpy as np
from jax import lax

D = 896
FF = 4864
H = 14
KVH = 2
HD = 64
SEQ = 128
MICRO = 2
QD = 896
KD = 128
SEQS = 128


def shard_levels(stream_key, extent, pieces, smallest, high):
    level = 1.0
    for axis_at, shards_of in pieces:
        draws = jax.random.uniform(jax.random.fold_in(jax.random.fold_in(stream_key, 6), axis_at), (shards_of,), jnp.float32, smallest / len(pieces), high / len(pieces))
        level = level * jnp.repeat(jnp.exp(draws), extent[axis_at] // shards_of).reshape((-1,) + (1,) * (len(extent) - 1 - axis_at))
    return level


def profile(count, total, bound, skew):
    portions = [(1 << 20) // math.isqrt(standing ** skew) + 1 for standing in range(2, count + 1)]
    rest, given = total - bound - (count - 1), [1] * (count - 1)
    while rest > 0:
        movable = [i for i in range(count - 1) if given[i] < bound]
        pool, left = sum([portions[i] for i in movable]), rest
        for i in movable:
            addition = min(bound - given[i], max(1, left * portions[i] // pool), rest)
            given[i] = given[i] + addition
            rest = rest - addition
    return np.array([bound] + given)


def uneven(rng, count, total, bound, lean):
    if count == 2:
        one = jax.random.randint(rng, (), max(1, total - bound), min(bound, total - 1) + 1)
        return jnp.stack([one, total - one])
    tallies = jnp.asarray(profile(count, total, bound, lean), jnp.int32)
    pairs = (count - 1) // 2
    source_of, receiver = tallies[1:1 + 2 * pairs:2], tallies[2:2 + 2 * pairs:2]
    margin = jnp.minimum(source_of - 1, bound - receiver)
    moved = jax.random.randint(jax.random.fold_in(rng, 1), (pairs,), 0, 1 << 20) % (margin + 1)
    tallies = tallies.at[1:1 + 2 * pairs:2].set(source_of - moved).at[2:2 + 2 * pairs:2].set(receiver + moved)
    return tallies[jax.random.permutation(jax.random.fold_in(rng, 2), count)]


def gaussian(own_key, shape, width, most, split=(), kind=jnp.bfloat16):
    result = width * jax.random.normal(own_key, shape, jnp.float32)
    if split:
        result = result * shard_levels(own_key, shape, split, -0.22, 0.18)
    return jnp.clip(result, -most, most).astype(kind)


def setup_inputs(seed: int = 0) -> dict:
    seeds = jax.random.split(jax.random.key(seed), 13)
    return {
        "tokens": gaussian(seeds[0], (MICRO, SEQS, SEQ, D), 1.0, 6.0, ((1, 128),)),
        "segments": jax.vmap(lambda own: jnp.searchsorted(jnp.cumsum(uneven(own, 4, SEQ, SEQ // 2, 0)), jnp.arange(SEQ), side="right"))(jax.random.split(seeds[1], MICRO * SEQS)).reshape((MICRO, SEQS, SEQ)).astype(jnp.int32),
        "w_query": gaussian(seeds[2], (D, QD), D ** -0.5, 0.1875, ((0, 128),)),
        "w_key": gaussian(seeds[3], (D, KD), D ** -0.5, 0.1875, ((0, 128),)),
        "w_value": gaussian(seeds[4], (D, KD), D ** -0.5, 0.1875, ((0, 128),)),
        "w_out": gaussian(seeds[5], (QD, D), (QD // 8) ** -0.5, 0.5, ((0, 128),)),
        "w_gate": gaussian(seeds[6], (D, FF), D ** -0.5, 0.1875, ((0, 128),)),
        "w_up": gaussian(seeds[7], (D, FF), D ** -0.5, 0.1875, ((0, 128),)),
        "w_down": gaussian(seeds[8], (FF, D), FF ** -0.5, 0.078125, ((0, 128),)),
        "gains": jnp.clip(1.0 + 0.18 * jax.random.normal(seeds[9], (D, 2), jnp.float32), 0.099609375, 1.8984375).astype(jnp.bfloat16),
        "biases": gaussian(seeds[10], (QD + 2 * KD,), 0.5, 3.0, ((0, 128),)),
        "cotangent": gaussian(seeds[11], (MICRO, SEQS, SEQ, D), 1.0, 6.0, ((1, 128),)),
    }


EPSILON = 1e-06
THETA = 1000000.0
NEG_FILL = -1e+30
HIGHEST = lax.Precision.HIGHEST

@jax.custom_vjp
def low(v):
    return lax.optimization_barrier(v.astype(jnp.bfloat16)).astype(jnp.float32)

@jax.custom_vjp
def low_back(v):
    return v

def low_keep(v):
    return (low(v), None)

def low_pass(kept, grad):
    return (grad,)

def back_keep(v):
    return (v, None)

def back_low(kept, grad):
    return (low(grad),)
low.defvjp(low_keep, low_pass)
low_back.defvjp(back_keep, back_low)

def positions(segment_ids):
    last_axis = segment_ids.ndim - 1
    counter = lax.broadcasted_iota(jnp.int32, segment_ids.shape, last_axis)
    starts = jnp.concatenate([jnp.ones(segment_ids.shape[:-1] + (1,), dtype=jnp.bool_), segment_ids[..., 1:] != segment_ids[..., :-1]], axis=last_axis)
    first_index = lax.cummax(jnp.where(starts, counter, 0), axis=last_axis)
    return counter - first_index

def rope_tables(position, head_size):
    half_size = head_size // 2
    exponent = jnp.arange(half_size, dtype=jnp.float32) * (2.0 / head_size)
    inverse = jnp.power(THETA, -exponent)
    angles = position.astype(jnp.float32)[..., None] * inverse
    cosine = jnp.cos(angles)
    sine = jnp.sin(angles)
    return (jnp.concatenate([cosine, cosine], axis=-1), jnp.concatenate([sine, sine], axis=-1))

def rotate(tensor, cosine, sine):
    half_size = tensor.shape[-1] // 2
    turned = jnp.concatenate([-tensor[..., half_size:], tensor[..., :half_size]], axis=-1)
    return tensor * cosine + turned * sine

def matmul_high(left, right):
    return jnp.dot(left, right, precision=HIGHEST)

def layer_forward(weights, source, segment_ids):
    w_query, w_key, w_value, w_out, w_gate, w_up, w_down, gains, biases = weights
    group_size = source.shape[0]
    cosine, sine = rope_tables(positions(segment_ids), HD)
    cosine = cosine[:, :, None, :]
    sine = sine[:, :, None, :]
    inv_one = lax.rsqrt(lax.optimization_barrier(jnp.mean(source * source, axis=-1, keepdims=True)) + EPSILON)
    normed = low(source * inv_one * gains[:, 0])
    query_raw = low_back(matmul_high(normed, w_query) + biases[:QD])
    key_raw = low_back(matmul_high(normed, w_key) + biases[QD:QD + KD])
    value_raw = low_back(matmul_high(normed, w_value) + biases[QD + KD:])
    queries = low(rotate(query_raw.reshape(group_size, SEQ, H, HD), cosine, sine)).reshape(group_size, SEQ, KVH, H // KVH, HD)
    key_rot = low(rotate(key_raw.reshape(group_size, SEQ, KVH, HD), cosine, sine))
    values = low(value_raw).reshape(group_size, SEQ, KVH, HD)
    scores = low_back(jnp.einsum('bqcrd,bkcd->bcrqk', queries, key_rot, precision=HIGHEST) * (1.0 / math.sqrt(HD)))
    row_idx = lax.broadcasted_iota(jnp.int32, (SEQ, SEQ), 0)
    col_idx = lax.broadcasted_iota(jnp.int32, (SEQ, SEQ), 1)
    allowed = jnp.logical_and((col_idx <= row_idx)[None], segment_ids[:, :, None] == segment_ids[:, None, :])[:, None, None, :, :]
    soft_weights = jax.nn.softmax(jnp.where(allowed, scores, NEG_FILL), axis=-1)
    mixed = jnp.einsum('bcrqk,bkcd->bqcrd', low(soft_weights), values, precision=HIGHEST)
    heads_out = low(low_back(mixed)).reshape(group_size, SEQ, QD)
    resid = source + low_back(matmul_high(heads_out, w_out))
    inv_two = lax.rsqrt(lax.optimization_barrier(jnp.mean(resid * resid, axis=-1, keepdims=True)) + EPSILON)
    normed_two = low(resid * inv_two * gains[:, 1])
    gate_act = low_back(matmul_high(normed_two, w_gate))
    up_act = low_back(matmul_high(normed_two, w_up))
    hidden = low(jax.nn.silu(gate_act) * up_act)
    return resid + low_back(matmul_high(hidden, w_down))

def reference(tokens, segments, w_query, w_key, w_value, w_out, w_gate, w_up, w_down, gains, biases, cotangent):
    weights_f32 = (w_query.astype(jnp.float32), w_key.astype(jnp.float32), w_value.astype(jnp.float32), w_out.astype(jnp.float32), w_gate.astype(jnp.float32), w_up.astype(jnp.float32), w_down.astype(jnp.float32), gains.astype(jnp.float32), biases.astype(jnp.float32))
    total_seqs = MICRO * SEQS
    group_size = math.gcd(total_seqs, max(1, 4096 // SEQ))
    block_count = total_seqs // group_size
    inputs = tokens.astype(jnp.float32).reshape(block_count, group_size, SEQ, D)
    seg_blocks = segments.reshape(block_count, group_size, SEQ)

    def forward(weights, source):

        def one_block(block_pair):
            return layer_forward(weights, block_pair[0], block_pair[1])
        return lax.map(jax.checkpoint(one_block), (source, seg_blocks))
    output, pullback = jax.vjp(forward, weights_f32, inputs)
    grad_weights, grad_inputs = pullback(cotangent.astype(jnp.float32).reshape(output.shape))
    out_shape = (MICRO, SEQS, SEQ, D)
    return (output.reshape(out_shape).astype(jnp.bfloat16), grad_inputs.reshape(out_shape).astype(jnp.bfloat16), grad_weights[0], grad_weights[1], grad_weights[2], grad_weights[3], grad_weights[4], grad_weights[5], grad_weights[6], grad_weights[7], grad_weights[8])
```

```python
import functools
import math

import jax
import jax.numpy as jnp
import numpy as np
from jax import lax
from jax.experimental import pallas as pl
from jax.experimental.pallas import tpu as pltpu
from jax.sharding import PartitionSpec as P

HD = 64
EPSILON = 1e-06
THETA = 1000000.0
NEG_FILL = -1e30
MESH = pl.DeviceIdType.MESH
AXES = ("dp", "fsdp")
BF = jnp.bfloat16
F32 = jnp.float32

WCOLS = 7040
DROWS = 48
W_PARTS = ((0, 7), (7, 10), (17, 10), (27, 10), (37, 9), (46, 9))
D_PARTS = ((0, 2), (2, 1), (3, 1), (4, 1), (5, 1), (6, 1))
ORDER = tuple(
    tuple(2 * ((p % 3 + k // 2) % 3) + ((k % 2) ^ (p // 3)) for k in range(6)) for p in range(6)
)


def here():
    dp = lax.axis_index("dp")
    fs = lax.axis_index("fsdp")
    return (fs // 4) % 4, fs % 4, (dp // 2) * 2 + fs // 16, dp % 2


def device(x, y, z, core):
    return ((z // 2) * 2 + core, (z % 2) * 16 + x * 4 + y)


def gray_bits(v):
    high = v // 2
    low = (v % 2 + high) % 2
    return low, high


def flip(v, bit):
    if bit == 0:
        return v + 1 - 2 * (v % 2)
    return 3 - v


def partner(bit):
    x, y, z, core = here()
    axis, low = bit // 2, bit % 2
    place = [x, y, z]
    place[axis] = flip(place[axis], low)
    return device(*place, core)


def sibling():
    x, y, z, core = here()
    return device(x, y, z, 1 - core)


def my_bits():
    x, y, z, _ = here()
    bits = []
    for v in (x, y, z):
        low, high = gray_bits(v)
        bits += [low, high]
    return bits


def slot(bits, full):
    return tuple(slice(None) if b in full else bits[b] for b in (1, 0, 3, 2, 5, 4))


def greet():
    barrier = pltpu.get_barrier_semaphore()
    for b in range(6):
        pl.semaphore_signal(barrier, inc=1, device_id=partner(b), device_id_type=MESH)
    pl.semaphore_signal(barrier, inc=1, device_id=sibling(), device_id_type=MESH)
    pl.semaphore_wait(barrier, 7)


def pieces(wref, dref, index, p):
    wo, wn = W_PARTS[p]
    do, dn = D_PARTS[p]
    return (
        wref.at[index + (slice(None), pl.ds(wo * 128, wn * 128))],
        dref.at[index + (slice(None), pl.ds(do * 128, dn * 128))],
    )


def gather_kernel(pair, down, wide, tall, stage, slab, ss, rs, ws, wr, ds_, dr, ls):
    greet()
    bits = my_bits()
    swap = pltpu.make_async_remote_copy(
        src_ref=pair.at[1], dst_ref=stage, send_sem=ss, recv_sem=rs,
        device_id=sibling(), device_id_type=MESH)
    swap.start()
    mine = slot(bits, ())
    own_down = pltpu.make_async_copy(down, tall.at[mine], ls.at[0])
    own_down.start()
    swap.wait()
    slab[...] = pair[0] + stage[...]
    own_wide = pltpu.make_async_copy(slab, wide.at[mine], ls.at[1])
    own_wide.start()
    own_down.wait()
    own_wide.wait()
    sends = []
    copies = [None] * 6
    for k in range(6):
        for p in range(6):
            order = ORDER[p]
            if k > 0:
                for c in copies[p]:
                    c.wait_recv()
            index = slot(bits, order[:k])
            w, d = pieces(wide, tall, index, p)
            made = []
            for ref, a, b in ((w, ws, wr), (d, ds_, dr)):
                c = pltpu.make_async_remote_copy(
                    src_ref=ref, dst_ref=ref, send_sem=a.at[p, k], recv_sem=b.at[p, k],
                    device_id=partner(order[k]), device_id_type=MESH)
                c.start()
                made.append(c)
            copies[p] = made
            sends += made
    for p in range(6):
        for c in copies[p]:
            c.wait_recv()
    for c in sends:
        c.wait_send()


def gather_all(pair, down):
    dma = pltpu.SemaphoreType.DMA
    return pl.pallas_call(
        gather_kernel,
        out_shape=(
            jax.ShapeDtypeStruct((2,) * 6 + (16, WCOLS), BF),
            jax.ShapeDtypeStruct((2,) * 6 + (DROWS, 896), BF),
        ),
        in_specs=[pl.BlockSpec(memory_space=pltpu.VMEM)] * 2,
        out_specs=[pl.BlockSpec(memory_space=pl.ANY)] * 2,
        scratch_shapes=[
            pltpu.VMEM((16, WCOLS), BF), pltpu.VMEM((16, WCOLS), BF),
            dma, dma, dma((6, 6)), dma((6, 6)), dma((6, 6)), dma((6, 6)), dma((2,)),
        ],
        compiler_params=pltpu.CompilerParams(collective_id=0, has_side_effects=True,
                                             vmem_limit_bytes=32 * 2**20),
    )(pair, down)


def scatter_kernel(gw, gd, own_w, sib_w, out_d, accw, accd, rw, rd, slab,
                   ss, rs, ws, wr, ds_, dr, ls):
    greet()
    bits = my_bits()
    flipped = [1 - b for b in bits]

    def with_bit(k, order, value):
        b = list(bits)
        b[order[k]] = value
        return slot(b, order[:k])

    sends = []
    copies = {}

    def send(k, p):
        order = ORDER[p]
        src = (gw, gd) if k == 5 else (accw, accd)
        srcs = pieces(*src, with_bit(k, order, flipped[order[k]]), p)
        dsts = pieces(rw, rd, with_bit(k, order, bits[order[k]]), p)
        made = []
        for s, d, a, b in zip(srcs, dsts, (ws, ds_), (wr, dr)):
            c = pltpu.make_async_remote_copy(
                src_ref=s, dst_ref=d, send_sem=a.at[p, k], recv_sem=b.at[p, k],
                device_id=partner(order[k]), device_id_type=MESH)
            c.start()
            made.append(c)
        copies[p] = made
        sends.extend(made)

    for p in range(6):
        send(5, p)
    loads = []
    for p in range(6):
        order = ORDER[p]
        index = with_bit(5, order, bits[order[5]])
        for i, (s, d) in enumerate(zip(pieces(gw, gd, index, p), pieces(accw, accd, index, p))):
            c = pltpu.make_async_copy(s, d, ls.at[i, p])
            c.start()
            loads.append(c)
    for c in loads:
        c.wait()

    def add(k, p):
        order = ORDER[p]
        (wo, wn), (do, dn) = W_PARTS[p], D_PARTS[p]

        def body(n, carry):
            b = list(bits)
            for i in range(k):
                b[order[i]] = (n // 2**i) % 2
            here_at = slot(b, ())
            b[order[k]] = flipped[order[k]]
            there_at = slot(b, ())
            for acc, got, o, m in ((accw, rw, wo, wn), (accd, rd, do, dn)):
                cols = (slice(None), pl.ds(o * 128, m * 128))
                acc[here_at + cols] = (acc[here_at + cols].astype(F32)
                                       + got[there_at + cols].astype(F32)).astype(BF)
            return carry

        lax.fori_loop(0, 2**k, body, 0)

    for k in range(5, -1, -1):
        for p in range(6):
            for c in copies[p]:
                c.wait_recv()
            if k > 0:
                add(k, p)
                send(k - 1, p)
    mine = slot(bits, ())
    for p in range(6):
        order = ORDER[p]
        (wo, wn), (do, dn) = W_PARTS[p], D_PARTS[p]
        other = with_bit(0, order, flipped[order[0]])
        cols = (slice(None), pl.ds(wo * 128, wn * 128))
        total = accw[mine + cols].astype(F32) + rw[other + cols].astype(F32)
        own_w[cols] = total
        slab[cols] = total.astype(BF)
        cols = (slice(None), pl.ds(do * 128, dn * 128))
        out_d[cols] = accd[mine + cols].astype(F32) + rd[other + cols].astype(F32)
    swap = pltpu.make_async_remote_copy(
        src_ref=slab, dst_ref=sib_w, send_sem=ss, recv_sem=rs,
        device_id=sibling(), device_id_type=MESH)
    swap.start()
    for c in sends:
        c.wait_send()
    swap.wait()


def scatter_all(gw, gd):
    dma = pltpu.SemaphoreType.DMA
    return pl.pallas_call(
        scatter_kernel,
        out_shape=(
            jax.ShapeDtypeStruct((16, WCOLS), F32),
            jax.ShapeDtypeStruct((16, WCOLS), BF),
            jax.ShapeDtypeStruct((DROWS, 896), F32),
        ),
        in_specs=[pl.BlockSpec(memory_space=pl.ANY)] * 2,
        out_specs=[pl.BlockSpec(memory_space=pltpu.VMEM)] * 3,
        scratch_shapes=[
            pltpu.VMEM((2,) * 6 + (16, WCOLS), BF), pltpu.VMEM((2,) * 6 + (DROWS, 896), BF),
            pltpu.VMEM((2,) * 6 + (16, WCOLS), BF), pltpu.VMEM((2,) * 6 + (DROWS, 896), BF),
            pltpu.VMEM((16, WCOLS), BF),
            dma, dma, dma((6, 6)), dma((6, 6)), dma((6, 6)), dma((6, 6)), dma((2, 6)),
        ],
        compiler_params=pltpu.CompilerParams(collective_id=1, has_side_effects=True,
                                             vmem_limit_bytes=56 * 2**20),
    )(gw, gd)


def positions(segment_ids):
    counter = lax.broadcasted_iota(jnp.int32, segment_ids.shape, 1)
    starts = jnp.concatenate(
        [jnp.ones((segment_ids.shape[0], 1), jnp.bool_), segment_ids[:, 1:] != segment_ids[:, :-1]],
        axis=1)
    return counter - lax.cummax(jnp.where(starts, counter, 0), axis=1)


def rope_tables(position):
    exponent = jnp.arange(HD // 2, dtype=F32) * (2.0 / HD)
    angles = position.astype(F32)[..., None] * jnp.power(THETA, -exponent)
    cosine, sine = jnp.cos(angles), jnp.sin(angles)
    return jnp.concatenate([cosine] * 2, -1), jnp.concatenate([sine] * 2, -1)


def rotate(v, cosine, sine):
    turned = jnp.concatenate([-v[..., HD // 2:], v[..., :HD // 2]], axis=-1)
    return v * cosine + turned * sine


def rotate_back(v, cosine, sine):
    scaled = v * sine
    turned = jnp.concatenate([scaled[..., HD // 2:], -scaled[..., :HD // 2]], axis=-1)
    return v * cosine + turned


def dot(a, b, **kw):
    return jnp.dot(a, b, preferred_element_type=F32, **kw)


def dot_t(a, b):
    return jnp.einsum("nf,df->nd", a, b, preferred_element_type=F32)


def outer(a, b):
    return jnp.einsum("nd,nf->df", a, b, preferred_element_type=F32)


def norm_back(grad, source, inv, gain):
    scaled = grad * gain
    return inv * scaled - source * inv**3 * jnp.mean(scaled * source, axis=-1, keepdims=True)


def slot_numbers():
    gray = (0, 1, 3, 2)
    slots = np.zeros(128, np.int32)
    for n in range(128):
        dp, fs = n // 32, n % 32
        x, y, z, core = fs // 4 % 4, fs % 4, (dp // 2) * 2 + fs // 16, dp % 2
        slots[n] = ((gray[x] * 4 + gray[y]) * 4 + gray[z]) * 2 + core
    return slots


def shards(tokens, segments, w_query, w_key, w_value, w_out, w_gate, w_up, w_down, gains, biases,
           cotangent):
    core = lax.axis_index("dp") % 2
    swap = ((0, 1), (1, 0), (2, 3), (3, 2))
    slots = slot_numbers()
    spread_np = np.zeros((896, 1024), np.float32)
    for d in range(896):
        spread_np[d, slots[d // 7] * 8 + d % 7] = 1.0
    spread = jnp.asarray(spread_np, BF)

    def half(w, c):
        return lax.dynamic_index_in_dim(w.reshape(7, 2, 2, 1216), c, 2, keepdims=False).reshape(7, 2432)

    small = jnp.zeros((8, 128), BF).at[:7, :2].set(gains).at[0, 16:25].set(biases)[:7]
    rest = [w_query, w_key, w_value, w_out, small]

    def build(c):
        rows = jnp.concatenate([half(w_gate, c), half(w_up, c)] + rest, axis=1)
        return lax.dynamic_update_slice(jnp.zeros((16, WCOLS), BF), rows, (8 * core, 0))

    pair = jnp.stack([build(core), build(1 - core)])
    wide, tall = gather_all(pair, jnp.pad(w_down, ((0, DROWS - 38), (0, 0))))
    wide = wide.reshape(1024, WCOLS)
    wg, wu = wide[:, :2432], wide[:, 2432:4864]
    wqkv, wo = wide[:, 4864:6016], wide[:, 6016:6912]
    small = wide[:, 6912:]
    order = np.zeros(64, np.int32)
    gray = (0, 1, 3, 2)
    for s in range(64):
        z, x, y = s // 16, s // 4 % 4, s % 4
        order[s] = (gray[x] * 4 + gray[y]) * 4 + gray[z]
    back = np.argsort(order)
    wd = tall.reshape(64, DROWS, 896)[order, :38].reshape(2432, 896)
    gain = dot(spread, small[:, :2])
    bias = small.reshape(128, 8, 128)[slots, 0, 16:25].reshape(1152).astype(F32)

    seqs, length, width = 2, 128, 896
    rows = 256
    seg = segments.reshape(seqs, length)
    source = tokens.astype(F32).reshape(rows, width)
    inv_one = lax.rsqrt(jnp.mean(source * source, axis=-1, keepdims=True) + EPSILON)
    normed = (source * inv_one * gain[:, 0]).astype(BF)
    normed_s = dot(normed, spread).astype(BF)
    qkv = dot(normed_s, wqkv) + bias
    cosine, sine = rope_tables(positions(seg))
    cosine, sine = cosine.reshape(rows, 1, HD), sine.reshape(rows, 1, HD)
    queries = rotate(qkv[:, :896].reshape(rows, 14, HD), cosine, sine).astype(BF).reshape(
        seqs, length, 2, 7, HD)
    keys = rotate(qkv[:, 896:1024].reshape(rows, 2, HD), cosine, sine).astype(BF).reshape(
        seqs, length, 2, HD)
    values = qkv[:, 1024:].astype(BF).reshape(seqs, length, 2, HD)
    r = lax.broadcasted_iota(jnp.int32, (length, length), 0)
    c = lax.broadcasted_iota(jnp.int32, (length, length), 1)
    allowed = ((c <= r)[None] & (seg[:, :, None] == seg[:, None, :]))[:, None, None]
    scale = 1.0 / math.sqrt(HD)
    scores = jnp.einsum("bqcrd,bkcd->bcrqk", queries, keys, preferred_element_type=F32) * scale
    scores = jnp.where(allowed, scores, NEG_FILL)
    peak = jnp.max(scores, axis=-1, keepdims=True)
    e = jnp.exp(scores - peak)
    soft = e / jnp.sum(e, axis=-1, keepdims=True)
    softb = soft.astype(BF)
    mixed = jnp.einsum("bcrqk,bkcd->bqcrd", softb, values, preferred_element_type=F32).astype(
        BF).reshape(rows, 896)
    mixed_s = dot(mixed, spread).astype(BF)
    resid = source + dot(mixed_s, wo)
    inv_two = lax.rsqrt(jnp.mean(resid * resid, axis=-1, keepdims=True) + EPSILON)
    normed_two = (resid * inv_two * gain[:, 1]).astype(BF)
    dy = cotangent.reshape(rows, width)

    mine = jnp.concatenate([normed_two, dy], axis=1)
    other = lax.ppermute(mine, "dp", swap)
    both = jnp.concatenate([mine, other], axis=0)
    a2, eb = both[:, :896], both[:, 896:]
    a2s = dot(a2, spread).astype(BF)
    g = dot(a2s, wg)
    u = dot(a2s, wu)
    sig = jax.nn.sigmoid(g)
    hidden = (g * sig * u).astype(BF)
    part = dot(hidden, wd)
    dm = dot_t(eb, wd)
    dg = (dm * u * sig * (1.0 + g * (1.0 - sig))).astype(BF)
    du = (dm * g * sig).astype(BF)
    grad_d = outer(hidden, eb)
    grad_g = outer(a2s, dg)
    grad_u = outer(a2s, du)
    da2_s = dot_t(dg, wg) + dot_t(du, wu)
    sums = jnp.concatenate([part, da2_s], axis=1)
    sums = sums[:rows] + lax.ppermute(sums[rows:], "dp", swap)
    output = resid + sums[:, :896]
    unspread = spread.astype(F32).T
    da2 = dot(sums[:, 896:], unspread, precision=lax.Precision.HIGHEST)

    gain_two_grad = jnp.sum(da2 * resid * inv_two, axis=0)
    dy1 = dy.astype(F32) + norm_back(da2, resid, inv_two, gain[:, 1])
    f = dy1.astype(BF)
    grad_o = outer(mixed_s, f)
    do = dot(dot_t(f, wo).astype(BF), spread.T).astype(BF).reshape(seqs, length, 2, 7, HD)
    dp = jnp.einsum("bqcrd,bkcd->bcrqk", do, values, preferred_element_type=F32)
    ds = (soft * (dp - jnp.sum(soft * dp, axis=-1, keepdims=True))).astype(BF)
    dq = jnp.einsum("bcrqk,bkcd->bqcrd", ds, keys, preferred_element_type=F32) * scale
    dk = jnp.einsum("bcrqk,bqcrd->bkcd", ds, queries, preferred_element_type=F32) * scale
    dv = jnp.einsum("bcrqk,bqcrd->bkcd", softb, do, preferred_element_type=F32)
    dq0 = rotate_back(dq.reshape(rows, 14, HD), cosine, sine).reshape(rows, 896)
    dk0 = rotate_back(dk.reshape(rows, 2, HD), cosine, sine).reshape(rows, 128)
    dqkv = jnp.concatenate([dq0, dk0, dv.reshape(rows, 128)], axis=1).astype(BF)
    grad_qkv = outer(normed_s, dqkv)
    grad_bias = jnp.sum(dqkv.astype(F32), axis=0)
    da1 = dot(dot_t(dqkv, wqkv), unspread, precision=lax.Precision.HIGHEST)
    gain_one_grad = jnp.sum(da1 * source * inv_one, axis=0)
    grad_in = dy1 + norm_back(da1, source, inv_one, gain[:, 0])

    gain_grad = jnp.stack([gain_one_grad, gain_two_grad], axis=1).reshape(128, 7, 2)
    inverse = np.argsort(slots)
    small = jnp.zeros((128, 8, 128), F32)
    small = small.at[:, :7, :2].set(gain_grad[inverse])
    small = small.at[:, 0, 16:25].set(grad_bias.reshape(128, 9)[inverse]).reshape(1024, 128)
    gw = jnp.concatenate([grad_g, grad_u, grad_qkv, grad_o, small], axis=1).astype(BF)
    gd = jnp.pad(grad_d.astype(BF).reshape(64, 38, 896)[back], ((0, 0), (0, DROWS - 38), (0, 0)))
    own, sib, own_d = scatter_all(gw.reshape((2,) * 6 + (16, WCOLS)), gd.reshape((2,) * 6 + (DROWS, 896)))
    own = lax.dynamic_slice(own, (8 * core, 0), (7, WCOLS))
    sib = lax.dynamic_slice(sib, (8 * core, 0), (7, WCOLS)).astype(F32)

    def whole(a):
        first = jnp.where(core == 0, own[:, a:a + 2432], sib[:, a:a + 2432]).reshape(7, 2, 1216)
        second = jnp.where(core == 0, sib[:, a:a + 2432], own[:, a:a + 2432]).reshape(7, 2, 1216)
        return jnp.stack([first, second], axis=2).reshape(7, 4864)

    both = own[:, 4864:] + sib[:, 4864:]
    return (
        output.astype(BF).reshape(tokens.shape),
        grad_in.astype(BF).reshape(tokens.shape),
        both[:, :896], both[:, 896:1024], both[:, 1024:1152], both[:, 1152:2048],
        whole(0), whole(2432), own_d[:38],
        both[:, 2048:2050], both[0, 2064:2073],
    )


def solution(mesh):
    row = P(AXES, None)
    batch = P(None, AXES, None, None)
    return jax.shard_map(
        shards, mesh=mesh,
        in_specs=(batch, P(None, AXES, None)) + (row,) * 8 + (P(AXES), batch),
        out_specs=(batch, batch) + (row,) * 8 + (P(AXES),),
        check_vma=False,
    )
```

```python
import functools

import jax
import jax.numpy as jnp
import numpy as np
from jax import lax
from jax.experimental import pallas as pl
from jax.experimental.pallas import tpu as pltpu
from jax.sharding import PartitionSpec as P

EPSILON = 1e-06
THETA = 1000000.0
NEG_FILL = -1e30
MESH = pl.DeviceIdType.MESH
AXES = ("dp", "fsdp")
BF = jnp.bfloat16
F32 = jnp.float32
GRAY = (0, 1, 3, 2)

FFN_WAVES = (
    ((0, 2), (2, 2), (4, 2), (6, 2), (8, 2), (10, 2)),
    ((12, 2), (14, 2), (16, 2), (18, 2), (20, 2), (22, 2)),
    ((24, 3), (27, 2), (29, 2), (31, 3), (34, 2), (36, 2)),
)
ATT_WAVE = ((38, 2), (40, 2), (42, 2), (44, 2), (46, 2), (48, 2))
DOWN_WAVE = ((0, 4), (4, 3), (7, 4), (11, 3), (14, 4), (18, 3))
WAVES = (ATT_WAVE, DOWN_WAVE) + FFN_WAVES
ATT, DOWN, FFN = 0, 1, 2
UNITS, TALL = 50, 21
ORDER = tuple(
    tuple(2 * ((p % 3 + k // 2) % 3) + ((k % 2) ^ (p // 3)) for k in range(6)) for p in range(6)
)


def here():
    dp = lax.axis_index("dp")
    fs = lax.axis_index("fsdp")
    return (fs // 4) % 4, fs % 4, (dp // 2) * 2 + fs // 16, dp % 2


def device(x, y, z, core):
    return ((z // 2) * 2 + core, (z % 2) * 16 + x * 4 + y)


def gray_bits(v):
    high = v // 2
    low = (v % 2 + high) % 2
    return low, high


def flip(v, bit):
    if bit == 0:
        return v + 1 - 2 * (v % 2)
    return 3 - v


def partner(bit):
    x, y, z, core = here()
    axis, low = bit // 2, bit % 2
    place = [x, y, z]
    place[axis] = flip(place[axis], low)
    return device(*place, core)


def sibling():
    x, y, z, core = here()
    return device(x, y, z, 1 - core)


def my_bits():
    x, y, z, _ = here()
    bits = []
    for v in (x, y, z):
        low, high = gray_bits(v)
        bits += [low, high]
    return bits


DIMS = (1, 0, 3, 2, 5, 4)


def slot(bits, full, skip=None):
    return tuple(slice(None) if b in full else bits[b] for b in DIMS if b != skip)


def dot(a, b):
    return lax.dot_general(a, b, (((1,), (0,)), ((), ())), preferred_element_type=F32)


def dot_t(a, b):
    return lax.dot_general(a, b, (((1,), (1,)), ((), ())), preferred_element_type=F32)


def layer_kernel(
    pair, down, x_own, e_own, seg_own, spread, spread_o, pack, unpack, brow, freq,
    out_ref, gtok_ref, own_ref, sib_ref,
    u_buf, t_buf, u_got, t_got, wd, x_all, e_all, seg_all, stage, a1s, a2s, a2st, qkv, o_s,
    y1, ypart, yrec, da2, darec, mrec, arec, cosine, sine, gain, bias, slab,
    ag_recv, rs_recv, sends_sem, credit, sib_send, sib_recv, loc_sem,
):
    _, _, _, core = here()
    bits = my_bits()
    flipped = [1 - b for b in bits]
    sib = sibling()
    peers = [partner(b) for b in range(6)]

    barrier = pltpu.get_barrier_semaphore()
    for b in range(6):
        pl.semaphore_signal(barrier, inc=1, device_id=peers[b], device_id_type=MESH)
    pl.semaphore_signal(barrier, inc=1, device_id=sib, device_id_type=MESH)
    pl.semaphore_wait(barrier, 7)

    def to_sibling(src, dst, i):
        return pltpu.make_async_remote_copy(
            src_ref=src, dst_ref=dst, send_sem=sib_send.at[i], recv_sem=sib_recv.at[i],
            device_id=sib, device_id_type=MESH)

    swap_pair = to_sibling(pair.at[1], stage, 0)
    swap_pair.start()
    own = pl.ds(pl.multiple_of(core * 256, 256), 256)
    swap_seg = to_sibling(seg_own, seg_all.at[core], 1)
    swap_x = to_sibling(x_own, x_all.at[own], 2)
    swap_e = to_sibling(e_own, e_all.at[own], 3)
    for c in (swap_seg, swap_x, swap_e):
        c.start()
    locals_ = [
        pltpu.make_async_copy(seg_own, seg_all.at[core], loc_sem.at[0]),
        pltpu.make_async_copy(x_own, x_all.at[own], loc_sem.at[1]),
        pltpu.make_async_copy(e_own, e_all.at[own], loc_sem.at[2]),
    ]
    for c in locals_:
        c.start()

    def bufs(w):
        return (t_buf, t_got) if w == DOWN else (u_buf, u_got)

    def ag_copy(w, k, p):
        start, n = WAVES[w][p]
        order = ORDER[p]
        ref = bufs(w)[0].at[(pl.ds(start, n),) + slot(bits, order[:k])]
        return pltpu.make_async_remote_copy(
            src_ref=ref, dst_ref=ref, send_sem=sends_sem.at[w, p, k],
            recv_sem=ag_recv.at[w, p, k], device_id=peers[order[k]], device_id_type=MESH)

    def ag(w, k):
        for p in range(6):
            if k > 0:
                ag_copy(w, k - 1, p).wait_recv()
            ag_copy(w, k, p).start()

    def ag_done(w):
        for p in range(6):
            ag_copy(w, 5, p).wait_recv()
        for p in range(6):
            for k in range(6):
                ag_copy(w, k, p).wait_send()

    def rs_copy(w, k, p):
        start, n = WAVES[w][p]
        order = ORDER[p]
        acc, got = bufs(w)
        b = list(bits)
        b[order[k]] = flipped[order[k]]
        src = acc.at[(pl.ds(start, n),) + slot(b, order[:k])]
        if k == 5:
            dst = got.at[pl.ds(start, n)]
        else:
            b = list(bits)
            b[order[5]] = flipped[order[5]]
            dst = acc.at[(pl.ds(start, n),) + slot(b, order[:k])]
        return pltpu.make_async_remote_copy(
            src_ref=src, dst_ref=dst, send_sem=sends_sem.at[w, p, k],
            recv_sem=rs_recv.at[w, p, k], device_id=peers[order[k]], device_id_type=MESH)

    def rs_add(w, k, p):
        start, n = WAVES[w][p]
        order = ORDER[p]
        acc, got = bufs(w)
        here_at = slot(bits, order[:k])
        b = list(bits)
        b[order[5]] = flipped[order[5]]
        b[order[k]] = flipped[order[k]]
        there_at = slot(b, order[:k])

        def one(u):
            add = got[u] if k == 5 else acc[(u,) + there_at]
            acc[(u,) + here_at] = acc[(u,) + here_at] + add

        if k >= 3:
            @pl.loop(0, n)
            def _(i):
                one(start + i)
        else:
            for i in range(n):
                one(start + i)

    def rs(w, k):
        if k == 4:
            for p in range(6):
                rs_copy(w, 5, p).wait_send()
            for b in range(6):
                pl.semaphore_signal(credit.at[w, b], inc=1, device_id=peers[b],
                                    device_id_type=MESH)
        for p in range(6):
            if k < 5:
                rs_copy(w, k + 1, p).wait_recv()
                rs_add(w, k + 1, p)
            if k == 4:
                pl.semaphore_wait(credit.at[w, ORDER[p][4]], 1)
            rs_copy(w, k, p).start()

    def rs_end(w):
        acc, _ = bufs(w)
        base = UNITS if w == DOWN else 0
        for p in range(6):
            start, n = WAVES[w][p]
            order = ORDER[p]
            rs_copy(w, 0, p).wait_recv()
            b = list(bits)
            b[order[5]] = flipped[order[5]]
            b[order[0]] = flipped[order[0]]
            units = pl.ds(start, n)
            total = (acc[(units,) + slot(bits, ())].astype(F32)
                     + acc[(units,) + slot(b, ())].astype(F32))
            own_ref[pl.ds(base + start, n)] = total
            if w != DOWN:
                slab[units] = total.astype(BF)
        for p in range(6):
            for k in range(5):
                rs_copy(w, k, p).wait_send()

    def last_swap(w):
        start = WAVES[w][0][0]
        n = sum(m for _, m in WAVES[w])
        return to_sibling(slab.at[pl.ds(start, n)], sib_ref.at[pl.ds(start, n)], 16 + w)

    def rows(s):
        return pl.ds(pl.multiple_of(s * 128, 128), 128)

    def unit(u):
        return u_buf[u].reshape(1024, 128)

    mine = slot(bits, ())
    t_buf[(slice(None),) + mine] = down[...]
    swap_pair.wait()
    u_buf[(slice(None),) + mine] = pair[0] + stage[...]
    ag(ATT, 0)
    ag(DOWN, 0)
    ag(ATT, 1)
    ag(FFN, 0)
    ag(ATT, 2)
    ag(DOWN, 1)
    ag(ATT, 3)
    ag(DOWN, 2)
    ag(ATT, 4)
    for c in locals_:
        c.wait()
    for c in (swap_seg, swap_x, swap_e):
        c.wait()
    ag(ATT, 5)

    causal = (lax.broadcasted_iota(jnp.int32, (128, 128), 1)
              <= lax.broadcasted_iota(jnp.int32, (128, 128), 0))

    def allowed(s):
        line = seg_all[s // 2, pl.ds(s % 2, 1), :]
        across = jnp.broadcast_to(line, (128, 128))
        return jnp.logical_and(causal, across == across.T)

    for s in range(4):
        place = jnp.sum(allowed(s).astype(F32), axis=1, keepdims=True) - 1.0
        angle = place * freq[0:1, :]
        cosine[rows(s), :] = jnp.cos(angle)
        sine[rows(s), :] = jnp.sin(angle)
    ag(DOWN, 3)
    ag(FFN, 1)
    ag_done(ATT)
    ag(DOWN, 4)
    ag(FFN, 2)

    small = unit(42).T
    gain[...] = dot_t(small[64:80], spread[...])[0:8]
    hit = (lax.broadcasted_iota(jnp.int32, (1024, 640), 0) == brow[core, 0:1, :]).astype(BF)
    picked = dot(small[80:96], hit)
    choose = lax.broadcasted_iota(jnp.int32, (16, 640), 0) == brow[core, 1:2, :]
    bias[...] = jnp.broadcast_to(
        jnp.sum(jnp.where(choose, picked, 0.0), axis=0, keepdims=True), (8, 640))

    def inv_root(v):
        return lax.rsqrt(jnp.mean(v * v, axis=-1, keepdims=True) + EPSILON)

    @pl.loop(0, 4)
    def _(s):
        v = x_all[rows(s), :].astype(F32)
        a1 = (v * inv_root(v) * gain[0:1, :]).astype(BF)
        a1s[rows(s), :] = dot(a1, spread[...]).astype(BF)

    ag(FFN + 1, 0)
    ag(FFN, 3)
    lane = lax.broadcasted_iota(jnp.int32, (128, 640), 1)
    first = lane % 64 < 32
    turns = lane < 512

    def wide(ref, s):
        return jnp.concatenate([ref[rows(s), :]] * 5, axis=1)

    w_qkv = jnp.concatenate([unit(38 + i) for i in range(5)], axis=1)
    for s in range(4):
        raw = dot(a1s[rows(s), :], w_qkv) + bias[0:1, :]
        turned = jnp.where(first, -pltpu.roll(raw, 608, 1), pltpu.roll(raw, 32, 1))
        turned = raw * wide(cosine, s) + turned * wide(sine, s)
        qkv[rows(s), :] = jnp.where(turns, turned, raw).astype(BF)
    ag(DOWN, 5)
    ag(FFN + 1, 1)

    def heads(v):
        return jnp.concatenate([v[:, 64 * h:64 * h + 64] for h in range(7)], axis=0)

    def unheads(v):
        return jnp.concatenate([v[128 * h:128 * h + 128, :] for h in range(7)], axis=1)

    def attend(s):
        q7 = heads(qkv[rows(s), 0:448])
        k = qkv[rows(s), 448:512]
        v = qkv[rows(s), 512:576]
        score = dot_t(q7, k) * 0.125
        ok = allowed(s)
        score = jnp.where(jnp.concatenate([ok] * 7, axis=0), score, NEG_FILL)
        e = jnp.exp(score - jnp.max(score, axis=-1, keepdims=True))
        soft = e / jnp.sum(e, axis=-1, keepdims=True)
        return q7, k, v, soft

    def w_out():
        return jnp.concatenate(
            [u_buf[43 + i, :, :, :, :, core].reshape(512, 128) for i in range(7)], axis=1)

    def y_swap(s):
        return to_sibling(ypart.at[rows(s)], yrec.at[rows(s)], 4 + s)

    @pl.loop(0, 4)
    def _(s):
        _, _, v, soft = attend(s)
        o = unheads(dot(soft.astype(BF), v)).astype(BF)
        os = dot(o, spread_o[core]).astype(BF)
        o_s[rows(s), :] = os
        ypart[rows(s), :] = dot(os, w_out())
        y_swap(s).start()
    ag(FFN, 4)
    ag(FFN + 1, 2)

    ag_done(DOWN)
    ag(FFN, 5)
    ag(FFN + 1, 3)
    ag(FFN + 2, 0)

    def slab_place(s):
        z, x, y = s // 16, s // 4 % 4, s % 4
        b = []
        for v in (x, y, z):
            low, high = gray_bits(v)
            b += [low, high]
        return slot(b, ())

    @pl.loop(0, 8)
    def _(g):
        lines = []
        for i in range(8):
            at = slab_place(g * 8 + i)
            for r in range(3):
                lines.append(jnp.concatenate(
                    [t_buf[(3 * c + r,) + at] for c in range(7)], axis=1))
        block = jnp.concatenate(lines, axis=0)
        wd[pl.ds(pl.multiple_of(g * 304, 16), 304), :] = dot(pack[...], block).astype(BF)

    ag(FFN + 1, 4)
    ag(FFN + 2, 1)

    @pl.loop(0, 4)
    def _(s):
        y_swap(s).wait()
        v = x_all[rows(s), :].astype(F32) + (ypart[rows(s), :] + yrec[rows(s), :])
        y1[rows(s), :] = v
        a2 = (v * inv_root(v) * gain[1:2, :]).astype(BF)
        a2s[rows(s), :] = dot(a2, spread[...]).astype(BF)
        ypart[rows(s), :] = jnp.zeros((128, 896), F32)
        da2[rows(s), :] = jnp.zeros((128, 1024), F32)

    ag(FFN + 1, 5)
    ag(FFN + 2, 2)
    a2st[...] = a2s[...].T
    ag(FFN + 2, 3)

    def ffn(gates, ups, row, n):
        width = 128 * n
        w = jnp.concatenate([unit(i) for i in gates + ups], axis=1)
        both = dot(a2s[...], w)
        g, u = both[:, :width], both[:, width:]
        at = pl.ds(pl.multiple_of(row, 128), width)
        w_d = wd[at, :]
        dm = dot_t(e_all[...], w_d)
        sig = 1.0 / (1.0 + jnp.exp(-g))
        silu = g * sig
        m = (silu * u).astype(BF)
        dg = (dm * u * sig * (1.0 + g * (1.0 - sig))).astype(BF)
        du = (dm * silu).astype(BF)
        dgu = jnp.concatenate([dg, du], axis=1)
        ypart[...] += dot(m, w_d)
        da2[...] += dot_t(dgu, w)
        wd[at, :] = dot(m.T, e_all[...]).astype(BF)
        for part, places in ((dg, gates), (du, ups)):
            grads = dot(a2st[...], part).astype(BF)
            for i, place in enumerate(places):
                u_buf[place] = grads[:, 128 * i:128 * i + 128].reshape((2,) * 6 + (16, 128))

    ag_done(FFN)

    @pl.loop(0, 9)
    def _(i):
        def at(t, *acts):
            @pl.when(i == t)
            def _():
                for f, a in acts:
                    f(*a)

        at(1, (ag, (FFN + 2, 4)))
        at(2, (ag, (FFN + 2, 5)))
        at(3, (rs, (FFN, 5)), (ag_done, (FFN + 1,)))
        at(4, (rs, (FFN, 4)))
        at(5, (rs, (FFN, 3)))
        at(6, (rs, (FFN + 1, 5)), (ag_done, (FFN + 2,)))
        at(7, (rs, (FFN, 2)), (rs, (FFN + 1, 4)))
        at(8, (rs, (FFN, 1)), (rs, (FFN + 1, 3)))
        g = 12 * (i // 3) + 2 * (i % 3) + (i + 1) // 8
        u = g + 6 + i // 6
        ffn([g, g + 1], [u, u + 1], i * 256, 2)

    ffn([26], [33], 2304, 1)
    rs(FFN + 2, 5)
    rs(FFN, 0)
    rs(FFN + 1, 2)

    other = pl.ds(pl.multiple_of((1 - core) * 256, 256), 256)
    out_swap = to_sibling(ypart.at[other], mrec, 8)
    out_swap.start()

    def unspread(v):
        high = v.astype(BF)
        low = (v - high.astype(F32)).astype(BF)
        return dot_t(high, spread[...]) + dot_t(low, spread[...])

    def da_swap(s):
        return to_sibling(yrec.at[rows(s)], darec.at[rows(s)], 9 + s)

    @pl.loop(0, 4)
    def _(s):
        yrec[rows(s), :] = unspread(da2[rows(s), :])
        da_swap(s).start()

    @pl.loop(0, 8)
    def _(g):
        block = dot(unpack[...], wd[pl.ds(pl.multiple_of(g * 304, 16), 304), :]).astype(BF)
        for i in range(8):
            at = slab_place(g * 8 + i)
            for r in range(3):
                for c in range(7):
                    t_buf[(3 * c + r,) + at] = block[48 * i + 16 * r:48 * i + 16 * r + 16,
                                                     128 * c:128 * c + 128]

    rs(DOWN, 5)
    rs_end(FFN)
    last_swap(FFN).start()
    rs(FFN + 1, 1)
    rs(FFN + 2, 4)
    out_swap.wait()
    for s in range(2):
        at = pl.ds(pl.multiple_of(core * 256 + 128 * s, 128), 128)
        out_ref[pl.ds(128 * s, 128), :] = (
            y1[at, :] + (ypart[at, :] + mrec[pl.ds(128 * s, 128), :])).astype(BF)

    gain_grads = gain.at[pl.ds(2, 2)]
    gain_grads[...] = jnp.zeros((2, 896), F32)

    @pl.loop(0, 4)
    def _(s):
        da_swap(s).wait()
        da = yrec[rows(s), :] + darec[rows(s), :]
        v = y1[rows(s), :]
        r = inv_root(v)

        @pl.when(s // 2 == core)
        def _():
            gain[3:4, :] += jnp.sum(da * v * r, axis=0, keepdims=True)

        w = da * gain[1:2, :]
        dy = (e_all[rows(s), :].astype(F32) + r * w
              - v * (r * r * r) * jnp.mean(w * v, axis=-1, keepdims=True))
        darec[rows(s), :] = dy
        f = dy.astype(BF)
        a2s[rows(s), 0:896] = f
        ds_ = dot_t(f, w_out()).astype(BF)
        a2s[rows(s), 896:1024] = jnp.zeros((128, 128), BF)
        a2st[rows(s), 0:448] = dot_t(ds_, spread_o[core]).astype(BF)

    rs(DOWN, 4)
    rs(FFN + 1, 0)
    rs(FFN + 2, 3)
    o_grad = dot(o_s[...].T, a2s[:, 0:896]).astype(BF)
    for i in range(7):
        part = o_grad[:, 128 * i:128 * i + 128].reshape((2,) * 5 + (16, 128))
        u_buf[43 + i, :, :, :, :, core] = part
        u_buf[43 + i, :, :, :, :, 1 - core] = jnp.zeros_like(part)
    rs_end(FFN + 1)
    last_swap(FFN + 1).start()
    rs(DOWN, 3)
    rs(FFN + 2, 2)

    bias[...] = jnp.zeros((8, 640), F32)

    @pl.loop(0, 4)
    def _(s):
        q7, k, v, soft = attend(s)
        do7 = heads(a2st[rows(s), 0:448])
        dp = dot_t(do7, v)
        ds_ = (soft * (dp - jnp.sum(soft * dp, axis=-1, keepdims=True))).astype(BF)
        dq = unheads(dot(ds_, k)) * 0.125
        dk = dot(ds_.T, q7) * 0.125
        dv = dot(soft.astype(BF).T, do7)
        raw = jnp.concatenate([dq, dk, dv, jnp.zeros((128, 64), F32)], axis=1)
        scaled = raw * wide(sine, s)
        turned = jnp.where(first, pltpu.roll(scaled, 608, 1), -pltpu.roll(scaled, 32, 1))
        grad = jnp.where(turns, raw * wide(cosine, s) + turned, raw).astype(BF)
        qkv[rows(s), :] = grad
        bias[0:1, :] += jnp.sum(grad.astype(F32), axis=0, keepdims=True)

    rs(DOWN, 2)
    rs(FFN + 2, 1)
    w_qkv = jnp.concatenate([unit(38 + i) for i in range(5)], axis=1)
    da2[...] = dot_t(qkv[...], w_qkv)

    @pl.loop(0, 4)
    def _(s):
        yrec[rows(s), :] = unspread(da2[rows(s), :])

    a_swap = to_sibling(yrec.at[other], arec, 13)
    a_swap.start()
    rs(DOWN, 1)
    rs(FFN + 2, 0)
    a2st[...] = a1s[...].T
    for i in range(4):
        part = dot(a2st[...], qkv[:, 128 * i:128 * i + 128])
        u_buf[38 + i] = part.astype(BF).reshape((2,) * 6 + (16, 128))
    a_swap.wait()
    for s in range(2):
        at = pl.ds(pl.multiple_of(core * 256 + 128 * s, 128), 128)
        da = yrec[at, :] + arec[pl.ds(128 * s, 128), :]
        v = x_all[at, :].astype(F32)
        r = inv_root(v)
        gain[2:3, :] += jnp.sum(da * v * r, axis=0, keepdims=True)
        w = da * gain[0:1, :]
        gtok_ref[pl.ds(128 * s, 128), :] = (
            darec[at, :] + r * w
            - v * (r * r * r) * jnp.mean(w * v, axis=-1, keepdims=True)).astype(BF)
    top = dot(jnp.concatenate([gain[2:4, :], jnp.zeros((14, 896), F32)], axis=0).astype(BF),
              spread[...])
    spot = jnp.where(choose, jnp.broadcast_to(bias[0:1, :], (16, 640)), 0.0).astype(BF)
    hit = (lax.broadcasted_iota(jnp.int32, (1024, 640), 0) == brow[core, 0:1, :]).astype(BF)
    low = dot_t(spot, hit)
    small = jnp.concatenate(
        [jnp.zeros((64, 1024), F32), top, low, jnp.zeros((32, 1024), F32)], axis=0).T
    part = dot(a2st[...], qkv[:, 512:640]) + small
    u_buf[42] = part.astype(BF).reshape((2,) * 6 + (16, 128))
    rs(ATT, 5)
    rs(DOWN, 0)
    rs_end(FFN + 2)
    last_swap(FFN + 2).start()
    rs(ATT, 4)
    rs_end(DOWN)
    for k in (3, 2, 1, 0):
        rs(ATT, k)
    rs_end(ATT)
    last_swap(ATT).start()
    for w in (ATT, FFN, FFN + 1, FFN + 2):
        last_swap(w).wait()


def layer(pair, down, x, e, seg, spread, spread_o, pack, unpack, brow, freq):
    dma = pltpu.SemaphoreType.DMA
    vm = pltpu.VMEM
    return pl.pallas_call(
        layer_kernel,
        out_shape=(
            jax.ShapeDtypeStruct((256, 896), BF),
            jax.ShapeDtypeStruct((256, 896), BF),
            jax.ShapeDtypeStruct((UNITS + TALL, 16, 128), F32),
            jax.ShapeDtypeStruct((UNITS, 16, 128), BF),
        ),
        in_specs=[pl.BlockSpec(memory_space=vm)] * 2 + [pl.BlockSpec(memory_space=pl.ANY)] * 2
        + [pl.BlockSpec(memory_space=vm)] * 7,
        out_specs=[pl.BlockSpec(memory_space=vm)] * 4,
        scratch_shapes=[
            vm((UNITS,) + (2,) * 6 + (16, 128), BF), vm((TALL,) + (2,) * 6 + (16, 128), BF),
            vm((UNITS,) + (2,) * 5 + (16, 128), BF), vm((TALL,) + (2,) * 5 + (16, 128), BF),
            vm((2432, 896), BF), vm((512, 896), BF), vm((512, 896), BF), vm((2, 8, 128), F32),
            vm((UNITS, 16, 128), BF), vm((512, 1024), BF), vm((512, 1024), BF),
            vm((1024, 512), BF), vm((512, 640), BF), vm((512, 512), BF),
            vm((512, 896), F32), vm((512, 896), F32), vm((512, 896), F32), vm((512, 1024), F32),
            vm((512, 896), F32), vm((256, 896), F32), vm((256, 896), F32), vm((512, 128), F32), vm((512, 128), F32),
            vm((8, 896), F32), vm((8, 640), F32), vm((UNITS, 16, 128), BF),
            dma((5, 6, 6)), dma((5, 6, 6)), dma((5, 6, 6)), pltpu.SemaphoreType.REGULAR((5, 6)),
            dma((21,)), dma((21,)), dma((3,)),
        ],
        compiler_params=pltpu.CompilerParams(collective_id=0, has_side_effects=True,
                                             vmem_limit_bytes=60 * 2**20),
    )(pair, down, x, e, seg, spread, spread_o, pack, unpack, brow, freq)


def constants():
    slots = np.zeros(128, np.int32)
    for n in range(128):
        dp, fs = n // 32, n % 32
        x, y, z, core = fs // 4 % 4, fs % 4, (dp // 2) * 2 + fs // 16, dp % 2
        slots[n] = ((GRAY[x] * 4 + GRAY[y]) * 4 + GRAY[z]) * 2 + core
    spread = np.zeros((896, 1024), np.float32)
    for d in range(896):
        spread[d, slots[d // 7] * 8 + d % 7] = 1.0
    spread_o = np.zeros((2, 448, 512), np.float32)
    for c in range(2):
        part = spread[448 * c:448 * c + 448].reshape(448, 16, 2, 32)
        spread_o[c] = part[:, :, c].reshape(448, 512)
    unpack = np.zeros((384, 304), np.float32)
    for a in range(8):
        for r in range(38):
            unpack[48 * a + r, 38 * a + r] = 1.0
    brow = np.full((2, 8, 640), -1, np.int32)
    for c in range(2):
        for i in range(576):
            if i < 448:
                nat = 448 * c + i
            elif i < 512:
                nat = 896 + 64 * c + i - 448
            else:
                nat = 1024 + 64 * c + i - 512
            brow[c, 0, i] = slots[nat // 9] * 8
            brow[c, 1, i] = nat % 9
    freq = THETA ** (-2.0 * (np.arange(128) % 32) / 64.0)
    freq = np.broadcast_to(freq.astype(np.float32), (8, 128))
    return (jnp.asarray(spread, BF), jnp.asarray(spread_o, BF), jnp.asarray(unpack.T, BF),
            jnp.asarray(unpack, BF), jnp.asarray(brow), jnp.asarray(freq))


def shards(tokens, segments, w_query, w_key, w_value, w_out, w_gate, w_up, w_down, gains, biases,
           cotangent):
    core = lax.axis_index("dp") % 2

    def pick(w, parts, c):
        cut = w.reshape(7, -1, 2, w.shape[1] // (2 * parts))
        return lax.dynamic_index_in_dim(cut, c, 2, keepdims=False).reshape(7, -1)

    small = jnp.concatenate(
        [gains, jnp.zeros((7, 14), BF), jnp.pad(biases[None], ((0, 6), (0, 0))),
         jnp.zeros((7, 39), BF)], axis=1)

    def build(c):
        g, u = pick(w_gate, 2, c), pick(w_up, 2, c)
        cols = [g[:, :768], u[:, :768], g[:, 768:1536], u[:, 768:1536],
                g[:, 1536:1792], g[:, 2304:], g[:, 1792:2304],
                u[:, 1536:1792], u[:, 2304:], u[:, 1792:2304],
                pick(w_query, 1, c), pick(w_key, 1, c), pick(w_value, 1, c), small, w_out]
        cols = jnp.concatenate(cols, axis=1)
        cols = lax.dynamic_update_slice(jnp.zeros((16, UNITS * 128), BF), cols, (8 * core, 0))
        return cols.reshape(16, UNITS, 128).transpose(1, 0, 2)

    pair = jnp.stack([build(core), build(1 - core)])
    down = jnp.pad(w_down, ((0, 10), (0, 0))).reshape(3, 16, 7, 128).transpose(2, 0, 1, 3)
    seg = jnp.pad(segments.reshape(2, 128).astype(F32), ((0, 6), (0, 0)))
    block_out, grad_in, own, sib = layer(
        pair, down.reshape(TALL, 16, 128), tokens.reshape(256, 896), cotangent.reshape(256, 896),
        seg, *constants())

    def lines(a):
        a = lax.dynamic_slice(a, (0, 8 * core, 0), (UNITS, 7, 128))
        return a.transpose(1, 0, 2).reshape(7, UNITS * 128).astype(F32)

    mine, theirs = lines(own[:UNITS]), lines(sib)
    zero, one = jnp.where(core == 0, mine, theirs), jnp.where(core == 0, theirs, mine)

    def columns(a, up):
        o = 128 * up
        return [a[:, 6 * o:6 * o + 768], a[:, 1536 + 6 * o:2304 + 6 * o]] + [
            a[:, 3072 + 7 * o:3072 + 7 * o + 896]]

    def whole(up):
        both = []
        for a in (zero, one):
            f0, f1, f2 = columns(a, up)
            f2 = jnp.concatenate([f2[:, :256], f2[:, 384:], f2[:, 256:384]], axis=1)
            both.append(jnp.concatenate([f0, f1, f2], axis=1).reshape(7, 2, 1216))
        return jnp.stack(both, axis=2).reshape(7, 4864)

    def halves(a, n):
        return jnp.concatenate([zero[:, a:a + n], one[:, a:a + n]], axis=1)

    q0 = 38 * 128
    both = mine[:, q0 + 576:] + theirs[:, q0 + 576:]
    grad_d = own[UNITS:].reshape(7, 48, 128)[:, :38].transpose(1, 0, 2).reshape(38, 896)
    return (
        block_out.reshape(tokens.shape), grad_in.reshape(tokens.shape),
        halves(q0, 448), halves(q0 + 448, 64), halves(q0 + 512, 64), both[:, 64:960],
        whole(0), whole(1), grad_d, both[:, :2], both[0, 16:25],
    )


def solution(mesh):
    row = P(AXES, None)
    batch = P(None, AXES, None, None)
    return jax.shard_map(
        shards, mesh=mesh,
        in_specs=(batch, P(None, AXES, None)) + (row,) * 8 + (P(AXES), batch),
        out_specs=(batch, batch) + (row,) * 8 + (P(AXES),),
        check_vma=False,
    )
```

```python
import functools

import jax
import jax.numpy as jnp
import numpy as np
from jax import lax
from jax.experimental import pallas as pl
from jax.experimental.pallas import tpu as pltpu
from jax.sharding import PartitionSpec as P

EPSILON = 1e-06
THETA = 1000000.0
NEG_FILL = -1e30
MESH = pl.DeviceIdType.MESH
AXES = ("dp", "fsdp")
BF = jnp.bfloat16
F32 = jnp.float32
GRAY = (0, 1, 3, 2)

BULK = ((0, 8), (8, 8), (16, 7), (23, 8), (31, 7), (38, 7))
TALLS = ((0, 4), (4, 3), (7, 4), (11, 3), (14, 4), (18, 3))
WAVES = (
    ((7, 1), (14, 2), (22, 1), (30, 1), (37, 1), (44, 1)),
    TALLS,
    ((0, 2), (8, 2), (16, 2), (23, 2), (31, 2), (38, 2)),
    ((2, 2), (10, 2), (18, 2), (25, 2), (33, 2), (40, 2)),
    ((4, 3), (12, 2), (20, 2), (27, 3), (35, 2), (42, 2)),
)
EARLY = ((0, 4), (8, 4), (16, 4), (23, 4), (31, 4), (38, 4))
LATE = ((4, 4), (12, 4), (20, 3), (27, 4), (35, 3), (42, 3))
OUT, DOWN, FFN = 0, 1, 2
OUT_UNITS = (7, 14, 15, 22, 30, 37, 44)
HEAD = ((45, 2), (47, 2), (49, 1))
UNITS, TALL, QKV = 50, 21, 45


def pair_units(starts, last):
    return tuple(starts[j % 6 // 2] + 2 * (j // 6) + j % 2 for j in range(18)) + (last,)


GATE_UNITS = pair_units((0, 8, 16), 6)
UP_UNITS = pair_units((23, 31, 38), 29)
GATE_AT, UP_AT, Q_AT, K_AT, V_AT, O_AT, S_AT, RAW = (
    0, 4864, 9728, 10624, 10752, 10880, 11776, 11904)
ORDER = tuple(
    tuple(2 * ((p % 3 + k // 2) % 3) + ((k % 2) ^ (p // 3)) for k in range(6)) for p in range(6)
)


def here():
    dp = lax.axis_index("dp")
    fs = lax.axis_index("fsdp")
    return (fs // 4) % 4, fs % 4, (dp // 2) * 2 + fs // 16, dp % 2


def device(x, y, z, core):
    return ((z // 2) * 2 + core, (z % 2) * 16 + x * 4 + y)


def gray_bits(v):
    high = v // 2
    low = (v % 2 + high) % 2
    return low, high


def flip(v, bit):
    if bit == 0:
        return v + 1 - 2 * (v % 2)
    return 3 - v


def partner(bit):
    x, y, z, core = here()
    axis, low = bit // 2, bit % 2
    place = [x, y, z]
    place[axis] = flip(place[axis], low)
    return device(*place, core)


def sibling():
    x, y, z, core = here()
    return device(x, y, z, 1 - core)


def my_bits():
    x, y, z, _ = here()
    bits = []
    for v in (x, y, z):
        low, high = gray_bits(v)
        bits += [low, high]
    return bits


DIMS = (1, 0, 3, 2, 5, 4)


def slot(bits, full):
    return tuple(slice(None) if b in full else bits[b] for b in DIMS)


def far(axis):
    x, y, z, core = here()
    place = [x, y, z]
    place[axis] = 3 - flip(place[axis], 0)
    return device(*place, core)


def dot(a, b):
    return lax.dot_general(a, b, (((1,), (0,)), ((), ())), preferred_element_type=F32)


def dot_t(a, b):
    return lax.dot_general(a, b, (((1,), (1,)), ((), ())), preferred_element_type=F32)


def layer_kernel(
    w_query, w_key, w_value, w_out_, w_gate, w_up, w_down, gains, biases, segments,
    x_own, e_own, spread_h, spread_o_h, pack_h, unpack_h, brow, freq,
    out_ref, gtok_ref, own_ref, sib_ref,
    u_buf, t_buf, u_got, t_got, wd, x_all, e_all, seg_all, stage, a1s, a2s, a2st, qkv, o_s,
    y1, ypart, yrec, da2, darec, mrec, arec, cosine, sine, gain, bias, slab,
    raw, last_rows, own_s, send_s, seg_own, spread, spread_o, pack, unpack,
    h_got0, h_got1, h_got2, ag_small_recv, rs_small_recv, small_send, ag_big_recv, rs_big_recv,
    big_send, ag_head_recv, rs_head_recv, head_send, credit, sib_send, sib_recv, loc_sem,
):
    _, _, _, core = here()
    bits = my_bits()
    flipped = [1 - b for b in bits]
    sib = sibling()
    peers = [partner(b) for b in range(6)]
    across_ = [far(a) for a in range(3)]

    barrier = pltpu.get_barrier_semaphore()
    for d in peers + across_ + [sib]:
        pl.semaphore_signal(barrier, inc=1, device_id=d, device_id_type=MESH)

    def to_sibling(src, dst, i):
        return pltpu.make_async_remote_copy(
            src_ref=src, dst_ref=dst, send_sem=sib_send.at[i], recv_sem=sib_recv.at[i],
            device_id=sib, device_id_type=MESH)

    own = pl.ds(pl.multiple_of(core * 256, 256), 256)
    locals_ = [
        pltpu.make_async_copy(a, b, loc_sem.at[i]) for i, (a, b) in enumerate((
            (x_own, x_all.at[own]), (e_own, e_all.at[own]), (spread_h, spread),
            (spread_o_h, spread_o), (pack_h, pack), (unpack_h, unpack)))]
    for c in locals_:
        c.start()

    raw[...] = jnp.zeros((8, RAW), F32)
    for ref, a in ((w_gate, GATE_AT), (w_up, UP_AT), (w_query, Q_AT), (w_key, K_AT),
                   (w_value, V_AT), (w_out_, O_AT), (gains, S_AT)):
        raw[0:7, a:a + ref.shape[1]] = ref[...].astype(F32)
    raw[0:1, S_AT + 16:S_AT + 25] = biases[...].astype(F32)
    seg_own[...] = jnp.zeros((8, 128), F32)
    seg_own[0:2, :] = segments[...].astype(F32)
    last_rows[...] = jnp.zeros((16, 896), F32)
    last_rows[0:6, :] = w_down[32:38, :].astype(F32)

    def lanes(first, second):
        if second == first + 64:
            return raw[:, first:first + 128]
        return jnp.concatenate([raw[:, first:first + 64], raw[:, second:second + 64]], axis=1)

    def hidden_at(base, c, h):
        return base + 1216 * (2 * (h // 19) + c) + 64 * (h % 19)

    def head_at(c, h):
        return (Q_AT + 448 * c + 64 * h, K_AT + 64 * c, V_AT + 64 * c, S_AT)[max(0, h - 6)]

    def units_of(c):
        for table, base in ((GATE_UNITS, GATE_AT), (UP_UNITS, UP_AT)):
            for j, place in enumerate(table):
                yield place, lanes(hidden_at(base, c, 2 * j), hidden_at(base, c, 2 * j + 1))
        for j in range(5):
            yield QKV + j, lanes(head_at(c, 2 * j), head_at(c, 2 * j + 1))
        for j, place in enumerate(OUT_UNITS):
            yield place, raw[:, O_AT + 128 * j:O_AT + 128 * j + 128]

    def fill(dst, other):
        for c in range(2):
            @pl.when(core == c)
            def _():
                zero = jnp.zeros((8, 128), F32)
                for place, v in units_of(1 - c if other else c):
                    tile = jnp.concatenate([zero, v] if c else [v, zero], axis=0)
                    dst[place] = tile.astype(BF)

    fill(send_s, True)
    pl.semaphore_wait(barrier, 10)
    swap_pair = to_sibling(send_s, stage, 0)
    swap_pair.start()
    swap_seg = to_sibling(seg_own, seg_all.at[core], 1)
    swap_x = to_sibling(x_own, x_all.at[own], 2)
    swap_e = to_sibling(e_own, e_all.at[own], 3)
    for c in (swap_seg, swap_x, swap_e):
        c.start()
    fill(own_s, False)
    seg_all[core] = seg_own[...]

    def remote(src, dst, send, recv, to):
        return pltpu.make_async_remote_copy(
            src_ref=src, dst_ref=dst, send_sem=send, recv_sem=recv, device_id=to,
            device_id_type=MESH)

    BOTH = ((u_buf, BULK), (t_buf, TALLS))

    def bufs(w):
        return (t_buf, t_got) if w == DOWN else (u_buf, u_got)

    def small_copy(k, p, i):
        buf, parts = BOTH[i]
        ref = buf.at[(pl.ds(*parts[p]),) + slot(bits, ORDER[p][:k])]
        return remote(ref, ref, small_send.at[k, p, i], ag_small_recv.at[k, p, i],
                      peers[ORDER[p][k]])

    def ag_small(k):
        for i in range(2):
            for p in range(6):
                if k > 0:
                    small_copy(k - 1, p, i).wait_recv()
                small_copy(k, p, i).start()

    def ag_small_end():
        for i in range(2):
            for p in range(6):
                small_copy(3, p, i).wait_recv()
        for i in range(2):
            for p in range(6):
                for k in range(4):
                    small_copy(k, p, i).wait_send()

    def ag_copy(w, k, p):
        order = ORDER[p]
        ref = bufs(w)[0].at[(pl.ds(*WAVES[w][p]),) + slot(bits, order[:k])]
        return remote(ref, ref, big_send.at[w, k - 4, p], ag_big_recv.at[w, k - 4, p],
                      peers[order[k]])

    def ag(w, k):
        for p in range(6):
            if k == 5:
                ag_copy(w, 4, p).wait_recv()
            ag_copy(w, k, p).start()

    def ag_done(w):
        for p in range(6):
            ag_copy(w, 5, p).wait_recv()
        for p in range(6):
            for k in (4, 5):
                ag_copy(w, k, p).wait_send()

    def given(k, p, *more):
        b = list(bits)
        for j in (k,) + more:
            b[ORDER[p][j]] = flipped[ORDER[p][j]]
        return slot(b, ORDER[p][:k])

    def rs_copy(w, k, p):
        acc, got = bufs(w)
        units = pl.ds(*WAVES[w][p])
        dst = got.at[units]
        if k < 5:
            b = list(bits)
            b[ORDER[p][5]] = flipped[ORDER[p][5]]
            dst = acc.at[(units,) + slot(b, ORDER[p][:k])]
        return remote(acc.at[(units,) + given(k, p)], dst, big_send.at[w, k - 4, p],
                      rs_big_recv.at[w, k - 4, p], peers[ORDER[p][k]])

    def rs_add(acc, got, part, k, p):
        start, n = part
        mine_ = slot(bits, ORDER[p][:k])

        def one(u):
            add = got[u] if k == 5 else acc[(u,) + given(k, p, 5)]
            acc[(u,) + mine_] = acc[(u,) + mine_] + add

        if k >= 2:
            @pl.loop(0, n)
            def _(i):
                one(start + i)
        else:
            for i in range(n):
                one(start + i)

    def rs(w, k):
        acc, got = bufs(w)
        if k == 4:
            for p in range(6):
                rs_copy(w, 5, p).wait_send()
            for b in range(6):
                pl.semaphore_signal(credit.at[w, b], inc=1, device_id=peers[b],
                                    device_id_type=MESH)
        for p in range(6):
            if k == 4:
                rs_copy(w, 5, p).wait_recv()
                rs_add(acc, got, WAVES[w][p], 5, p)
                pl.semaphore_wait(credit.at[w, ORDER[p][4]], 1)
            rs_copy(w, k, p).start()

    def rs_fold(w):
        acc, got = bufs(w)
        for p in range(6):
            rs_copy(w, 4, p).wait_recv()
            rs_add(acc, got, WAVES[w][p], 4, p)

    GROUPS = (((u_buf, EARLY),), ((u_buf, LATE), (t_buf, TALLS)))

    def rs_small_copy(g, k, p, i):
        buf, parts = GROUPS[g][i]
        units = pl.ds(*parts[p])
        b = list(bits)
        b[ORDER[p][5]] = flipped[ORDER[p][5]]
        return remote(buf.at[(units,) + given(k, p)], buf.at[(units,) + slot(b, ORDER[p][:k])],
                      small_send.at[k, p, g + i], rs_small_recv.at[k, p, g + i],
                      peers[ORDER[p][k]])

    def rs_small(g, k):
        if k == 3:
            for b in range(6):
                pl.semaphore_signal(credit.at[5 + g, b], inc=1, device_id=peers[b],
                                    device_id_type=MESH)
        for i in range(len(GROUPS[g])):
            for p in range(6):
                if k == 3:
                    if i == 0:
                        pl.semaphore_wait(credit.at[5 + g, ORDER[p][3]], 1)
                else:
                    rs_small_copy(g, k + 1, p, i).wait_recv()
                    rs_add(GROUPS[g][i][0], None, GROUPS[g][i][1][p], k + 1, p)
                rs_small_copy(g, k, p, i).start()

    def rs_small_end(g):
        for i, (buf, parts) in enumerate(GROUPS[g]):
            for p in range(6):
                start, n = parts[p]
                units = pl.ds(start, n)
                rs_small_copy(g, 0, p, i).wait_recv()
                total = (buf[(units,) + slot(bits, ())].astype(F32)
                         + buf[(units,) + given(0, p, 5)].astype(F32))
                own_ref[pl.ds(start + i * UNITS, n)] = total
                if i == 0:
                    slab[units] = total.astype(BF)

    def rs_sent():
        for p in range(6):
            for w in range(5):
                rs_copy(w, 4, p).wait_send()
            for g, i in ((0, 0), (1, 0), (1, 1)):
                for k in range(4):
                    rs_small_copy(g, k, p, i).wait_send()

    def turned_bits(axis, j):
        b = list(bits)
        for i in ((0,), (1,), (0, 1))[j]:
            b[2 * axis + i] = flipped[2 * axis + i]
        return b

    def head_to(axis, j):
        return across_[axis] if j == 2 else peers[2 * axis + j]

    def head_full(r, stage):
        return [2 * ((r + i) % 3) + j for i in range(stage) for j in range(2)]

    def head_copy(stage, r, j):
        ref = u_buf.at[(pl.ds(*HEAD[r]),) + slot(bits, head_full(r, stage))]
        return remote(ref, ref, head_send.at[stage, r, j], ag_head_recv.at[stage, r, j],
                      head_to((r + stage) % 3, j))

    def ag_head(stage):
        for r in range(3):
            for j in range(3):
                if stage > 0:
                    head_copy(stage - 1, r, j).wait_recv()
            for j in range(3):
                head_copy(stage, r, j).start()

    def ag_head_done():
        for r in range(3):
            for j in range(3):
                head_copy(2, r, j).wait_recv()
        for r in range(3):
            for j in range(3):
                for stage in range(3):
                    head_copy(stage, r, j).wait_send()

    def head_rs_copy(stage, r, j):
        start, n = HEAD[r]
        axis = (r + stage) % 3
        src = u_buf.at[(pl.ds(start, n),) + slot(turned_bits(axis, j), head_full(r, stage))]
        dst = (h_got0, h_got1, h_got2)[stage].at[j, pl.ds(start - QKV, n)]
        return remote(src, dst, head_send.at[stage, r, j], rs_head_recv.at[stage, r, j],
                      head_to(axis, j))

    def head_sum(stage, r):
        start, n = HEAD[r]
        for j in range(3):
            head_rs_copy(stage, r, j).wait_recv()
        got = (h_got0, h_got1, h_got2)[stage]
        totals = []
        for i in range(n):
            at = (start + i,) + slot(bits, head_full(r, stage))
            total = u_buf[at].astype(F32)
            for j in range(3):
                total = total + got[j, start + i - QKV].astype(F32)
            if stage:
                u_buf[at] = total.astype(BF)
            else:
                own_ref[start + i] = total
                slab[start + i] = total.astype(BF)

    def rs_head(stage):
        for r in range(3):
            if stage < 2:
                head_sum(stage + 1, r)
            for j in range(3):
                head_rs_copy(stage, r, j).start()

    def rs_head_end():
        for r in range(3):
            head_sum(0, r)
        for r in range(3):
            for j in range(3):
                for stage in range(3):
                    head_rs_copy(stage, r, j).wait_send()

    def last_swap(i):
        at = pl.ds(0, QKV) if i == 0 else pl.ds(QKV, UNITS - QKV)
        return to_sibling(slab.at[at], sib_ref.at[at], 16 + i)

    def rows(s):
        return pl.ds(pl.multiple_of(s * 128, 128), 128)

    def unit(u):
        return u_buf[u].reshape(1024, 128)

    mine = slot(bits, ())
    for c in range(7):
        cols = slice(128 * c, 128 * c + 128)
        for r in range(2):
            t_buf[(3 * c + r,) + mine] = w_down[16 * r:16 * r + 16, cols]
        t_buf[(3 * c + 2,) + mine] = last_rows[:, cols].astype(BF)
    swap_pair.wait()
    u_buf[(slice(None),) + mine] = own_s[...] + stage[...]
    ag_head(0)
    ag_small(0)
    ag_head(1)
    ag_small(1)
    ag_head(2)
    for c in locals_:
        c.wait()
    for c in (swap_seg, swap_x, swap_e):
        c.wait()
    ag_small(2)

    causal = (lax.broadcasted_iota(jnp.int32, (128, 128), 1)
              <= lax.broadcasted_iota(jnp.int32, (128, 128), 0))

    def allowed(s):
        line = seg_all[s // 2, pl.ds(s % 2, 1), :]
        across = jnp.broadcast_to(line, (128, 128))
        return jnp.logical_and(causal, across == across.T)

    for s in range(4):
        place = jnp.sum(allowed(s).astype(F32), axis=1, keepdims=True) - 1.0
        angle = place * freq[0:1, :]
        cosine[rows(s), :] = jnp.cos(angle)
        sine[rows(s), :] = jnp.sin(angle)
    ag_small(3)
    ag_head_done()

    small = unit(49).T
    gain[...] = dot_t(small[64:80], spread[...])[0:8]
    hit = (lax.broadcasted_iota(jnp.int32, (1024, 640), 0) == brow[core, 0:1, :]).astype(BF)
    picked = dot(small[80:96], hit)
    choose = lax.broadcasted_iota(jnp.int32, (16, 640), 0) == brow[core, 1:2, :]
    bias[...] = jnp.broadcast_to(
        jnp.sum(jnp.where(choose, picked, 0.0), axis=0, keepdims=True), (8, 640))

    def inv_root(v):
        return lax.rsqrt(jnp.mean(v * v, axis=-1, keepdims=True) + EPSILON)

    @pl.loop(0, 4)
    def _(s):
        v = x_all[rows(s), :].astype(F32)
        a1 = (v * inv_root(v) * gain[0:1, :]).astype(BF)
        a1s[rows(s), :] = dot(a1, spread[...]).astype(BF)

    ag_small_end()
    ag(OUT, 4)
    ag(DOWN, 4)
    lane = lax.broadcasted_iota(jnp.int32, (128, 640), 1)
    first = lane % 64 < 32
    turns = lane < 512

    def wide(ref, s):
        return jnp.concatenate([ref[rows(s), :]] * 5, axis=1)

    w_qkv = jnp.concatenate([unit(QKV + i) for i in range(5)], axis=1)
    for s in range(4):
        raw = dot(a1s[rows(s), :], w_qkv) + bias[0:1, :]
        turned = jnp.where(first, -pltpu.roll(raw, 608, 1), pltpu.roll(raw, 32, 1))
        turned = raw * wide(cosine, s) + turned * wide(sine, s)
        qkv[rows(s), :] = jnp.where(turns, turned, raw).astype(BF)
    ag(OUT, 5)
    ag(FFN, 4)
    ag_done(OUT)
    ag(DOWN, 5)

    def heads(v):
        return jnp.concatenate([v[:, 64 * h:64 * h + 64] for h in range(7)], axis=0)

    def unheads(v):
        return jnp.concatenate([v[128 * h:128 * h + 128, :] for h in range(7)], axis=1)

    def attend(s):
        q7 = heads(qkv[rows(s), 0:448])
        k = qkv[rows(s), 448:512]
        v = qkv[rows(s), 512:576]
        score = dot_t(q7, k) * 0.125
        ok = allowed(s)
        score = jnp.where(jnp.concatenate([ok] * 7, axis=0), score, NEG_FILL)
        e = jnp.exp(score - jnp.max(score, axis=-1, keepdims=True))
        soft = e / jnp.sum(e, axis=-1, keepdims=True)
        return q7, k, v, soft

    def w_out():
        return jnp.concatenate(
            [u_buf[OUT_UNITS[i], :, :, :, :, core].reshape(512, 128) for i in range(7)], axis=1)

    def y_swap(s):
        return to_sibling(ypart.at[rows(s)], yrec.at[rows(s)], 4 + s)

    def tick(now, t, *acts):
        @pl.when(now == t)
        def _():
            for f, a in acts:
                f(*a)

    @pl.loop(0, 4)
    def _(s):
        tick(s, 1, (ag, (FFN, 5)))
        tick(s, 2, (ag, (FFN + 1, 4)))
        tick(s, 3, (ag, (FFN + 1, 5)))
        _, _, v, soft = attend(s)
        o = unheads(dot(soft.astype(BF), v)).astype(BF)
        os = dot(o, spread_o[core]).astype(BF)
        o_s[rows(s), :] = os
        ypart[rows(s), :] = dot(os, w_out())
        y_swap(s).start()

    ag_done(DOWN)
    ag(FFN + 2, 4)

    def slab_place(s):
        z, x, y = s // 16, s // 4 % 4, s % 4
        b = []
        for v in (x, y, z):
            low, high = gray_bits(v)
            b += [low, high]
        return slot(b, ())

    @pl.loop(0, 8)
    def _(g):
        lines = []
        for i in range(8):
            at = slab_place(g * 8 + i)
            for r in range(3):
                lines.append(jnp.concatenate(
                    [t_buf[(3 * c + r,) + at] for c in range(7)], axis=1))
        block = jnp.concatenate(lines, axis=0)
        wd[pl.ds(pl.multiple_of(g * 304, 16), 304), :] = dot(pack[...], block).astype(BF)

    ag(FFN + 2, 5)

    @pl.loop(0, 4)
    def _(s):
        y_swap(s).wait()
        v = x_all[rows(s), :].astype(F32) + (ypart[rows(s), :] + yrec[rows(s), :])
        y1[rows(s), :] = v
        a2 = (v * inv_root(v) * gain[1:2, :]).astype(BF)
        a2s[rows(s), :] = dot(a2, spread[...]).astype(BF)
        ypart[rows(s), :] = jnp.zeros((128, 896), F32)
        da2[rows(s), :] = jnp.zeros((128, 1024), F32)

    a2st[...] = a2s[...].T

    def ffn(gates, ups, row, n):
        width = 128 * n
        w = jnp.concatenate([unit(i) for i in gates + ups], axis=1)
        both = dot(a2s[...], w)
        g, u = both[:, :width], both[:, width:]
        at = pl.ds(pl.multiple_of(row, 128), width)
        w_d = wd[at, :]
        dm = dot_t(e_all[...], w_d)
        sig = 1.0 / (1.0 + jnp.exp(-g))
        silu = g * sig
        m = (silu * u).astype(BF)
        dg = (dm * u * sig * (1.0 + g * (1.0 - sig))).astype(BF)
        du = (dm * silu).astype(BF)
        dgu = jnp.concatenate([dg, du], axis=1)
        ypart[...] += dot(m, w_d)
        da2[...] += dot_t(dgu, w)
        wd[at, :] = dot(m.T, e_all[...]).astype(BF)
        for part, places in ((dg, gates), (du, ups)):
            grads = dot(a2st[...], part).astype(BF)
            for i, place in enumerate(places):
                u_buf[place] = grads[:, 128 * i:128 * i + 128].reshape((2,) * 6 + (16, 128))

    ag_done(FFN)

    @pl.loop(0, 9)
    def _(i):
        tick(i, 3, (rs, (FFN, 5)), (ag_done, (FFN + 1,)))
        tick(i, 6, (rs, (FFN + 1, 5)), (ag_done, (FFN + 2,)))
        tick(i, 7, (rs, (FFN, 4)))
        wave, q = i // 3, i % 3
        g = 8 * q + 2 * wave
        u = 23 + 8 * q - q // 2 + 2 * wave
        ffn([g, g + 1], [u, u + 1], i * 256, 2)

    ffn([6], [29], 2304, 1)
    rs(FFN + 2, 5)

    other = pl.ds(pl.multiple_of((1 - core) * 256, 256), 256)
    out_swap = to_sibling(ypart.at[other], mrec, 8)
    out_swap.start()

    def unspread(v):
        high = v.astype(BF)
        low = (v - high.astype(F32)).astype(BF)
        return dot_t(high, spread[...]) + dot_t(low, spread[...])

    def da_swap(s):
        return to_sibling(yrec.at[rows(s)], darec.at[rows(s)], 9 + s)

    @pl.loop(0, 4)
    def _(s):
        yrec[rows(s), :] = unspread(da2[rows(s), :])
        da_swap(s).start()

    rs(FFN + 1, 4)

    @pl.loop(0, 8)
    def _(g):
        block = dot(unpack[...], wd[pl.ds(pl.multiple_of(g * 304, 16), 304), :]).astype(BF)
        for i in range(8):
            at = slab_place(g * 8 + i)
            for r in range(3):
                for c in range(7):
                    t_buf[(3 * c + r,) + at] = block[48 * i + 16 * r:48 * i + 16 * r + 16,
                                                     128 * c:128 * c + 128]

    rs(DOWN, 5)
    rs_fold(FFN)
    out_swap.wait()
    for s in range(2):
        at = pl.ds(pl.multiple_of(core * 256 + 128 * s, 128), 128)
        out_ref[pl.ds(128 * s, 128), :] = (
            y1[at, :] + (ypart[at, :] + mrec[pl.ds(128 * s, 128), :])).astype(BF)

    rs(FFN + 2, 4)

    gain_grads = gain.at[pl.ds(2, 2)]
    gain_grads[...] = jnp.zeros((2, 896), F32)

    @pl.loop(0, 4)
    def _(s):
        da_swap(s).wait()
        da = yrec[rows(s), :] + darec[rows(s), :]
        v = y1[rows(s), :]
        r = inv_root(v)

        @pl.when(s // 2 == core)
        def _():
            gain[3:4, :] += jnp.sum(da * v * r, axis=0, keepdims=True)

        w = da * gain[1:2, :]
        dy = (e_all[rows(s), :].astype(F32) + r * w
              - v * (r * r * r) * jnp.mean(w * v, axis=-1, keepdims=True))
        darec[rows(s), :] = dy
        f = dy.astype(BF)
        a2s[rows(s), 0:896] = f
        ds_ = dot_t(f, w_out()).astype(BF)
        a2s[rows(s), 896:1024] = jnp.zeros((128, 128), BF)
        a2st[rows(s), 0:448] = dot_t(ds_, spread_o[core]).astype(BF)

    rs_fold(FFN + 1)
    rs_small(0, 3)
    o_grad = dot(o_s[...].T, a2s[:, 0:896]).astype(BF)
    for i in range(7):
        part = o_grad[:, 128 * i:128 * i + 128].reshape((2,) * 5 + (16, 128))
        u_buf[OUT_UNITS[i], :, :, :, :, core] = part
        u_buf[OUT_UNITS[i], :, :, :, :, 1 - core] = jnp.zeros_like(part)
    rs(OUT, 5)
    rs_small(0, 2)
    rs(DOWN, 4)

    bias[...] = jnp.zeros((8, 640), F32)

    @pl.loop(0, 4)
    def _(s):
        tick(s, 1, (rs_small, (0, 1)), (rs_fold, (FFN + 2,)))
        tick(s, 2, (rs, (OUT, 4)), (rs_small, (0, 0)))
        tick(s, 3, (rs_fold, (DOWN,)))
        q7, k, v, soft = attend(s)
        do7 = heads(a2st[rows(s), 0:448])
        dp = dot_t(do7, v)
        ds_ = (soft * (dp - jnp.sum(soft * dp, axis=-1, keepdims=True))).astype(BF)
        dq = unheads(dot(ds_, k)) * 0.125
        dk = dot(ds_.T, q7) * 0.125
        dv = dot(soft.astype(BF).T, do7)
        raw = jnp.concatenate([dq, dk, dv, jnp.zeros((128, 64), F32)], axis=1)
        scaled = raw * wide(sine, s)
        turned = jnp.where(first, pltpu.roll(scaled, 608, 1), -pltpu.roll(scaled, 32, 1))
        grad = jnp.where(turns, raw * wide(cosine, s) + turned, raw).astype(BF)
        qkv[rows(s), :] = grad
        bias[0:1, :] += jnp.sum(grad.astype(F32), axis=0, keepdims=True)

    rs_fold(OUT)
    rs_small(1, 3)
    w_qkv = jnp.concatenate([unit(QKV + i) for i in range(5)], axis=1)
    da2[...] = dot_t(qkv[...], w_qkv)

    @pl.loop(0, 4)
    def _(s):
        yrec[rows(s), :] = unspread(da2[rows(s), :])

    a_swap = to_sibling(yrec.at[other], arec, 13)
    a_swap.start()
    rs_small(1, 2)
    a2st[...] = a1s[...].T
    for i in range(4):
        part = dot(a2st[...], qkv[:, 128 * i:128 * i + 128])
        u_buf[QKV + i] = part.astype(BF).reshape((2,) * 6 + (16, 128))
    a_swap.wait()
    for s in range(2):
        at = pl.ds(pl.multiple_of(core * 256 + 128 * s, 128), 128)
        da = yrec[at, :] + arec[pl.ds(128 * s, 128), :]
        v = x_all[at, :].astype(F32)
        r = inv_root(v)
        gain[2:3, :] += jnp.sum(da * v * r, axis=0, keepdims=True)
        w = da * gain[0:1, :]
        gtok_ref[pl.ds(128 * s, 128), :] = (
            darec[at, :] + r * w
            - v * (r * r * r) * jnp.mean(w * v, axis=-1, keepdims=True)).astype(BF)
    top = dot(jnp.concatenate([gain[2:4, :], jnp.zeros((14, 896), F32)], axis=0).astype(BF),
              spread[...])
    spot = jnp.where(choose, jnp.broadcast_to(bias[0:1, :], (16, 640)), 0.0).astype(BF)
    hit = (lax.broadcasted_iota(jnp.int32, (1024, 640), 0) == brow[core, 0:1, :]).astype(BF)
    low = dot_t(spot, hit)
    small = jnp.concatenate(
        [jnp.zeros((64, 1024), F32), top, low, jnp.zeros((32, 1024), F32)], axis=0).T
    part = dot(a2st[...], qkv[:, 512:640]) + small
    u_buf[49] = part.astype(BF).reshape((2,) * 6 + (16, 128))
    rs_head(2)
    rs_small(1, 1)
    rs_small_end(0)
    rs_head(1)
    rs_small(1, 0)
    rs_head(0)
    rs_small_end(1)
    last_swap(0).start()
    rs_head_end()
    last_swap(1).start()
    rs_sent()
    for i in range(2):
        last_swap(i).wait()


def layer(*arrays):
    dma = pltpu.SemaphoreType.DMA
    vm = pltpu.VMEM
    return pl.pallas_call(
        layer_kernel,
        out_shape=(
            jax.ShapeDtypeStruct((256, 896), BF),
            jax.ShapeDtypeStruct((256, 896), BF),
            jax.ShapeDtypeStruct((UNITS + TALL, 16, 128), F32),
            jax.ShapeDtypeStruct((UNITS, 16, 128), BF),
        ),
        in_specs=[pl.BlockSpec(memory_space=vm)] * 10 + [pl.BlockSpec(memory_space=pl.ANY)] * 6
        + [pl.BlockSpec(memory_space=vm)] * 2,
        out_specs=[pl.BlockSpec(memory_space=vm)] * 4,
        scratch_shapes=[
            vm((UNITS,) + (2,) * 6 + (16, 128), BF), vm((TALL,) + (2,) * 6 + (16, 128), BF),
            vm((QKV,) + (2,) * 5 + (16, 128), BF), vm((TALL,) + (2,) * 5 + (16, 128), BF),
            vm((2432, 896), BF), vm((512, 896), BF), vm((512, 896), BF), vm((2, 8, 128), F32),
            vm((UNITS, 16, 128), BF), vm((512, 1024), BF), vm((512, 1024), BF),
            vm((1024, 512), BF), vm((512, 640), BF), vm((512, 512), BF),
            vm((512, 896), F32), vm((512, 896), F32), vm((512, 896), F32), vm((512, 1024), F32),
            vm((512, 896), F32), vm((256, 896), F32), vm((256, 896), F32), vm((512, 128), F32), vm((512, 128), F32),
            vm((8, 896), F32), vm((8, 640), F32), vm((UNITS, 16, 128), BF),
            vm((8, RAW), F32), vm((16, 896), F32), vm((UNITS, 16, 128), BF),
            vm((UNITS, 16, 128), BF), vm((8, 128), F32), vm((896, 1024), BF), vm((2, 448, 512), BF),
            vm((304, 384), BF), vm((384, 304), BF),
            vm((3, 5, 16, 128), BF), vm((3, 5) + (2,) * 2 + (16, 128), BF),
            vm((3, 5) + (2,) * 4 + (16, 128), BF),
            dma((4, 6, 2)), dma((4, 6, 3)), dma((4, 6, 3)), dma((5, 2, 6)), dma((5, 2, 6)),
            dma((5, 2, 6)), dma((3, 3, 3)), dma((3, 3, 3)), dma((3, 3, 3)),
            pltpu.SemaphoreType.REGULAR((7, 6)),
            dma((21,)), dma((21,)), dma((6,)),
        ],
        compiler_params=pltpu.CompilerParams(collective_id=0, has_side_effects=True,
                                             vmem_limit_bytes=60 * 2**20),
    )(*arrays)


def finish_kernel(own, sib, out, tok, out_ref, tok_ref, q_ref, k_ref, v_ref, o_ref, g_ref, u_ref,
                  d_ref, gain_ref, bias_ref):
    out_ref[...] = out[...]
    tok_ref[...] = tok[...]
    for c in range(7):
        for r in range(3):
            n = 16 if r < 2 else 6
            d_ref[16 * r:16 * r + n, 128 * c:128 * c + 128] = own[UNITS + 3 * c + r][0:n]
    core = lax.axis_index("dp") % 2
    for c in range(2):
        @pl.when(core == c)
        def _():
            def mine(u):
                return own[u, 8 * c:8 * c + 8, :]

            def theirs(u):
                return sib[u].astype(F32)[8 * c:8 * c + 8]

            def half(plane, u, h):
                return (mine if plane == c else theirs)(u)[:, 64 * h:64 * h + 64]

            def put(ref, count, where):
                for n in range(count):
                    (p0, u0, h0), (p1, u1, h1) = where(2 * n), where(2 * n + 1)
                    if (p0, u0, h0, h1) == (p1, u1, 0, 1):
                        v = (mine if p0 == c else theirs)(u0)
                    else:
                        v = jnp.concatenate([half(p0, u0, h0), half(p1, u1, h1)], axis=1)
                    ref[:, 128 * n:128 * n + 128] = v[0:7]

            def hidden(table):
                def where(h):
                    t = h // 38 * 19 + h % 19
                    return h // 19 % 2, table[t // 2], t % 2
                return where

            put(g_ref, 38, hidden(GATE_UNITS))
            put(u_ref, 38, hidden(UP_UNITS))
            put(q_ref, 7, lambda h: (h // 7, QKV + h % 7 // 2, h % 7 % 2))
            put(k_ref, 1, lambda h: (h, QKV + 3, 1))
            put(v_ref, 1, lambda h: (h, QKV + 4, 0))
            for j, u in enumerate(OUT_UNITS):
                o_ref[:, 128 * j:128 * j + 128] = (mine(u) + theirs(u))[0:7]
            small = mine(QKV + 4) + theirs(QKV + 4)
            gain_ref[...] = small[0:7, 64:66]
            bias_ref[...] = small[0:1, 80:89]


def finish(own, sib, out, tok):
    vm = pl.BlockSpec(memory_space=pltpu.VMEM)
    shapes = [((256, 896), BF), ((256, 896), BF), ((7, 896), F32), ((7, 128), F32),
              ((7, 128), F32), ((7, 896), F32), ((7, 4864), F32), ((7, 4864), F32),
              ((38, 896), F32), ((7, 2), F32), ((1, 9), F32)]
    return pl.pallas_call(
        finish_kernel,
        out_shape=tuple(jax.ShapeDtypeStruct(s, d) for s, d in shapes),
        in_specs=[vm] * 4, out_specs=[vm] * 11,
    )(own, sib, out, tok)


def constants():
    slots = np.zeros(128, np.int32)
    for n in range(128):
        dp, fs = n // 32, n % 32
        x, y, z, core = fs // 4 % 4, fs % 4, (dp // 2) * 2 + fs // 16, dp % 2
        slots[n] = ((GRAY[x] * 4 + GRAY[y]) * 4 + GRAY[z]) * 2 + core
    spread = np.zeros((896, 1024), np.float32)
    for d in range(896):
        spread[d, slots[d // 7] * 8 + d % 7] = 1.0
    spread_o = np.zeros((2, 448, 512), np.float32)
    for c in range(2):
        part = spread[448 * c:448 * c + 448].reshape(448, 16, 2, 32)
        spread_o[c] = part[:, :, c].reshape(448, 512)
    unpack = np.zeros((384, 304), np.float32)
    for a in range(8):
        for r in range(38):
            unpack[48 * a + r, 38 * a + r] = 1.0
    brow = np.full((2, 8, 640), -1, np.int32)
    for c in range(2):
        for i in range(576):
            if i < 448:
                nat = 448 * c + i
            elif i < 512:
                nat = 896 + 64 * c + i - 448
            else:
                nat = 1024 + 64 * c + i - 512
            brow[c, 0, i] = slots[nat // 9] * 8
            brow[c, 1, i] = nat % 9
    freq = THETA ** (-2.0 * (np.arange(128) % 32) / 64.0)
    freq = np.broadcast_to(freq.astype(np.float32), (8, 128))
    return (jnp.asarray(spread, BF), jnp.asarray(spread_o, BF), jnp.asarray(unpack.T, BF),
            jnp.asarray(unpack, BF), jnp.asarray(brow), jnp.asarray(freq))


def shards(tokens, segments, w_query, w_key, w_value, w_out, w_gate, w_up, w_down, gains, biases,
           cotangent):
    out, tok, own, sib = layer(
        w_query, w_key, w_value, w_out, w_gate, w_up, w_down, gains, biases.reshape(1, 9),
        segments.reshape(2, 128), tokens.reshape(256, 896), cotangent.reshape(256, 896),
        *constants())
    out, tok, *grads, bias = finish(own, sib, out, tok)
    return (out.reshape(tokens.shape), tok.reshape(tokens.shape), *grads, bias.reshape(9))


def solution(mesh):
    row = P(AXES, None)
    batch = P(None, AXES, None, None)
    return jax.shard_map(
        shards, mesh=mesh,
        in_specs=(batch, P(None, AXES, None)) + (row,) * 8 + (P(AXES), batch),
        out_specs=(batch, batch) + (row,) * 8 + (P(AXES),),
        check_vma=False,
    )
```

```python
import functools

import jax
import jax.numpy as jnp
import numpy as np
from jax import lax
from jax.experimental import pallas as pl
from jax.experimental.pallas import tpu as pltpu
from jax.sharding import PartitionSpec as P

EPSILON = 1e-06
THETA = 1000000.0
NEG_FILL = -1e30
MESH = pl.DeviceIdType.MESH
AXES = ("dp", "fsdp")
BF = jnp.bfloat16
F32 = jnp.float32
GRAY = (0, 1, 3, 2)

BULK = ((0, 8), (8, 8), (16, 7), (23, 8), (31, 7), (38, 7))
TALLS = ((0, 3), (3, 3), (6, 3), (9, 3), (12, 3), (15, 2))
WAVES = (
    ((7, 1), (14, 2), (22, 1), (30, 1), (37, 1), (44, 1)),
    TALLS,
    ((0, 2), (8, 2), (16, 2), (23, 2), (31, 2), (38, 2)),
    ((2, 2), (10, 2), (18, 2), (25, 2), (33, 2), (40, 2)),
    ((4, 3), (12, 2), (20, 2), (27, 3), (35, 2), (42, 2)),
)
EARLY = ((0, 4), (8, 4), (16, 4), (23, 4), (31, 4), (38, 4))
LATE = ((4, 4), (12, 4), (20, 3), (27, 4), (35, 3), (42, 3))
OUT, DOWN, FFN = 0, 1, 2
OUT_UNITS = (7, 14, 15, 22, 30, 37, 44)
HEAD = ((45, 2), (47, 2), (49, 1))
UNITS, TALL, QKV = 50, 17, 45


def pair_units(starts, last):
    return tuple(starts[j % 6 // 2] + 2 * (j // 6) + j % 2 for j in range(18)) + (last,)


GATE_UNITS = pair_units((0, 8, 16), 6)
UP_UNITS = pair_units((23, 31, 38), 29)
GATE_AT, UP_AT, Q_AT, K_AT, V_AT, O_AT, S_AT, RAW = (
    0, 4864, 9728, 10624, 10752, 10880, 11776, 11904)
ORDER = tuple(
    tuple(2 * ((p % 3 + k // 2) % 3) + ((k % 2) ^ (p // 3)) for k in range(6)) for p in range(6)
)


def here():
    dp = lax.axis_index("dp")
    fs = lax.axis_index("fsdp")
    return (fs // 4) % 4, fs % 4, (dp // 2) * 2 + fs // 16, dp % 2


def device(x, y, z, core):
    return ((z // 2) * 2 + core, (z % 2) * 16 + x * 4 + y)


def gray_bits(v):
    high = v // 2
    low = (v % 2 + high) % 2
    return low, high


def flip(v, bit):
    if bit == 0:
        return v + 1 - 2 * (v % 2)
    return 3 - v


def partner(bit):
    x, y, z, core = here()
    axis, low = bit // 2, bit % 2
    place = [x, y, z]
    place[axis] = flip(place[axis], low)
    return device(*place, core)


def sibling():
    x, y, z, core = here()
    return device(x, y, z, 1 - core)


def my_bits():
    x, y, z, _ = here()
    bits = []
    for v in (x, y, z):
        low, high = gray_bits(v)
        bits += [low, high]
    return bits


DIMS = (1, 0, 3, 2, 5, 4)


def slot(bits, full):
    return tuple(slice(None) if b in full else bits[b] for b in DIMS)


def far(axis):
    x, y, z, core = here()
    place = [x, y, z]
    place[axis] = 3 - flip(place[axis], 0)
    return device(*place, core)


def dot(a, b):
    return lax.dot_general(a, b, (((1,), (0,)), ((), ())), preferred_element_type=F32)


def dot_t(a, b):
    return lax.dot_general(a, b, (((1,), (1,)), ((), ())), preferred_element_type=F32)


def layer_kernel(
    w_query, w_key, w_value, w_out_, w_gate, w_up, w_down, gains, biases, segments,
    x_own, e_own, spread_h, spread_o_h, pack_h, unpack_h, pick_in, pick_out, brow, freq,
    out_ref, gtok_ref, own_ref, sib_ref,
    u_buf, t_buf, u_got, t_got, wd, x_all, e_all, seg_all, stage, a1s, a2s, a2st, qkv, o_s,
    y1, ypart, yrec, da2, darec, mrec, arec, cosine, sine, gain, bias, slab,
    raw, last_rows, own_s, send_s, seg_own, spread, spread_o, pack, unpack,
    h_got0, h_got1, h_got2, ag_small_recv, rs_small_recv, small_send, ag_big_recv, rs_big_recv,
    big_send, ag_head_recv, rs_head_recv, head_send, credit, sib_send, sib_recv, loc_sem,
):
    _, _, _, core = here()
    bits = my_bits()
    flipped = [1 - b for b in bits]
    sib = sibling()
    peers = [partner(b) for b in range(6)]
    across_ = [far(a) for a in range(3)]

    barrier = pltpu.get_barrier_semaphore()
    for d in peers + across_ + [sib]:
        pl.semaphore_signal(barrier, inc=1, device_id=d, device_id_type=MESH)

    def to_sibling(src, dst, i):
        return pltpu.make_async_remote_copy(
            src_ref=src, dst_ref=dst, send_sem=sib_send.at[i], recv_sem=sib_recv.at[i],
            device_id=sib, device_id_type=MESH)

    own = pl.ds(pl.multiple_of(core * 256, 256), 256)
    locals_ = [
        pltpu.make_async_copy(a, b, loc_sem.at[i]) for i, (a, b) in enumerate((
            (x_own, x_all.at[own]), (e_own, e_all.at[own]), (spread_h, spread),
            (spread_o_h, spread_o), (pack_h, pack), (unpack_h, unpack)))]
    for c in locals_:
        c.start()

    raw[...] = jnp.zeros((8, RAW), F32)
    for ref, a in ((w_gate, GATE_AT), (w_up, UP_AT), (w_query, Q_AT), (w_key, K_AT),
                   (w_value, V_AT), (w_out_, O_AT), (gains, S_AT)):
        raw[0:7, a:a + ref.shape[1]] = ref[...].astype(F32)
    raw[0:1, S_AT + 16:S_AT + 25] = biases[...].astype(F32)
    seg_own[...] = jnp.zeros((8, 128), F32)
    seg_own[0:2, :] = segments[...].astype(F32)
    last_rows[...] = jnp.zeros((48, 128), F32)
    ends = w_down[32:38, :].astype(F32)
    for c in range(7):
        last_rows[6 * c:6 * c + 6, :] = ends[:, 128 * c:128 * c + 128]

    def lanes(first, second):
        if second == first + 64:
            return raw[:, first:first + 128]
        return jnp.concatenate([raw[:, first:first + 64], raw[:, second:second + 64]], axis=1)

    def hidden_at(base, c, h):
        return base + 1216 * (2 * (h // 19) + c) + 64 * (h % 19)

    def head_at(c, h):
        return (Q_AT + 448 * c + 64 * h, K_AT + 64 * c, V_AT + 64 * c, S_AT)[max(0, h - 6)]

    def units_of(c):
        for table, base in ((GATE_UNITS, GATE_AT), (UP_UNITS, UP_AT)):
            for j, place in enumerate(table):
                yield place, lanes(hidden_at(base, c, 2 * j), hidden_at(base, c, 2 * j + 1))
        for j in range(5):
            yield QKV + j, lanes(head_at(c, 2 * j), head_at(c, 2 * j + 1))
        for j, place in enumerate(OUT_UNITS):
            yield place, raw[:, O_AT + 128 * j:O_AT + 128 * j + 128]

    def fill(dst, other):
        for c in range(2):
            @pl.when(core == c)
            def _():
                zero = jnp.zeros((8, 128), F32)
                for place, v in units_of(1 - c if other else c):
                    tile = jnp.concatenate([zero, v] if c else [v, zero], axis=0)
                    dst[place] = tile.astype(BF)

    fill(send_s, True)
    pl.semaphore_wait(barrier, 10)
    swap_pair = to_sibling(send_s, stage, 0)
    swap_pair.start()
    swap_seg = to_sibling(seg_own, seg_all.at[core], 1)
    swap_x = to_sibling(x_own, x_all.at[own], 2)
    swap_e = to_sibling(e_own, e_all.at[own], 3)
    for c in (swap_seg, swap_x, swap_e):
        c.start()
    fill(own_s, False)
    seg_all[core] = seg_own[...]

    def remote(src, dst, send, recv, to):
        return pltpu.make_async_remote_copy(
            src_ref=src, dst_ref=dst, send_sem=send, recv_sem=recv, device_id=to,
            device_id_type=MESH)

    BOTH = ((u_buf, BULK), (t_buf, TALLS))

    def bufs(w):
        return (t_buf, t_got) if w == DOWN else (u_buf, u_got)

    def small_copy(k, p, i):
        buf, parts = BOTH[i]
        ref = buf.at[(pl.ds(*parts[p]),) + slot(bits, ORDER[p][:k])]
        return remote(ref, ref, small_send.at[k, p, i], ag_small_recv.at[k, p, i],
                      peers[ORDER[p][k]])

    def ag_small(k):
        for i in range(2):
            for p in range(6):
                if k > 0:
                    small_copy(k - 1, p, i).wait_recv()
                small_copy(k, p, i).start()

    def ag_small_end():
        for i in range(2):
            for p in range(6):
                small_copy(3, p, i).wait_recv()
        for i in range(2):
            for p in range(6):
                for k in range(4):
                    small_copy(k, p, i).wait_send()

    def ag_copy(w, k, p):
        order = ORDER[p]
        ref = bufs(w)[0].at[(pl.ds(*WAVES[w][p]),) + slot(bits, order[:k])]
        return remote(ref, ref, big_send.at[w, k - 4, p], ag_big_recv.at[w, k - 4, p],
                      peers[order[k]])

    def ag(w, k):
        for p in range(6):
            if k == 5:
                ag_copy(w, 4, p).wait_recv()
            ag_copy(w, k, p).start()

    def ag_done(w):
        for p in range(6):
            ag_copy(w, 5, p).wait_recv()
        for p in range(6):
            for k in (4, 5):
                ag_copy(w, k, p).wait_send()

    def given(k, p, *more):
        b = list(bits)
        for j in (k,) + more:
            b[ORDER[p][j]] = flipped[ORDER[p][j]]
        return slot(b, ORDER[p][:k])

    def rs_copy(w, k, p):
        acc, got = bufs(w)
        units = pl.ds(*WAVES[w][p])
        dst = got.at[units]
        if k < 5:
            b = list(bits)
            b[ORDER[p][5]] = flipped[ORDER[p][5]]
            dst = acc.at[(units,) + slot(b, ORDER[p][:k])]
        return remote(acc.at[(units,) + given(k, p)], dst, big_send.at[w, k - 4, p],
                      rs_big_recv.at[w, k - 4, p], peers[ORDER[p][k]])

    def rs_add(acc, got, part, k, p):
        start, n = part
        mine_ = slot(bits, ORDER[p][:k])

        def one(u):
            add = got[u] if k == 5 else acc[(u,) + given(k, p, 5)]
            acc[(u,) + mine_] = acc[(u,) + mine_] + add

        if k >= 2:
            @pl.loop(0, n)
            def _(i):
                one(start + i)
        else:
            for i in range(n):
                one(start + i)

    def rs(w, k):
        acc, got = bufs(w)
        if k == 4:
            for p in range(6):
                rs_copy(w, 5, p).wait_send()
            for b in range(6):
                pl.semaphore_signal(credit.at[w, b], inc=1, device_id=peers[b],
                                    device_id_type=MESH)
        for p in range(6):
            if k == 4:
                rs_copy(w, 5, p).wait_recv()
                rs_add(acc, got, WAVES[w][p], 5, p)
                pl.semaphore_wait(credit.at[w, ORDER[p][4]], 1)
            rs_copy(w, k, p).start()

    def rs_fold(w):
        acc, got = bufs(w)
        for p in range(6):
            rs_copy(w, 4, p).wait_recv()
            rs_add(acc, got, WAVES[w][p], 4, p)

    GROUPS = (((u_buf, EARLY),), ((u_buf, LATE), (t_buf, TALLS)))

    def rs_small_copy(g, k, p, i):
        buf, parts = GROUPS[g][i]
        units = pl.ds(*parts[p])
        b = list(bits)
        b[ORDER[p][5]] = flipped[ORDER[p][5]]
        return remote(buf.at[(units,) + given(k, p)], buf.at[(units,) + slot(b, ORDER[p][:k])],
                      small_send.at[k, p, g + i], rs_small_recv.at[k, p, g + i],
                      peers[ORDER[p][k]])

    def rs_small(g, k):
        if k == 3:
            for b in range(6):
                pl.semaphore_signal(credit.at[5 + g, b], inc=1, device_id=peers[b],
                                    device_id_type=MESH)
        for i in range(len(GROUPS[g])):
            for p in range(6):
                if k == 3:
                    if i == 0:
                        pl.semaphore_wait(credit.at[5 + g, ORDER[p][3]], 1)
                else:
                    rs_small_copy(g, k + 1, p, i).wait_recv()
                    rs_add(GROUPS[g][i][0], None, GROUPS[g][i][1][p], k + 1, p)
                rs_small_copy(g, k, p, i).start()

    def rs_small_end(g):
        for i, (buf, parts) in enumerate(GROUPS[g]):
            for p in range(6):
                start, n = parts[p]
                units = pl.ds(start, n)
                rs_small_copy(g, 0, p, i).wait_recv()
                total = (buf[(units,) + slot(bits, ())].astype(F32)
                         + buf[(units,) + given(0, p, 5)].astype(F32))
                own_ref[pl.ds(start + i * UNITS, n)] = total
                if i == 0:
                    slab[units] = total.astype(BF)

    def rs_sent():
        for p in range(6):
            for w in range(5):
                rs_copy(w, 4, p).wait_send()
            for g, i in ((0, 0), (1, 0), (1, 1)):
                for k in range(4):
                    rs_small_copy(g, k, p, i).wait_send()

    def turned_bits(axis, j):
        b = list(bits)
        for i in ((0,), (1,), (0, 1))[j]:
            b[2 * axis + i] = flipped[2 * axis + i]
        return b

    def head_to(axis, j):
        return across_[axis] if j == 2 else peers[2 * axis + j]

    def head_full(r, stage):
        return [2 * ((r + i) % 3) + j for i in range(stage) for j in range(2)]

    def head_copy(stage, r, j):
        ref = u_buf.at[(pl.ds(*HEAD[r]),) + slot(bits, head_full(r, stage))]
        return remote(ref, ref, head_send.at[stage, r, j], ag_head_recv.at[stage, r, j],
                      head_to((r + stage) % 3, j))

    def ag_head(stage):
        for r in range(3):
            for j in range(3):
                if stage > 0:
                    head_copy(stage - 1, r, j).wait_recv()
            for j in range(3):
                head_copy(stage, r, j).start()

    def ag_head_done():
        for r in range(3):
            for j in range(3):
                head_copy(2, r, j).wait_recv()
        for r in range(3):
            for j in range(3):
                for stage in range(3):
                    head_copy(stage, r, j).wait_send()

    def head_rs_copy(stage, r, j):
        start, n = HEAD[r]
        axis = (r + stage) % 3
        src = u_buf.at[(pl.ds(start, n),) + slot(turned_bits(axis, j), head_full(r, stage))]
        dst = (h_got0, h_got1, h_got2)[stage].at[j, pl.ds(start - QKV, n)]
        return remote(src, dst, head_send.at[stage, r, j], rs_head_recv.at[stage, r, j],
                      head_to(axis, j))

    def head_sum(stage, r):
        start, n = HEAD[r]
        for j in range(3):
            head_rs_copy(stage, r, j).wait_recv()
        got = (h_got0, h_got1, h_got2)[stage]
        totals = []
        for i in range(n):
            at = (start + i,) + slot(bits, head_full(r, stage))
            total = u_buf[at].astype(F32)
            for j in range(3):
                total = total + got[j, start + i - QKV].astype(F32)
            if stage:
                u_buf[at] = total.astype(BF)
            else:
                own_ref[start + i] = total
                slab[start + i] = total.astype(BF)

    def rs_head(stage):
        for r in range(3):
            if stage < 2:
                head_sum(stage + 1, r)
            for j in range(3):
                head_rs_copy(stage, r, j).start()

    def rs_head_end():
        for r in range(3):
            head_sum(0, r)
        for r in range(3):
            for j in range(3):
                for stage in range(3):
                    head_rs_copy(stage, r, j).wait_send()

    def last_swap(i):
        at = pl.ds(0, QKV) if i == 0 else pl.ds(QKV, UNITS - QKV)
        return to_sibling(slab.at[at], sib_ref.at[at], 16 + i)

    def rows(s):
        return pl.ds(pl.multiple_of(s * 128, 128), 128)

    def unit(u):
        return u_buf[u].reshape(1024, 128)

    mine = slot(bits, ())
    for c in range(7):
        cols = slice(128 * c, 128 * c + 128)
        for r in range(2):
            t_buf[(2 * c + r,) + mine] = w_down[16 * r:16 * r + 16, cols]
    for r in range(3):
        t_buf[(14 + r,) + mine] = last_rows[16 * r:16 * r + 16, :].astype(BF)
    swap_pair.wait()
    u_buf[(slice(None),) + mine] = own_s[...] + stage[...]
    ag_head(0)
    ag_small(0)
    ag_head(1)
    ag_small(1)
    ag_head(2)
    for c in locals_:
        c.wait()
    for c in (swap_seg, swap_x, swap_e):
        c.wait()
    ag_small(2)

    causal = (lax.broadcasted_iota(jnp.int32, (128, 128), 1)
              <= lax.broadcasted_iota(jnp.int32, (128, 128), 0))

    def allowed(s):
        line = seg_all[s // 2, pl.ds(s % 2, 1), :]
        across = jnp.broadcast_to(line, (128, 128))
        return jnp.logical_and(causal, across == across.T)

    for s in range(4):
        place = jnp.sum(allowed(s).astype(F32), axis=1, keepdims=True) - 1.0
        angle = place * freq[0:1, :]
        cosine[rows(s), :] = jnp.cos(angle)
        sine[rows(s), :] = jnp.sin(angle)
    ag_small(3)
    ag_head_done()

    small = unit(49).T
    gain[...] = dot_t(small[64:80], spread[...])[0:8]
    hit = (lax.broadcasted_iota(jnp.int32, (1024, 640), 0) == brow[core, 0:1, :]).astype(BF)
    picked = dot(small[80:96], hit)
    choose = lax.broadcasted_iota(jnp.int32, (16, 640), 0) == brow[core, 1:2, :]
    bias[...] = jnp.broadcast_to(
        jnp.sum(jnp.where(choose, picked, 0.0), axis=0, keepdims=True), (8, 640))

    def inv_root(v):
        return lax.rsqrt(jnp.mean(v * v, axis=-1, keepdims=True) + EPSILON)

    @pl.loop(0, 4)
    def _(s):
        v = x_all[rows(s), :].astype(F32)
        a2s[rows(s), 0:896] = (v * inv_root(v) * gain[0:1, :]).astype(BF)

    def spread_rows(dst):
        for h in range(2):
            at = pl.ds(256 * h, 256)
            dst[at, :] = dot(a2s[at, 0:896], spread[...]).astype(BF)

    spread_rows(a1s)

    ag_small_end()
    ag(OUT, 4)
    ag(DOWN, 4)
    lane = lax.broadcasted_iota(jnp.int32, (128, 640), 1)
    first = lane % 64 < 32
    turns = lane < 512

    def wide(ref, s):
        return jnp.concatenate([ref[rows(s), :]] * 5, axis=1)

    w_qkv = jnp.concatenate([unit(QKV + i) for i in range(5)], axis=1)
    da2[:, 0:640] = dot(a1s[...], w_qkv)
    for s in range(4):
        raw = da2[rows(s), 0:640] + bias[0:1, :]
        turned = jnp.where(first, -pltpu.roll(raw, 608, 1), pltpu.roll(raw, 32, 1))
        turned = raw * wide(cosine, s) + turned * wide(sine, s)
        qkv[rows(s), :] = jnp.where(turns, turned, raw).astype(BF)
    ag(OUT, 5)
    ag(FFN, 4)
    ag_done(OUT)
    ag(DOWN, 5)

    def heads(v):
        return jnp.concatenate([v[:, 64 * h:64 * h + 64] for h in range(7)], axis=0)

    def unheads(v):
        return jnp.concatenate([v[128 * h:128 * h + 128, :] for h in range(7)], axis=1)

    def attend(s):
        q7 = heads(qkv[rows(s), 0:448])
        k = qkv[rows(s), 448:512]
        v = qkv[rows(s), 512:576]
        score = dot_t(q7, k) * 0.125
        ok = allowed(s)
        score = jnp.where(jnp.concatenate([ok] * 7, axis=0), score, NEG_FILL)
        e = jnp.exp(score - jnp.max(score, axis=-1, keepdims=True))
        soft = e / jnp.sum(e, axis=-1, keepdims=True)
        return q7, k, v, soft

    def w_out():
        return jnp.concatenate(
            [u_buf[OUT_UNITS[i], :, :, :, :, core].reshape(512, 128) for i in range(7)], axis=1)

    def y_swap(s):
        return to_sibling(ypart.at[rows(s)], yrec.at[rows(s)], 4 + s)

    def tick(now, t, *acts):
        @pl.when(now == t)
        def _():
            for f, a in acts:
                f(*a)

    @pl.loop(0, 4)
    def _(s):
        tick(s, 1, (ag, (FFN, 5)))
        tick(s, 2, (ag, (FFN + 1, 4)))
        tick(s, 3, (ag, (FFN + 1, 5)))
        _, _, v, soft = attend(s)
        a2s[rows(s), 0:448] = unheads(dot(soft.astype(BF), v)).astype(BF)

    o_s[...] = dot(a2s[:, 0:448], spread_o[core]).astype(BF)
    for h in range(2):
        at = pl.ds(256 * h, 256)
        ypart[at, :] = dot(o_s[at, :], w_out())
        for s in (2 * h, 2 * h + 1):
            y_swap(s).start()

    ag_done(DOWN)
    ag(FFN + 2, 4)

    def slab_place(s):
        z, x, y = s // 16, s // 4 % 4, s % 4
        b = []
        for v in (x, y, z):
            low, high = gray_bits(v)
            b += [low, high]
        return slot(b, ())

    @pl.loop(0, 8)
    def _(g):
        lines, ends = [], []
        for i in range(8):
            at = slab_place(g * 8 + i)
            for r in range(2):
                lines.append(jnp.concatenate(
                    [t_buf[(2 * c + r,) + at] for c in range(7)], axis=1))
            ends += [t_buf[(14 + r,) + at] for r in range(3)]
        ends = dot(pick_in[...], jnp.concatenate(ends, axis=0)).astype(BF)
        lines.append(jnp.concatenate([ends[48 * c:48 * c + 48] for c in range(7)], axis=1))
        block = jnp.concatenate(lines, axis=0)
        wd[pl.ds(pl.multiple_of(g * 304, 16), 304), :] = dot(pack[...], block).astype(BF)

    ag(FFN + 2, 5)

    @pl.loop(0, 4)
    def _(s):
        y_swap(s).wait()
        v = x_all[rows(s), :].astype(F32) + (ypart[rows(s), :] + yrec[rows(s), :])
        y1[rows(s), :] = v
        a2s[rows(s), 0:896] = (v * inv_root(v) * gain[1:2, :]).astype(BF)
        ypart[rows(s), :] = jnp.zeros((128, 896), F32)
        da2[rows(s), :] = jnp.zeros((128, 1024), F32)

    spread_rows(a2s)
    a2st[...] = a2s[...].T

    def ffn(gates, ups, row, n):
        width = 128 * n
        w = jnp.concatenate([unit(i) for i in gates + ups], axis=1)
        both = dot(a2s[...], w)
        g, u = both[:, :width], both[:, width:]
        at = pl.ds(pl.multiple_of(row, 128), width)
        w_d = wd[at, :]
        dm = dot_t(e_all[...], w_d)
        sig = 1.0 / (1.0 + jnp.exp(-g))
        silu = g * sig
        m = (silu * u).astype(BF)
        dg = (dm * u * sig * (1.0 + g * (1.0 - sig))).astype(BF)
        du = (dm * silu).astype(BF)
        dgu = jnp.concatenate([dg, du], axis=1)
        ypart[...] += dot(m, w_d)
        da2[...] += dot_t(dgu, w)
        wd[at, :] = dot(m.T, e_all[...]).astype(BF)
        for part, places in ((dg, gates), (du, ups)):
            grads = dot(a2st[...], part).astype(BF)
            for i, place in enumerate(places):
                u_buf[place] = grads[:, 128 * i:128 * i + 128].reshape((2,) * 6 + (16, 128))

    ag_done(FFN)

    @pl.loop(0, 9)
    def _(i):
        tick(i, 3, (rs, (FFN, 5)), (ag_done, (FFN + 1,)))
        tick(i, 6, (rs, (FFN + 1, 5)), (ag_done, (FFN + 2,)))
        tick(i, 7, (rs, (FFN, 4)))
        wave, q = i // 3, i % 3
        g = 8 * q + 2 * wave
        u = 23 + 8 * q - q // 2 + 2 * wave
        ffn([g, g + 1], [u, u + 1], i * 256, 2)

    ffn([6], [29], 2304, 1)
    rs(FFN + 2, 5)

    other = pl.ds(pl.multiple_of((1 - core) * 256, 256), 256)
    out_swap = to_sibling(ypart.at[other], mrec, 8)
    out_swap.start()

    def unspread(v):
        n = v.shape[0]
        high = v.astype(BF)
        low = (v - high.astype(F32)).astype(BF)
        both = dot_t(jnp.concatenate([high, low], axis=0), spread[...])
        return both[:n] + both[n:]

    def unspread_rows(h):
        at = pl.ds(256 * h, 256)
        yrec[at, :] = unspread(da2[at, :])

    def da_swap(s):
        return to_sibling(yrec.at[rows(s)], darec.at[rows(s)], 9 + s)

    for h in range(2):
        unspread_rows(h)
        for s in (2 * h, 2 * h + 1):
            da_swap(s).start()

    rs(FFN + 1, 4)

    @pl.loop(0, 8)
    def _(g):
        block = dot(unpack[...], wd[pl.ds(pl.multiple_of(g * 304, 16), 304), :]).astype(BF)
        ends = jnp.concatenate([block[256:304, 128 * c:128 * c + 128] for c in range(7)], axis=0)
        ends = dot(pick_out[...], ends).astype(BF)
        for i in range(8):
            at = slab_place(g * 8 + i)
            for r in range(2):
                for c in range(7):
                    t_buf[(2 * c + r,) + at] = block[32 * i + 16 * r:32 * i + 16 * r + 16,
                                                     128 * c:128 * c + 128]
            for r in range(3):
                t_buf[(14 + r,) + at] = ends[48 * i + 16 * r:48 * i + 16 * r + 16]

    rs(DOWN, 5)
    out_swap.wait()
    for s in range(2):
        at = pl.ds(pl.multiple_of(core * 256 + 128 * s, 128), 128)
        out_ref[pl.ds(128 * s, 128), :] = (
            y1[at, :] + (ypart[at, :] + mrec[pl.ds(128 * s, 128), :])).astype(BF)

    gain_grads = gain.at[pl.ds(2, 2)]
    gain_grads[...] = jnp.zeros((2, 896), F32)

    @pl.loop(0, 4)
    def _(s):
        da_swap(s).wait()
        da = yrec[rows(s), :] + darec[rows(s), :]
        v = y1[rows(s), :]
        r = inv_root(v)

        @pl.when(s // 2 == core)
        def _():
            gain[3:4, :] += jnp.sum(da * v * r, axis=0, keepdims=True)

        w = da * gain[1:2, :]
        dy = (e_all[rows(s), :].astype(F32) + r * w
              - v * (r * r * r) * jnp.mean(w * v, axis=-1, keepdims=True))
        darec[rows(s), :] = dy
        f = dy.astype(BF)
        a2s[rows(s), 0:896] = f

    rs(FFN + 2, 4)
    w_o = w_out()
    a2st[0:512, 0:448] = dot_t(dot_t(a2s[:, 0:896], w_o).astype(BF), spread_o[core]).astype(BF)

    o_grad = dot(o_s[...].T, a2s[:, 0:896]).astype(BF)
    for i in range(7):
        part = o_grad[:, 128 * i:128 * i + 128].reshape((2,) * 5 + (16, 128))
        u_buf[OUT_UNITS[i], :, :, :, :, core] = part
        u_buf[OUT_UNITS[i], :, :, :, :, 1 - core] = jnp.zeros_like(part)
    rs(OUT, 5)
    rs_fold(FFN)
    rs_fold(FFN + 1)
    rs_small(0, 3)

    bias[...] = jnp.zeros((8, 640), F32)

    @pl.loop(0, 4)
    def _(s):
        tick(s, 2, (rs, (DOWN, 4)))
        tick(s, 3, (rs, (OUT, 4)), (rs_fold, (FFN + 2,)))
        q7, k, v, soft = attend(s)
        do7 = heads(a2st[rows(s), 0:448])
        dp = dot_t(do7, v)
        ds_ = (soft * (dp - jnp.sum(soft * dp, axis=-1, keepdims=True))).astype(BF)
        dq = unheads(dot(ds_, k)) * 0.125
        dk = dot(ds_.T, q7) * 0.125
        dv = dot(soft.astype(BF).T, do7)
        raw = jnp.concatenate([dq, dk, dv, jnp.zeros((128, 64), F32)], axis=1)
        scaled = raw * wide(sine, s)
        turned = jnp.where(first, pltpu.roll(scaled, 608, 1), -pltpu.roll(scaled, 32, 1))
        grad = jnp.where(turns, raw * wide(cosine, s) + turned, raw).astype(BF)
        qkv[rows(s), :] = grad
        bias[0:1, :] += jnp.sum(grad.astype(F32), axis=0, keepdims=True)

    rs_small(0, 2)
    w_qkv = jnp.concatenate([unit(QKV + i) for i in range(5)], axis=1)
    da2[...] = dot_t(qkv[...], w_qkv)
    rs_fold(DOWN)
    rs_fold(OUT)
    rs_small(1, 3)
    for h in range(2):
        unspread_rows(h)
    a_swap = to_sibling(yrec.at[other], arec, 13)
    a_swap.start()
    rs_small(0, 1)
    a2st[...] = a1s[...].T
    for i in range(4):
        part = dot(a2st[...], qkv[:, 128 * i:128 * i + 128])
        u_buf[QKV + i] = part.astype(BF).reshape((2,) * 6 + (16, 128))
    rs_small(1, 2)
    a_swap.wait()
    for s in range(2):
        at = pl.ds(pl.multiple_of(core * 256 + 128 * s, 128), 128)
        da = yrec[at, :] + arec[pl.ds(128 * s, 128), :]
        v = x_all[at, :].astype(F32)
        r = inv_root(v)
        gain[2:3, :] += jnp.sum(da * v * r, axis=0, keepdims=True)
        w = da * gain[0:1, :]
        gtok_ref[pl.ds(128 * s, 128), :] = (
            darec[at, :] + r * w
            - v * (r * r * r) * jnp.mean(w * v, axis=-1, keepdims=True)).astype(BF)
    rs_small(0, 0)
    top = dot(jnp.concatenate([gain[2:4, :], jnp.zeros((14, 896), F32)], axis=0).astype(BF),
              spread[...])
    spot = jnp.where(choose, jnp.broadcast_to(bias[0:1, :], (16, 640)), 0.0).astype(BF)
    hit = (lax.broadcasted_iota(jnp.int32, (1024, 640), 0) == brow[core, 0:1, :]).astype(BF)
    low = dot_t(spot, hit)
    small = jnp.concatenate(
        [jnp.zeros((64, 1024), F32), top, low, jnp.zeros((32, 1024), F32)], axis=0).T
    part = dot(a2st[...], qkv[:, 512:640]) + small
    u_buf[49] = part.astype(BF).reshape((2,) * 6 + (16, 128))
    rs_head(2)
    rs_small(1, 1)
    rs_small_end(0)
    rs_head(1)
    rs_small(1, 0)
    rs_head(0)
    rs_small_end(1)
    last_swap(0).start()
    rs_head_end()
    last_swap(1).start()
    rs_sent()
    for i in range(2):
        last_swap(i).wait()


def layer(*arrays):
    dma = pltpu.SemaphoreType.DMA
    vm = pltpu.VMEM
    return pl.pallas_call(
        layer_kernel,
        out_shape=(
            jax.ShapeDtypeStruct((256, 896), BF),
            jax.ShapeDtypeStruct((256, 896), BF),
            jax.ShapeDtypeStruct((UNITS + TALL, 16, 128), F32),
            jax.ShapeDtypeStruct((UNITS, 16, 128), BF),
        ),
        in_specs=[pl.BlockSpec(memory_space=vm)] * 10 + [pl.BlockSpec(memory_space=pl.ANY)] * 6
        + [pl.BlockSpec(memory_space=vm)] * 4,
        out_specs=[pl.BlockSpec(memory_space=vm)] * 4,
        scratch_shapes=[
            vm((UNITS,) + (2,) * 6 + (16, 128), BF), vm((TALL,) + (2,) * 6 + (16, 128), BF),
            vm((QKV,) + (2,) * 5 + (16, 128), BF), vm((TALL,) + (2,) * 5 + (16, 128), BF),
            vm((2432, 896), BF), vm((512, 896), BF), vm((512, 896), BF), vm((2, 8, 128), F32),
            vm((UNITS, 16, 128), BF), vm((512, 1024), BF), vm((512, 1024), BF),
            vm((1024, 512), BF), vm((512, 640), BF), vm((512, 512), BF),
            vm((512, 896), F32), vm((512, 896), F32), vm((512, 896), F32), vm((512, 1024), F32),
            vm((512, 896), F32), vm((256, 896), F32), vm((256, 896), F32), vm((512, 128), F32), vm((512, 128), F32),
            vm((8, 896), F32), vm((8, 640), F32), vm((UNITS, 16, 128), BF),
            vm((8, RAW), F32), vm((48, 128), F32), vm((UNITS, 16, 128), BF),
            vm((UNITS, 16, 128), BF), vm((8, 128), F32), vm((896, 1024), BF), vm((2, 448, 512), BF),
            vm((304, 304), BF), vm((304, 304), BF),
            vm((3, 5, 16, 128), BF), vm((3, 5) + (2,) * 2 + (16, 128), BF),
            vm((3, 5) + (2,) * 4 + (16, 128), BF),
            dma((4, 6, 2)), dma((4, 6, 3)), dma((4, 6, 3)), dma((5, 2, 6)), dma((5, 2, 6)),
            dma((5, 2, 6)), dma((3, 3, 3)), dma((3, 3, 3)), dma((3, 3, 3)),
            pltpu.SemaphoreType.REGULAR((7, 6)),
            dma((21,)), dma((21,)), dma((6,)),
        ],
        compiler_params=pltpu.CompilerParams(collective_id=0, has_side_effects=True,
                                             vmem_limit_bytes=60 * 2**20),
    )(*arrays)


def finish_kernel(own, sib, out, tok, out_ref, tok_ref, q_ref, k_ref, v_ref, o_ref, g_ref, u_ref,
                  d_ref, gain_ref, bias_ref):
    out_ref[...] = out[...]
    tok_ref[...] = tok[...]
    for c in range(7):
        for r in range(2):
            d_ref[16 * r:16 * r + 16, 128 * c:128 * c + 128] = own[UNITS + 2 * c + r]
    ends = jnp.concatenate([own[UNITS + 14 + r] for r in range(3)], axis=0)
    for c in range(7):
        d_ref[32:38, 128 * c:128 * c + 128] = ends[6 * c:6 * c + 6]
    core = lax.axis_index("dp") % 2
    for c in range(2):
        @pl.when(core == c)
        def _():
            def mine(u):
                return own[u, 8 * c:8 * c + 8, :]

            def theirs(u):
                return sib[u].astype(F32)[8 * c:8 * c + 8]

            def half(plane, u, h):
                return (mine if plane == c else theirs)(u)[:, 64 * h:64 * h + 64]

            def put(ref, count, where):
                for n in range(count):
                    (p0, u0, h0), (p1, u1, h1) = where(2 * n), where(2 * n + 1)
                    if (p0, u0, h0, h1) == (p1, u1, 0, 1):
                        v = (mine if p0 == c else theirs)(u0)
                    else:
                        v = jnp.concatenate([half(p0, u0, h0), half(p1, u1, h1)], axis=1)
                    ref[:, 128 * n:128 * n + 128] = v[0:7]

            def hidden(table):
                def where(h):
                    t = h // 38 * 19 + h % 19
                    return h // 19 % 2, table[t // 2], t % 2
                return where

            put(g_ref, 38, hidden(GATE_UNITS))
            put(u_ref, 38, hidden(UP_UNITS))
            put(q_ref, 7, lambda h: (h // 7, QKV + h % 7 // 2, h % 7 % 2))
            put(k_ref, 1, lambda h: (h, QKV + 3, 1))
            put(v_ref, 1, lambda h: (h, QKV + 4, 0))
            for j, u in enumerate(OUT_UNITS):
                o_ref[:, 128 * j:128 * j + 128] = (mine(u) + theirs(u))[0:7]
            small = mine(QKV + 4) + theirs(QKV + 4)
            gain_ref[...] = small[0:7, 64:66]
            bias_ref[...] = small[0:1, 80:89]


def finish(own, sib, out, tok):
    vm = pl.BlockSpec(memory_space=pltpu.VMEM)
    shapes = [((256, 896), BF), ((256, 896), BF), ((7, 896), F32), ((7, 128), F32),
              ((7, 128), F32), ((7, 896), F32), ((7, 4864), F32), ((7, 4864), F32),
              ((38, 896), F32), ((7, 2), F32), ((1, 9), F32)]
    return pl.pallas_call(
        finish_kernel,
        out_shape=tuple(jax.ShapeDtypeStruct(s, d) for s, d in shapes),
        in_specs=[vm] * 4, out_specs=[vm] * 11,
    )(own, sib, out, tok)


def constants():
    slots = np.zeros(128, np.int32)
    for n in range(128):
        dp, fs = n // 32, n % 32
        x, y, z, core = fs // 4 % 4, fs % 4, (dp // 2) * 2 + fs // 16, dp % 2
        slots[n] = ((GRAY[x] * 4 + GRAY[y]) * 4 + GRAY[z]) * 2 + core
    spread = np.zeros((896, 1024), np.float32)
    for d in range(896):
        spread[d, slots[d // 7] * 8 + d % 7] = 1.0
    spread_o = np.zeros((2, 448, 512), np.float32)
    for c in range(2):
        part = spread[448 * c:448 * c + 448].reshape(448, 16, 2, 32)
        spread_o[c] = part[:, :, c].reshape(448, 512)
    unpack = np.zeros((304, 304), np.float32)
    pick_in = np.zeros((336, 384), np.float32)
    for a in range(8):
        for r in range(38):
            unpack[32 * a + r if r < 32 else 256 + 6 * a + r - 32, 38 * a + r] = 1.0
        for r in range(6):
            for c in range(7):
                pick_in[48 * c + 6 * a + r, 48 * a + 6 * c + r] = 1.0
    brow = np.full((2, 8, 640), -1, np.int32)
    for c in range(2):
        for i in range(576):
            if i < 448:
                nat = 448 * c + i
            elif i < 512:
                nat = 896 + 64 * c + i - 448
            else:
                nat = 1024 + 64 * c + i - 512
            brow[c, 0, i] = slots[nat // 9] * 8
            brow[c, 1, i] = nat % 9
    freq = THETA ** (-2.0 * (np.arange(128) % 32) / 64.0)
    freq = np.broadcast_to(freq.astype(np.float32), (8, 128))
    return (jnp.asarray(spread, BF), jnp.asarray(spread_o, BF), jnp.asarray(unpack.T, BF),
            jnp.asarray(unpack, BF), jnp.asarray(pick_in, BF), jnp.asarray(pick_in.T, BF),
            jnp.asarray(brow), jnp.asarray(freq))


def shards(tokens, segments, w_query, w_key, w_value, w_out, w_gate, w_up, w_down, gains, biases,
           cotangent):
    out, tok, own, sib = layer(
        w_query, w_key, w_value, w_out, w_gate, w_up, w_down, gains, biases.reshape(1, 9),
        segments.reshape(2, 128), tokens.reshape(256, 896), cotangent.reshape(256, 896),
        *constants())
    out, tok, *grads, bias = finish(own, sib, out, tok)
    return (out.reshape(tokens.shape), tok.reshape(tokens.shape), *grads, bias.reshape(9))


def solution(mesh):
    row = P(AXES, None)
    batch = P(None, AXES, None, None)
    return jax.shard_map(
        shards, mesh=mesh,
        in_specs=(batch, P(None, AXES, None)) + (row,) * 8 + (P(AXES), batch),
        out_specs=(batch, batch) + (row,) * 8 + (P(AXES),),
        check_vma=False,
    )
```

```python
import functools

import jax
import jax.numpy as jnp
import numpy as np
from jax import lax
from jax.experimental import pallas as pl
from jax.experimental.pallas import tpu as pltpu
from jax.sharding import PartitionSpec as P

EPSILON = 1e-06
THETA = 1000000.0
NEG_FILL = -1e30
MESH = pl.DeviceIdType.MESH
AXES = ("dp", "fsdp")
BF = jnp.bfloat16
F32 = jnp.float32
GRAY = (0, 1, 3, 2)

BULK = ((0, 8), (8, 8), (16, 7), (23, 8), (31, 7), (38, 7))
TALLS = ((0, 3), (3, 3), (6, 3), (9, 3), (12, 3), (15, 2))
WAVES = (
    ((7, 1), (14, 2), (22, 1), (30, 1), (37, 1), (44, 1)),
    TALLS,
    ((0, 2), (8, 2), (16, 2), (23, 2), (31, 2), (38, 2)),
    ((2, 2), (10, 2), (18, 2), (25, 2), (33, 2), (40, 2)),
    ((4, 3), (12, 2), (20, 2), (27, 3), (35, 2), (42, 2)),
)
EARLY = ((0, 4), (8, 4), (16, 4), (23, 4), (31, 4), (38, 4))
LATE = ((4, 4), (12, 4), (20, 3), (27, 4), (35, 3), (42, 3))
OUT, DOWN, FFN = 0, 1, 2
OUT_UNITS = (7, 14, 15, 22, 30, 37, 44)
HEAD = ((45, 2), (47, 2), (49, 1))
UNITS, TALL, QKV = 50, 17, 45


def pair_units(starts, last):
    return tuple(starts[j % 6 // 2] + 2 * (j // 6) + j % 2 for j in range(18)) + (last,)


GATE_UNITS = pair_units((0, 8, 16), 6)
UP_UNITS = pair_units((23, 31, 38), 29)
GATE_AT, UP_AT, Q_AT, K_AT, V_AT, O_AT, S_AT, RAW = (
    0, 4864, 9728, 10624, 10752, 10880, 11776, 11904)
ORDER = tuple(
    tuple(2 * ((p % 3 + k // 2) % 3) + ((k % 2) ^ (p // 3)) for k in range(6)) for p in range(6)
)


def here():
    dp = lax.axis_index("dp")
    fs = lax.axis_index("fsdp")
    return (fs // 4) % 4, fs % 4, (dp // 2) * 2 + fs // 16, dp % 2


def device(x, y, z, core):
    return ((z // 2) * 2 + core, (z % 2) * 16 + x * 4 + y)


def gray_bits(v):
    high = v // 2
    low = (v % 2 + high) % 2
    return low, high


def flip(v, bit):
    if bit == 0:
        return v + 1 - 2 * (v % 2)
    return 3 - v


def partner(bit):
    x, y, z, core = here()
    axis, low = bit // 2, bit % 2
    place = [x, y, z]
    place[axis] = flip(place[axis], low)
    return device(*place, core)


def sibling():
    x, y, z, core = here()
    return device(x, y, z, 1 - core)


def my_bits():
    x, y, z, _ = here()
    bits = []
    for v in (x, y, z):
        low, high = gray_bits(v)
        bits += [low, high]
    return bits


DIMS = (1, 0, 3, 2, 5, 4)


def slot(bits, full):
    return tuple(slice(None) if b in full else bits[b] for b in DIMS)


def far(axis):
    x, y, z, core = here()
    place = [x, y, z]
    place[axis] = 3 - flip(place[axis], 0)
    return device(*place, core)


def dot(a, b):
    return lax.dot_general(a, b, (((1,), (0,)), ((), ())), preferred_element_type=F32)


def dot_t(a, b):
    return lax.dot_general(a, b, (((1,), (1,)), ((), ())), preferred_element_type=F32)


def layer_kernel(
    w_query, w_key, w_value, w_out_, w_gate, w_up, w_down, gains, biases, segments,
    x_own, e_own, spread_h, spread_o_h, pack_h, unpack_h, pick_in, pick_out, brow, freq,
    out_ref, gtok_ref, own_ref, sib_ref,
    u_buf, t_buf, u_got, t_got, wd, x_all, e_all, seg_all, stage, a1s, a2s, a2st, qkv, o_s,
    y1, ypart, yrec, da2, darec, mrec, arec, cosine, sine, gain, bias, slab,
    raw, last_rows, own_s, send_s, seg_own, spread, spread_o, pack, unpack,
    h_got0, h_got1, h_got2, ag_small_recv, rs_small_recv, small_send, ag_big_recv, rs_big_recv,
    big_send, ag_head_recv, rs_head_recv, head_send, credit, sib_send, sib_recv, loc_sem,
):
    _, _, _, core = here()
    bits = my_bits()
    flipped = [1 - b for b in bits]
    sib = sibling()
    peers = [partner(b) for b in range(6)]
    across_ = [far(a) for a in range(3)]

    barrier = pltpu.get_barrier_semaphore()
    for d in peers + across_ + [sib]:
        pl.semaphore_signal(barrier, inc=1, device_id=d, device_id_type=MESH)

    def to_sibling(src, dst, i):
        return pltpu.make_async_remote_copy(
            src_ref=src, dst_ref=dst, send_sem=sib_send.at[i], recv_sem=sib_recv.at[i],
            device_id=sib, device_id_type=MESH)

    own = pl.ds(pl.multiple_of(core * 256, 256), 256)
    locals_ = [
        pltpu.make_async_copy(a, b, loc_sem.at[i]) for i, (a, b) in enumerate((
            (x_own, x_all.at[own]), (e_own, e_all.at[own]), (spread_h, spread),
            (spread_o_h, spread_o), (pack_h, pack), (unpack_h, unpack)))]
    for c in locals_:
        c.start()

    raw[...] = jnp.zeros((8, RAW), F32)
    for ref, a in ((w_gate, GATE_AT), (w_up, UP_AT), (w_query, Q_AT), (w_key, K_AT),
                   (w_value, V_AT), (w_out_, O_AT)):
        raw[0:7, a:a + ref.shape[1]] = ref[...].astype(F32)
    last_rows[0:8, :] = jnp.zeros((8, 128), F32)
    last_rows[0:2, 0:7] = gains[...].astype(F32)
    raw[0:7, S_AT:S_AT + 2] = last_rows[0:8, :].T[0:7, 0:2]
    raw[0:1, S_AT + 16:S_AT + 25] = biases[...].astype(F32)
    seg_own[...] = jnp.zeros((8, 128), F32)
    seg_own[0:2, :] = segments[...].astype(F32)
    last_rows[...] = jnp.zeros((48, 128), F32)
    ends = w_down[32:38, :].astype(F32)
    for c in range(7):
        last_rows[6 * c:6 * c + 6, :] = ends[:, 128 * c:128 * c + 128]

    def lanes(first, second):
        if second == first + 64:
            return raw[:, first:first + 128]
        return jnp.concatenate([raw[:, first:first + 64], raw[:, second:second + 64]], axis=1)

    def hidden_at(base, c, h):
        return base + 1216 * (2 * (h // 19) + c) + 64 * (h % 19)

    def head_at(c, h):
        return (Q_AT + 448 * c + 64 * h, K_AT + 64 * c, V_AT + 64 * c, S_AT)[max(0, h - 6)]

    def units_of(c):
        for table, base in ((GATE_UNITS, GATE_AT), (UP_UNITS, UP_AT)):
            for j, place in enumerate(table):
                yield place, lanes(hidden_at(base, c, 2 * j), hidden_at(base, c, 2 * j + 1))
        for j in range(5):
            yield QKV + j, lanes(head_at(c, 2 * j), head_at(c, 2 * j + 1))
        for j, place in enumerate(OUT_UNITS):
            yield place, raw[:, O_AT + 128 * j:O_AT + 128 * j + 128]

    def fill(dst, other):
        for c in range(2):
            @pl.when(core == c)
            def _():
                zero = jnp.zeros((8, 128), F32)
                for place, v in units_of(1 - c if other else c):
                    tile = jnp.concatenate([zero, v] if c else [v, zero], axis=0)
                    dst[place] = tile.astype(BF)

    fill(send_s, True)
    pl.semaphore_wait(barrier, 10)
    swap_pair = to_sibling(send_s, stage, 0)
    swap_pair.start()
    swap_seg = to_sibling(seg_own, seg_all.at[core], 1)
    swap_x = to_sibling(x_own, x_all.at[own], 2)
    swap_e = to_sibling(e_own, e_all.at[own], 3)
    for c in (swap_seg, swap_x, swap_e):
        c.start()
    fill(own_s, False)
    seg_all[core] = seg_own[...]

    def remote(src, dst, send, recv, to):
        return pltpu.make_async_remote_copy(
            src_ref=src, dst_ref=dst, send_sem=send, recv_sem=recv, device_id=to,
            device_id_type=MESH)

    BOTH = ((u_buf, BULK), (t_buf, TALLS))

    def bufs(w):
        return (t_buf, t_got) if w == DOWN else (u_buf, u_got)

    def small_copy(k, p, i):
        buf, parts = BOTH[i]
        ref = buf.at[(pl.ds(*parts[p]),) + slot(bits, ORDER[p][:k])]
        return remote(ref, ref, small_send.at[k, p, i], ag_small_recv.at[k, p, i],
                      peers[ORDER[p][k]])

    def ag_small(k):
        for i in range(2):
            for p in range(6):
                if k > 0:
                    small_copy(k - 1, p, i).wait_recv()
                small_copy(k, p, i).start()

    def ag_small_end():
        for i in range(2):
            for p in range(6):
                small_copy(3, p, i).wait_recv()
        for i in range(2):
            for p in range(6):
                for k in range(4):
                    small_copy(k, p, i).wait_send()

    def ag_copy(w, k, p):
        order = ORDER[p]
        ref = bufs(w)[0].at[(pl.ds(*WAVES[w][p]),) + slot(bits, order[:k])]
        return remote(ref, ref, big_send.at[w, k - 4, p], ag_big_recv.at[w, k - 4, p],
                      peers[order[k]])

    def ag(w, k):
        for p in range(6):
            if k == 5:
                ag_copy(w, 4, p).wait_recv()
            ag_copy(w, k, p).start()

    def ag_done(w):
        for p in range(6):
            ag_copy(w, 5, p).wait_recv()
        for p in range(6):
            for k in (4, 5):
                ag_copy(w, k, p).wait_send()

    def given(k, p, *more):
        b = list(bits)
        for j in (k,) + more:
            b[ORDER[p][j]] = flipped[ORDER[p][j]]
        return slot(b, ORDER[p][:k])

    def rs_copy(w, k, p):
        acc, got = bufs(w)
        units = pl.ds(*WAVES[w][p])
        dst = got.at[units]
        if k < 5:
            b = list(bits)
            b[ORDER[p][5]] = flipped[ORDER[p][5]]
            dst = acc.at[(units,) + slot(b, ORDER[p][:k])]
        return remote(acc.at[(units,) + given(k, p)], dst, big_send.at[w, k - 4, p],
                      rs_big_recv.at[w, k - 4, p], peers[ORDER[p][k]])

    def rs_add(acc, got, part, k, p):
        start, n = part
        mine_ = slot(bits, ORDER[p][:k])

        def one(u):
            add = got[u] if k == 5 else acc[(u,) + given(k, p, 5)]
            acc[(u,) + mine_] = acc[(u,) + mine_] + add

        if k >= 2:
            @pl.loop(0, n)
            def _(i):
                one(start + i)
        else:
            for i in range(n):
                one(start + i)

    def rs(w, k):
        acc, got = bufs(w)
        if k == 4:
            for p in range(6):
                rs_copy(w, 5, p).wait_send()
            for b in range(6):
                pl.semaphore_signal(credit.at[w, b], inc=1, device_id=peers[b],
                                    device_id_type=MESH)
        for p in range(6):
            if k == 4:
                rs_copy(w, 5, p).wait_recv()
                rs_add(acc, got, WAVES[w][p], 5, p)
                pl.semaphore_wait(credit.at[w, ORDER[p][4]], 1)
            rs_copy(w, k, p).start()

    def rs_fold(w):
        acc, got = bufs(w)
        for p in range(6):
            rs_copy(w, 4, p).wait_recv()
            rs_add(acc, got, WAVES[w][p], 4, p)

    GROUPS = (((u_buf, EARLY),), ((u_buf, LATE), (t_buf, TALLS)))

    def rs_small_copy(g, k, p, i):
        buf, parts = GROUPS[g][i]
        units = pl.ds(*parts[p])
        b = list(bits)
        b[ORDER[p][5]] = flipped[ORDER[p][5]]
        return remote(buf.at[(units,) + given(k, p)], buf.at[(units,) + slot(b, ORDER[p][:k])],
                      small_send.at[k, p, g + i], rs_small_recv.at[k, p, g + i],
                      peers[ORDER[p][k]])

    def rs_small(g, k):
        if k == 3:
            for b in range(6):
                pl.semaphore_signal(credit.at[5 + g, b], inc=1, device_id=peers[b],
                                    device_id_type=MESH)
        for i in range(len(GROUPS[g])):
            for p in range(6):
                if k == 3:
                    if i == 0:
                        pl.semaphore_wait(credit.at[5 + g, ORDER[p][3]], 1)
                else:
                    rs_small_copy(g, k + 1, p, i).wait_recv()
                    rs_add(GROUPS[g][i][0], None, GROUPS[g][i][1][p], k + 1, p)
                rs_small_copy(g, k, p, i).start()

    def rs_small_end(g):
        for i, (buf, parts) in enumerate(GROUPS[g]):
            for p in range(6):
                start, n = parts[p]
                units = pl.ds(start, n)
                rs_small_copy(g, 0, p, i).wait_recv()
                total = (buf[(units,) + slot(bits, ())].astype(F32)
                         + buf[(units,) + given(0, p, 5)].astype(F32))
                own_ref[pl.ds(start + i * UNITS, n)] = total
                if i == 0:
                    slab[units] = total.astype(BF)

    def rs_sent():
        for p in range(6):
            for w in range(5):
                rs_copy(w, 4, p).wait_send()
            for g, i in ((0, 0), (1, 0), (1, 1)):
                for k in range(4):
                    rs_small_copy(g, k, p, i).wait_send()

    def turned_bits(axis, j):
        b = list(bits)
        for i in ((0,), (1,), (0, 1))[j]:
            b[2 * axis + i] = flipped[2 * axis + i]
        return b

    def head_to(axis, j):
        return across_[axis] if j == 2 else peers[2 * axis + j]

    def head_full(r, stage):
        return [2 * ((r + i) % 3) + j for i in range(stage) for j in range(2)]

    def head_copy(stage, r, j):
        ref = u_buf.at[(pl.ds(*HEAD[r]),) + slot(bits, head_full(r, stage))]
        return remote(ref, ref, head_send.at[stage, r, j], ag_head_recv.at[stage, r, j],
                      head_to((r + stage) % 3, j))

    def ag_head(stage):
        for r in range(3):
            for j in range(3):
                if stage > 0:
                    head_copy(stage - 1, r, j).wait_recv()
            for j in range(3):
                head_copy(stage, r, j).start()

    def ag_head_done():
        for r in range(3):
            for j in range(3):
                head_copy(2, r, j).wait_recv()
        for r in range(3):
            for j in range(3):
                for stage in range(3):
                    head_copy(stage, r, j).wait_send()

    def head_rs_copy(stage, r, j):
        start, n = HEAD[r]
        axis = (r + stage) % 3
        src = u_buf.at[(pl.ds(start, n),) + slot(turned_bits(axis, j), head_full(r, stage))]
        dst = (h_got0, h_got1, h_got2)[stage].at[j, pl.ds(start - QKV, n)]
        return remote(src, dst, head_send.at[stage, r, j], rs_head_recv.at[stage, r, j],
                      head_to(axis, j))

    def head_sum(stage, r):
        start, n = HEAD[r]
        for j in range(3):
            head_rs_copy(stage, r, j).wait_recv()
        got = (h_got0, h_got1, h_got2)[stage]
        totals = []
        for i in range(n):
            at = (start + i,) + slot(bits, head_full(r, stage))
            total = u_buf[at].astype(F32)
            for j in range(3):
                total = total + got[j, start + i - QKV].astype(F32)
            if stage:
                u_buf[at] = total.astype(BF)
            else:
                own_ref[start + i] = total
                slab[start + i] = total.astype(BF)

    def rs_head(stage):
        for r in range(3):
            if stage < 2:
                head_sum(stage + 1, r)
            for j in range(3):
                head_rs_copy(stage, r, j).start()

    def rs_head_end():
        for r in range(3):
            head_sum(0, r)
        for r in range(3):
            for j in range(3):
                for stage in range(3):
                    head_rs_copy(stage, r, j).wait_send()

    def last_swap(i):
        at = pl.ds(0, QKV) if i == 0 else pl.ds(QKV, UNITS - QKV)
        return to_sibling(slab.at[at], sib_ref.at[at], 16 + i)

    def rows(s):
        return pl.ds(pl.multiple_of(s * 128, 128), 128)

    def unit(u):
        return u_buf[u].reshape(1024, 128)

    mine = slot(bits, ())
    for c in range(7):
        cols = slice(128 * c, 128 * c + 128)
        for r in range(2):
            t_buf[(2 * c + r,) + mine] = w_down[16 * r:16 * r + 16, cols]
    for r in range(3):
        t_buf[(14 + r,) + mine] = last_rows[16 * r:16 * r + 16, :].astype(BF)
    swap_pair.wait()
    u_buf[(slice(None),) + mine] = own_s[...] + stage[...]
    ag_head(0)
    ag_small(0)
    ag_head(1)
    ag_small(1)
    ag_head(2)
    for c in locals_:
        c.wait()
    for c in (swap_seg, swap_x, swap_e):
        c.wait()
    ag_small(2)

    causal = (lax.broadcasted_iota(jnp.int32, (128, 128), 1)
              <= lax.broadcasted_iota(jnp.int32, (128, 128), 0))

    def allowed(s):
        line = seg_all[s // 2, pl.ds(s % 2, 1), :]
        across = jnp.broadcast_to(line, (128, 128))
        return jnp.logical_and(causal, across == across.T)

    for s in range(4):
        place = jnp.sum(allowed(s).astype(F32), axis=1, keepdims=True) - 1.0
        angle = place * freq[0:1, :]
        cosine[rows(s), :] = jnp.cos(angle)
        sine[rows(s), :] = jnp.sin(angle)
    ag_small(3)
    ag_head_done()

    small = unit(49).T
    gain[...] = dot_t(small[64:80], spread[...])[0:8]
    hit = (lax.broadcasted_iota(jnp.int32, (1024, 640), 0) == brow[core, 0:1, :]).astype(BF)
    picked = dot(small[80:96], hit)
    choose = lax.broadcasted_iota(jnp.int32, (16, 640), 0) == brow[core, 1:2, :]
    bias[...] = jnp.broadcast_to(
        jnp.sum(jnp.where(choose, picked, 0.0), axis=0, keepdims=True), (8, 640))

    def inv_root(v):
        return lax.rsqrt(jnp.mean(v * v, axis=-1, keepdims=True) + EPSILON)

    @pl.loop(0, 4)
    def _(s):
        v = x_all[rows(s), :].astype(F32)
        a2s[rows(s), 0:896] = (v * inv_root(v) * gain[0:1, :]).astype(BF)

    def spread_rows(dst):
        for h in range(2):
            at = pl.ds(256 * h, 256)
            dst[at, :] = dot(a2s[at, 0:896], spread[...]).astype(BF)

    spread_rows(a1s)

    ag_small_end()
    ag(OUT, 4)
    ag(DOWN, 4)
    ag(FFN, 4)
    lane = lax.broadcasted_iota(jnp.int32, (128, 640), 1)
    first = lane % 64 < 32
    turns = lane < 512

    def wide(ref, s):
        return jnp.concatenate([ref[rows(s), :]] * 5, axis=1)

    w_qkv = jnp.concatenate([unit(QKV + i) for i in range(5)], axis=1)
    da2[:, 0:640] = dot(a1s[...], w_qkv)
    for s in range(4):
        raw = da2[rows(s), 0:640] + bias[0:1, :]
        turned = jnp.where(first, -pltpu.roll(raw, 608, 1), pltpu.roll(raw, 32, 1))
        turned = raw * wide(cosine, s) + turned * wide(sine, s)
        qkv[rows(s), :] = jnp.where(turns, turned, raw).astype(BF)
    ag(OUT, 5)
    ag(DOWN, 5)

    def heads(v):
        return jnp.concatenate([v[:, 64 * h:64 * h + 64] for h in range(7)], axis=0)

    def unheads(v):
        return jnp.concatenate([v[128 * h:128 * h + 128, :] for h in range(7)], axis=1)

    def attend(s):
        q7 = heads(qkv[rows(s), 0:448])
        k = qkv[rows(s), 448:512]
        v = qkv[rows(s), 512:576]
        score = dot_t(q7, k) * 0.125
        ok = allowed(s)
        score = jnp.where(jnp.concatenate([ok] * 7, axis=0), score, NEG_FILL)
        e = jnp.exp(score - jnp.max(score, axis=-1, keepdims=True))
        soft = e / jnp.sum(e, axis=-1, keepdims=True)
        return q7, k, v, soft

    def w_out():
        return jnp.concatenate(
            [u_buf[OUT_UNITS[i], :, :, :, :, core].reshape(512, 128) for i in range(7)], axis=1)

    def y_swap(s):
        return to_sibling(ypart.at[rows(s)], yrec.at[rows(s)], 4 + s)

    def tick(now, t, *acts):
        @pl.when(now == t)
        def _():
            for f, a in acts:
                f(*a)

    @pl.loop(0, 4)
    def _(s):
        tick(s, 2, (ag, (FFN, 5)), (ag, (FFN + 1, 4)))
        _, _, v, soft = attend(s)
        a2s[rows(s), 0:448] = unheads(dot(soft.astype(BF), v)).astype(BF)

    ag_done(OUT)
    o_s[...] = dot(a2s[:, 0:448], spread_o[core]).astype(BF)
    for h in range(2):
        at = pl.ds(256 * h, 256)
        ypart[at, :] = dot(o_s[at, :], w_out())
        for s in (2 * h, 2 * h + 1):
            y_swap(s).start()

    ag_done(DOWN)

    def slab_place(s):
        z, x, y = s // 16, s // 4 % 4, s % 4
        b = []
        for v in (x, y, z):
            low, high = gray_bits(v)
            b += [low, high]
        return slot(b, ())

    @pl.loop(0, 8)
    def _(g):
        lines, ends = [], []
        for i in range(8):
            at = slab_place(g * 8 + i)
            for r in range(2):
                lines.append(jnp.concatenate(
                    [t_buf[(2 * c + r,) + at] for c in range(7)], axis=1))
            ends += [t_buf[(14 + r,) + at] for r in range(3)]
        ends = dot(pick_in[...], jnp.concatenate(ends, axis=0)).astype(BF)
        lines.append(jnp.concatenate([ends[48 * c:48 * c + 48] for c in range(7)], axis=1))
        block = jnp.concatenate(lines, axis=0)
        wd[pl.ds(pl.multiple_of(g * 304, 16), 304), :] = dot(pack[...], block).astype(BF)

    ag(FFN + 1, 5)
    ag(FFN + 2, 4)

    @pl.loop(0, 4)
    def _(s):
        y_swap(s).wait()
        v = x_all[rows(s), :].astype(F32) + (ypart[rows(s), :] + yrec[rows(s), :])
        y1[rows(s), :] = v
        a2s[rows(s), 0:896] = (v * inv_root(v) * gain[1:2, :]).astype(BF)
        ypart[rows(s), :] = jnp.zeros((128, 896), F32)
        da2[rows(s), :] = jnp.zeros((128, 1024), F32)

    spread_rows(a2s)
    a2st[...] = a2s[...].T

    def ffn(gates, ups, row, n):
        width = 128 * n
        w = jnp.concatenate([unit(i) for i in gates + ups], axis=1)
        both = dot(a2s[...], w)
        g, u = both[:, :width], both[:, width:]
        at = pl.ds(pl.multiple_of(row, 128), width)
        w_d = wd[at, :]
        dm = dot_t(e_all[...], w_d)
        sig = 1.0 / (1.0 + jnp.exp(-g))
        silu = g * sig
        m = (silu * u).astype(BF)
        dg = (dm * u * sig * (1.0 + g * (1.0 - sig))).astype(BF)
        du = (dm * silu).astype(BF)
        dgu = jnp.concatenate([dg, du], axis=1)
        ypart[...] += dot(m, w_d)
        da2[...] += dot_t(dgu, w)
        wd[at, :] = dot(m.T, e_all[...]).astype(BF)
        for part, places in ((dg, gates), (du, ups)):
            grads = dot(a2st[...], part).astype(BF)
            for i, place in enumerate(places):
                u_buf[place] = grads[:, 128 * i:128 * i + 128].reshape((2,) * 6 + (16, 128))

    ag_done(FFN)

    @pl.loop(0, 9)
    def _(i):
        tick(i, 2, (ag, (FFN + 2, 5)))
        tick(i, 3, (rs, (FFN, 5)), (ag_done, (FFN + 1,)))
        tick(i, 6, (rs, (FFN + 1, 5)), (ag_done, (FFN + 2,)))
        wave, q = i // 3, i % 3
        g = 8 * q + 2 * wave
        u = 23 + 8 * q - q // 2 + 2 * wave
        ffn([g, g + 1], [u, u + 1], i * 256, 2)

    ffn([6], [29], 2304, 1)
    rs(FFN, 4)
    rs(FFN + 2, 5)

    other = pl.ds(pl.multiple_of((1 - core) * 256, 256), 256)
    out_swap = to_sibling(ypart.at[other], mrec, 8)
    out_swap.start()

    def unspread(v):
        n = v.shape[0]
        high = v.astype(BF)
        low = (v - high.astype(F32)).astype(BF)
        both = dot_t(jnp.concatenate([high, low], axis=0), spread[...])
        return both[:n] + both[n:]

    def unspread_rows(h):
        at = pl.ds(256 * h, 256)
        yrec[at, :] = unspread(da2[at, :])

    def da_swap(s):
        return to_sibling(yrec.at[rows(s)], darec.at[rows(s)], 9 + s)

    for h in range(2):
        unspread_rows(h)
        for s in (2 * h, 2 * h + 1):
            da_swap(s).start()

    rs(FFN + 1, 4)

    @pl.loop(0, 8)
    def _(g):
        block = dot(unpack[...], wd[pl.ds(pl.multiple_of(g * 304, 16), 304), :]).astype(BF)
        ends = jnp.concatenate([block[256:304, 128 * c:128 * c + 128] for c in range(7)], axis=0)
        ends = dot(pick_out[...], ends).astype(BF)
        for i in range(8):
            at = slab_place(g * 8 + i)
            for r in range(2):
                for c in range(7):
                    t_buf[(2 * c + r,) + at] = block[32 * i + 16 * r:32 * i + 16 * r + 16,
                                                     128 * c:128 * c + 128]
            for r in range(3):
                t_buf[(14 + r,) + at] = ends[48 * i + 16 * r:48 * i + 16 * r + 16]

    rs(DOWN, 5)
    out_swap.wait()
    for s in range(2):
        at = pl.ds(pl.multiple_of(core * 256 + 128 * s, 128), 128)
        out_ref[pl.ds(128 * s, 128), :] = (
            y1[at, :] + (ypart[at, :] + mrec[pl.ds(128 * s, 128), :])).astype(BF)

    gain_grads = gain.at[pl.ds(2, 2)]
    gain_grads[...] = jnp.zeros((2, 896), F32)

    @pl.loop(0, 4)
    def _(s):
        da_swap(s).wait()
        da = yrec[rows(s), :] + darec[rows(s), :]
        v = y1[rows(s), :]
        r = inv_root(v)

        @pl.when(s // 2 == core)
        def _():
            gain[3:4, :] += jnp.sum(da * v * r, axis=0, keepdims=True)

        w = da * gain[1:2, :]
        dy = (e_all[rows(s), :].astype(F32) + r * w
              - v * (r * r * r) * jnp.mean(w * v, axis=-1, keepdims=True))
        darec[rows(s), :] = dy
        f = dy.astype(BF)
        a2s[rows(s), 0:896] = f

    rs(FFN + 2, 4)
    w_o = w_out()
    a2st[0:512, 0:448] = dot_t(dot_t(a2s[:, 0:896], w_o).astype(BF), spread_o[core]).astype(BF)

    o_grad = dot(o_s[...].T, a2s[:, 0:896]).astype(BF)
    for i in range(7):
        part = o_grad[:, 128 * i:128 * i + 128].reshape((2,) * 5 + (16, 128))
        u_buf[OUT_UNITS[i], :, :, :, :, core] = part
        u_buf[OUT_UNITS[i], :, :, :, :, 1 - core] = jnp.zeros_like(part)
    rs(OUT, 5)
    rs_fold(FFN)
    rs_fold(FFN + 1)
    rs_small(0, 3)

    bias[...] = jnp.zeros((8, 640), F32)

    @pl.loop(0, 4)
    def _(s):
        tick(s, 2, (rs, (DOWN, 4)))
        tick(s, 3, (rs, (OUT, 4)), (rs_fold, (FFN + 2,)))
        q7, k, v, soft = attend(s)
        do7 = heads(a2st[rows(s), 0:448])
        dp = dot_t(do7, v)
        ds_ = (soft * (dp - jnp.sum(soft * dp, axis=-1, keepdims=True))).astype(BF)
        dq = unheads(dot(ds_, k)) * 0.125
        dk = dot(ds_.T, q7) * 0.125
        dv = dot(soft.astype(BF).T, do7)
        raw = jnp.concatenate([dq, dk, dv, jnp.zeros((128, 64), F32)], axis=1)
        scaled = raw * wide(sine, s)
        turned = jnp.where(first, pltpu.roll(scaled, 608, 1), -pltpu.roll(scaled, 32, 1))
        grad = jnp.where(turns, raw * wide(cosine, s) + turned, raw).astype(BF)
        qkv[rows(s), :] = grad
        bias[0:1, :] += jnp.sum(grad.astype(F32), axis=0, keepdims=True)

    rs_small(0, 2)
    w_qkv = jnp.concatenate([unit(QKV + i) for i in range(5)], axis=1)
    da2[...] = dot_t(qkv[...], w_qkv)
    rs_fold(DOWN)
    rs_fold(OUT)
    rs_small(1, 3)
    for h in range(2):
        unspread_rows(h)
    a_swap = to_sibling(yrec.at[other], arec, 13)
    a_swap.start()
    rs_small(0, 1)
    a2st[...] = a1s[...].T
    for i in range(4):
        part = dot(a2st[...], qkv[:, 128 * i:128 * i + 128])
        u_buf[QKV + i] = part.astype(BF).reshape((2,) * 6 + (16, 128))
    rs_small(1, 2)
    a_swap.wait()
    for s in range(2):
        at = pl.ds(pl.multiple_of(core * 256 + 128 * s, 128), 128)
        da = yrec[at, :] + arec[pl.ds(128 * s, 128), :]
        v = x_all[at, :].astype(F32)
        r = inv_root(v)
        gain[2:3, :] += jnp.sum(da * v * r, axis=0, keepdims=True)
        w = da * gain[0:1, :]
        gtok_ref[pl.ds(128 * s, 128), :] = (
            darec[at, :] + r * w
            - v * (r * r * r) * jnp.mean(w * v, axis=-1, keepdims=True)).astype(BF)
    rs_small(0, 0)
    top = dot(jnp.concatenate([gain[2:4, :], jnp.zeros((14, 896), F32)], axis=0).astype(BF),
              spread[...])
    spot = jnp.where(choose, jnp.broadcast_to(bias[0:1, :], (16, 640)), 0.0).astype(BF)
    hit = (lax.broadcasted_iota(jnp.int32, (1024, 640), 0) == brow[core, 0:1, :]).astype(BF)
    low = dot_t(spot, hit)
    small = jnp.concatenate(
        [jnp.zeros((64, 1024), F32), top, low, jnp.zeros((32, 1024), F32)], axis=0).T
    part = dot(a2st[...], qkv[:, 512:640]) + small
    u_buf[49] = part.astype(BF).reshape((2,) * 6 + (16, 128))
    rs_head(2)
    rs_small(1, 1)
    rs_small_end(0)
    rs_head(1)
    rs_small(1, 0)
    rs_head(0)
    rs_small_end(1)
    last_swap(0).start()
    rs_head_end()
    last_swap(1).start()
    rs_sent()
    for i in range(2):
        last_swap(i).wait()


def layer(*arrays):
    dma = pltpu.SemaphoreType.DMA
    vm = pltpu.VMEM
    return pl.pallas_call(
        layer_kernel,
        out_shape=(
            jax.ShapeDtypeStruct((256, 896), BF),
            jax.ShapeDtypeStruct((256, 896), BF),
            jax.ShapeDtypeStruct((UNITS + TALL, 16, 128), F32),
            jax.ShapeDtypeStruct((UNITS, 16, 128), BF),
        ),
        in_specs=[pl.BlockSpec(memory_space=vm)] * 10 + [pl.BlockSpec(memory_space=pl.ANY)] * 6
        + [pl.BlockSpec(memory_space=vm)] * 4,
        out_specs=[pl.BlockSpec(memory_space=vm)] * 4,
        scratch_shapes=[
            vm((UNITS,) + (2,) * 6 + (16, 128), BF), vm((TALL,) + (2,) * 6 + (16, 128), BF),
            vm((QKV,) + (2,) * 5 + (16, 128), BF), vm((TALL,) + (2,) * 5 + (16, 128), BF),
            vm((2432, 896), BF), vm((512, 896), BF), vm((512, 896), BF), vm((2, 8, 128), F32),
            vm((UNITS, 16, 128), BF), vm((512, 1024), BF), vm((512, 1024), BF),
            vm((1024, 512), BF), vm((512, 640), BF), vm((512, 512), BF),
            vm((512, 896), F32), vm((512, 896), F32), vm((512, 896), F32), vm((512, 1024), F32),
            vm((512, 896), F32), vm((256, 896), F32), vm((256, 896), F32), vm((512, 128), F32), vm((512, 128), F32),
            vm((8, 896), F32), vm((8, 640), F32), vm((UNITS, 16, 128), BF),
            vm((8, RAW), F32), vm((48, 128), F32), vm((UNITS, 16, 128), BF),
            vm((UNITS, 16, 128), BF), vm((8, 128), F32), vm((896, 1024), BF), vm((2, 448, 512), BF),
            vm((304, 304), BF), vm((304, 304), BF),
            vm((3, 5, 16, 128), BF), vm((3, 5) + (2,) * 2 + (16, 128), BF),
            vm((3, 5) + (2,) * 4 + (16, 128), BF),
            dma((4, 6, 2)), dma((4, 6, 3)), dma((4, 6, 3)), dma((5, 2, 6)), dma((5, 2, 6)),
            dma((5, 2, 6)), dma((3, 3, 3)), dma((3, 3, 3)), dma((3, 3, 3)),
            pltpu.SemaphoreType.REGULAR((7, 6)),
            dma((21,)), dma((21,)), dma((6,)),
        ],
        compiler_params=pltpu.CompilerParams(collective_id=0, has_side_effects=True,
                                             vmem_limit_bytes=60 * 2**20),
    )(*arrays)


def finish_kernel(own, sib, out, tok, out_ref, tok_ref, q_ref, k_ref, v_ref, o_ref, g_ref, u_ref,
                  d_ref, gain_ref, bias_ref):
    out_ref[...] = out[...]
    tok_ref[...] = tok[...]
    for c in range(7):
        for r in range(2):
            d_ref[16 * r:16 * r + 16, 128 * c:128 * c + 128] = own[UNITS + 2 * c + r]
    ends = jnp.concatenate([own[UNITS + 14 + r] for r in range(3)], axis=0)
    for c in range(7):
        d_ref[32:38, 128 * c:128 * c + 128] = ends[6 * c:6 * c + 6]
    core = lax.axis_index("dp") % 2
    for c in range(2):
        @pl.when(core == c)
        def _():
            def mine(u):
                return own[u, 8 * c:8 * c + 8, :]

            def theirs(u):
                return sib[u].astype(F32)[8 * c:8 * c + 8]

            def half(plane, u, h):
                return (mine if plane == c else theirs)(u)[:, 64 * h:64 * h + 64]

            def put(ref, count, where):
                for n in range(count):
                    (p0, u0, h0), (p1, u1, h1) = where(2 * n), where(2 * n + 1)
                    if (p0, u0, h0, h1) == (p1, u1, 0, 1):
                        v = (mine if p0 == c else theirs)(u0)
                    else:
                        v = jnp.concatenate([half(p0, u0, h0), half(p1, u1, h1)], axis=1)
                    ref[:, 128 * n:128 * n + 128] = v[0:7]

            def hidden(table):
                def where(h):
                    t = h // 38 * 19 + h % 19
                    return h // 19 % 2, table[t // 2], t % 2
                return where

            put(g_ref, 38, hidden(GATE_UNITS))
            put(u_ref, 38, hidden(UP_UNITS))
            put(q_ref, 7, lambda h: (h // 7, QKV + h % 7 // 2, h % 7 % 2))
            put(k_ref, 1, lambda h: (h, QKV + 3, 1))
            put(v_ref, 1, lambda h: (h, QKV + 4, 0))
            for j, u in enumerate(OUT_UNITS):
                o_ref[:, 128 * j:128 * j + 128] = (mine(u) + theirs(u))[0:7]
            small = mine(QKV + 4) + theirs(QKV + 4)
            gain_ref[...] = small.T[64:66, 0:7]
            bias_ref[...] = small[0:1, 80:89]


def finish(own, sib, out, tok):
    vm = pl.BlockSpec(memory_space=pltpu.VMEM)
    shapes = [((256, 896), BF), ((256, 896), BF), ((7, 896), F32), ((7, 128), F32),
              ((7, 128), F32), ((7, 896), F32), ((7, 4864), F32), ((7, 4864), F32),
              ((38, 896), F32), ((2, 7), F32), ((1, 9), F32)]
    return pl.pallas_call(
        finish_kernel,
        out_shape=tuple(jax.ShapeDtypeStruct(s, d) for s, d in shapes),
        in_specs=[vm] * 4, out_specs=[vm] * 11,
    )(own, sib, out, tok)


def constants():
    slots = np.zeros(128, np.int32)
    for n in range(128):
        dp, fs = n // 32, n % 32
        x, y, z, core = fs // 4 % 4, fs % 4, (dp // 2) * 2 + fs // 16, dp % 2
        slots[n] = ((GRAY[x] * 4 + GRAY[y]) * 4 + GRAY[z]) * 2 + core
    spread = np.zeros((896, 1024), np.float32)
    for d in range(896):
        spread[d, slots[d // 7] * 8 + d % 7] = 1.0
    spread_o = np.zeros((2, 448, 512), np.float32)
    for c in range(2):
        part = spread[448 * c:448 * c + 448].reshape(448, 16, 2, 32)
        spread_o[c] = part[:, :, c].reshape(448, 512)
    unpack = np.zeros((304, 304), np.float32)
    pick_in = np.zeros((336, 384), np.float32)
    for a in range(8):
        for r in range(38):
            unpack[32 * a + r if r < 32 else 256 + 6 * a + r - 32, 38 * a + r] = 1.0
        for r in range(6):
            for c in range(7):
                pick_in[48 * c + 6 * a + r, 48 * a + 6 * c + r] = 1.0
    brow = np.full((2, 8, 640), -1, np.int32)
    for c in range(2):
        for i in range(576):
            if i < 448:
                nat = 448 * c + i
            elif i < 512:
                nat = 896 + 64 * c + i - 448
            else:
                nat = 1024 + 64 * c + i - 512
            brow[c, 0, i] = slots[nat // 9] * 8
            brow[c, 1, i] = nat % 9
    freq = THETA ** (-2.0 * (np.arange(128) % 32) / 64.0)
    freq = np.concatenate([freq[None], np.zeros((7, 128))]).astype(np.float32)
    return (jnp.asarray(spread, BF), jnp.asarray(spread_o, BF), jnp.asarray(unpack.T, BF),
            jnp.asarray(unpack, BF), jnp.asarray(pick_in, BF), jnp.asarray(pick_in.T, BF),
            jnp.asarray(brow), jnp.asarray(freq))


def shards(tokens, segments, w_query, w_key, w_value, w_out, w_gate, w_up, w_down, gains, biases,
           cotangent):
    out, tok, own, sib = layer(
        w_query, w_key, w_value, w_out, w_gate, w_up, w_down, gains.T, biases.reshape(1, 9),
        segments.reshape(2, 128), tokens.reshape(256, 896), cotangent.reshape(256, 896),
        *constants())
    out, tok, *grads, gain, bias = finish(own, sib, out, tok)
    return (out.reshape(tokens.shape), tok.reshape(tokens.shape), *grads, gain.T,
            bias.reshape(9))


def solution(mesh):
    row = P(AXES, None)
    batch = P(None, AXES, None, None)
    return jax.shard_map(
        shards, mesh=mesh,
        in_specs=(batch, P(None, AXES, None)) + (row,) * 8 + (P(AXES), batch),
        out_specs=(batch, batch) + (row,) * 8 + (P(AXES),),
        check_vma=False,
    )
```

```python
import functools

import jax
import jax.numpy as jnp
import numpy as np
from jax import lax
from jax.experimental import pallas as pl
from jax.experimental.pallas import tpu as pltpu
from jax.sharding import PartitionSpec as P

EPSILON = 1e-06
THETA = 1000000.0
NEG_FILL = -1e30
MESH = pl.DeviceIdType.MESH
AXES = ("dp", "fsdp")
BF = jnp.bfloat16
F32 = jnp.float32
GRAY = (0, 1, 3, 2)

BULK = ((0, 8), (8, 8), (16, 7), (23, 8), (31, 7), (38, 7))
TALLS = ((0, 3), (3, 3), (6, 3), (9, 3), (12, 3), (15, 2))
WAVES = (
    ((7, 1), (14, 2), (22, 1), (30, 1), (37, 1), (44, 1)),
    TALLS,
    ((0, 3), (8, 2), (16, 2), (23, 3), (31, 2), (38, 2)),
    ((3, 2), (10, 2), (18, 2), (26, 2), (33, 2), (40, 2)),
    ((5, 2), (12, 2), (20, 2), (28, 2), (35, 2), (42, 2)),
)
EARLY = ((0, 5), (8, 4), (16, 4), (23, 5), (31, 4), (38, 4))
LATE = ((5, 3), (12, 4), (20, 3), (28, 3), (35, 3), (42, 3))
OUT, DOWN, FFN = 0, 1, 2
OUT_UNITS = (7, 14, 15, 22, 30, 37, 44)
HEAD = ((45, 2), (47, 2), (49, 1))
UNITS, TALL, QKV = 50, 17, 45


def pair_units(starts, last):
    return tuple(starts[j % 6 // 2] + 2 * (j // 6) + j % 2 + (j > 5 and j % 6 < 2)
                 for j in range(18)) + (last,)


GATE_UNITS = pair_units((0, 8, 16), 2)
UP_UNITS = pair_units((23, 31, 38), 25)
GATE_AT, UP_AT, Q_AT, K_AT, V_AT, O_AT, S_AT, RAW = (
    0, 4864, 9728, 10624, 10752, 10880, 11776, 11904)
ORDER = tuple(
    tuple(2 * ((p % 3 + k // 2) % 3) + ((k % 2) ^ (p // 3)) for k in range(6)) for p in range(6)
)


def here():
    dp = lax.axis_index("dp")
    fs = lax.axis_index("fsdp")
    return (fs // 4) % 4, fs % 4, (dp // 2) * 2 + fs // 16, dp % 2


def device(x, y, z, core):
    return ((z // 2) * 2 + core, (z % 2) * 16 + x * 4 + y)


def gray_bits(v):
    high = v // 2
    low = (v % 2 + high) % 2
    return low, high


def flip(v, bit):
    if bit == 0:
        return v + 1 - 2 * (v % 2)
    return 3 - v


def partner(bit):
    x, y, z, core = here()
    axis, low = bit // 2, bit % 2
    place = [x, y, z]
    place[axis] = flip(place[axis], low)
    return device(*place, core)


def sibling():
    x, y, z, core = here()
    return device(x, y, z, 1 - core)


def my_bits():
    x, y, z, _ = here()
    bits = []
    for v in (x, y, z):
        low, high = gray_bits(v)
        bits += [low, high]
    return bits


DIMS = (1, 0, 3, 2, 5, 4)


def slot(bits, full):
    return tuple(slice(None) if b in full else bits[b] for b in DIMS)


def far(axis):
    x, y, z, core = here()
    place = [x, y, z]
    place[axis] = 3 - flip(place[axis], 0)
    return device(*place, core)


def dot(a, b):
    return lax.dot_general(a, b, (((1,), (0,)), ((), ())), preferred_element_type=F32)


def dot_t(a, b):
    return lax.dot_general(a, b, (((1,), (1,)), ((), ())), preferred_element_type=F32)


def layer_kernel(
    w_query, w_key, w_value, w_out_, w_gate, w_up, w_down, gains, biases, segments,
    x_own, e_own, spread_h, spread_o_h, pack_h, unpack_h, pick_in, pick_out, brow, freq,
    out_ref, gtok_ref, own_ref, sib_ref,
    u_buf, t_buf, u_got, t_got, wd, x_all, e_all, seg_all, stage, a1s, a2s, a2st, qkv, o_s,
    y1, ypart, yrec, da2, darec, mrec, arec, cosine, sine, gain, bias, slab,
    raw, last_rows, own_s, send_s, seg_own, spread, spread_o, pack, unpack,
    h_got0, h_got1, h_got2, ag_small_recv, rs_small_recv, small_send, ag_big_recv, rs_big_recv,
    big_send, ag_head_recv, rs_head_recv, head_send, credit, sib_send, sib_recv, loc_sem,
):
    _, _, _, core = here()
    bits = my_bits()
    flipped = [1 - b for b in bits]
    sib = sibling()
    peers = [partner(b) for b in range(6)]
    across_ = [far(a) for a in range(3)]

    barrier = pltpu.get_barrier_semaphore()
    for d in peers + across_ + [sib]:
        pl.semaphore_signal(barrier, inc=1, device_id=d, device_id_type=MESH)

    def to_sibling(src, dst, i):
        return pltpu.make_async_remote_copy(
            src_ref=src, dst_ref=dst, send_sem=sib_send.at[i], recv_sem=sib_recv.at[i],
            device_id=sib, device_id_type=MESH)

    own = pl.ds(pl.multiple_of(core * 256, 256), 256)
    locals_ = [
        pltpu.make_async_copy(a, b, loc_sem.at[i]) for i, (a, b) in enumerate((
            (x_own, x_all.at[own]), (e_own, e_all.at[own]), (spread_h, spread),
            (spread_o_h, spread_o), (pack_h, pack), (unpack_h, unpack)))]
    for c in locals_:
        c.start()

    raw[...] = jnp.zeros((8, RAW), F32)
    for ref, a in ((w_gate, GATE_AT), (w_up, UP_AT), (w_query, Q_AT), (w_key, K_AT),
                   (w_value, V_AT), (w_out_, O_AT)):
        raw[0:7, a:a + ref.shape[1]] = ref[...].astype(F32)
    last_rows[0:8, :] = jnp.zeros((8, 128), F32)
    last_rows[0:2, 0:7] = gains[...].astype(F32)
    raw[0:7, S_AT:S_AT + 2] = last_rows[0:8, :].T[0:7, 0:2]
    raw[0:1, S_AT + 16:S_AT + 25] = biases[...].astype(F32)
    seg_own[...] = jnp.zeros((8, 128), F32)
    seg_own[0:2, :] = segments[...].astype(F32)
    last_rows[...] = jnp.zeros((48, 128), F32)
    ends = w_down[32:38, :].astype(F32)
    for c in range(7):
        last_rows[6 * c:6 * c + 6, :] = ends[:, 128 * c:128 * c + 128]

    def lanes(first, second):
        if second == first + 64:
            return raw[:, first:first + 128]
        return jnp.concatenate([raw[:, first:first + 64], raw[:, second:second + 64]], axis=1)

    def hidden_at(base, c, h):
        return base + 1216 * (2 * (h // 19) + c) + 64 * (h % 19)

    def head_at(c, h):
        return (Q_AT + 448 * c + 64 * h, K_AT + 64 * c, V_AT + 64 * c, S_AT)[max(0, h - 6)]

    def units_of(c):
        for table, base in ((GATE_UNITS, GATE_AT), (UP_UNITS, UP_AT)):
            for j, place in enumerate(table):
                yield place, lanes(hidden_at(base, c, 2 * j), hidden_at(base, c, 2 * j + 1))
        for j in range(5):
            yield QKV + j, lanes(head_at(c, 2 * j), head_at(c, 2 * j + 1))
        for j, place in enumerate(OUT_UNITS):
            yield place, raw[:, O_AT + 128 * j:O_AT + 128 * j + 128]

    def fill(dst, other):
        for c in range(2):
            @pl.when(core == c)
            def _():
                zero = jnp.zeros((8, 128), F32)
                for place, v in units_of(1 - c if other else c):
                    tile = jnp.concatenate([zero, v] if c else [v, zero], axis=0)
                    dst[place] = tile.astype(BF)

    def remote(src, dst, send, recv, to):
        return pltpu.make_async_remote_copy(
            src_ref=src, dst_ref=dst, send_sem=send, recv_sem=recv, device_id=to,
            device_id_type=MESH)

    BOTH = ((u_buf, BULK), (t_buf, TALLS))

    def bufs(w):
        return (t_buf, t_got) if w == DOWN else (u_buf, u_got)

    def small_copy(k, p, i):
        buf, parts = BOTH[i]
        ref = buf.at[(pl.ds(*parts[p]),) + slot(bits, ORDER[p][:k])]
        return remote(ref, ref, small_send.at[k, p, i], ag_small_recv.at[k, p, i],
                      peers[ORDER[p][k]])

    def ag_small(k, i):
        for p in range(6):
            if k > 0:
                small_copy(k - 1, p, i).wait_recv()
            small_copy(k, p, i).start()

    def ag_small_end(i):
        for p in range(6):
            small_copy(3, p, i).wait_recv()

    def ag_small_sent():
        for i in range(2):
            for p in range(6):
                for k in range(4):
                    small_copy(k, p, i).wait_send()

    is_mine = bits[5] == core

    def when(test, f):
        if test is None:
            f()
        else:
            pl.when(test)(f)

    def open_bit(w, k, p):
        return ORDER[p].index(5) - k if w == OUT else None

    def ag_tests(w, k, p):
        at = open_bit(w, k, p)
        if at is None or at < 0:
            return None, None
        return is_mine, (jnp.logical_not(is_mine) if at == 0 else is_mine)

    def rs_tests(w, k, p):
        send, take = ag_tests(w, k, p)
        return take, send

    def cut(w, k, p, b, full):
        if w == OUT and open_bit(w, k, p) < 0:
            b, full = list(b), [i for i in full if i != 5]
            b[5] = core
        return slot(b, full)

    def ag_copy(w, k, p):
        order = ORDER[p]
        ref = bufs(w)[0].at[(pl.ds(*WAVES[w][p]),) + cut(w, k, p, bits, order[:k])]
        return remote(ref, ref, big_send.at[w, k - 4, p], ag_big_recv.at[w, k - 4, p],
                      peers[order[k]])

    def ag(w, k):
        for p in range(6):
            if k == 5:
                when(ag_tests(w, 4, p)[1], ag_copy(w, 4, p).wait_recv)
            when(ag_tests(w, k, p)[0], ag_copy(w, k, p).start)

    def ag_done(w):
        for p in range(6):
            when(ag_tests(w, 5, p)[1], ag_copy(w, 5, p).wait_recv)
        for p in range(6):
            for k in (4, 5):
                when(ag_tests(w, k, p)[0], ag_copy(w, k, p).wait_send)

    def given(k, p, *more):
        b = list(bits)
        for j in (k,) + more:
            b[ORDER[p][j]] = flipped[ORDER[p][j]]
        return slot(b, ORDER[p][:k])

    def flipped_at(p, *steps):
        b = list(bits)
        for j in steps:
            b[ORDER[p][j]] = flipped[ORDER[p][j]]
        return b

    def got_at(w, p):
        if w == OUT and ORDER[p][5] != 5:
            return tuple(core if b == 5 else slice(None) for b in DIMS if b != ORDER[p][5])
        return ()

    def rs_copy(w, k, p):
        acc, got = bufs(w)
        units = pl.ds(*WAVES[w][p])
        full = ORDER[p][:k]
        src = acc.at[(units,) + cut(w, k, p, flipped_at(p, k), full)]
        if k == 5:
            dst = got.at[(units,) + got_at(w, p)]
        else:
            dst = acc.at[(units,) + cut(w, k, p, flipped_at(p, 5), full)]
        return remote(src, dst, big_send.at[w, k - 4, p], rs_big_recv.at[w, k - 4, p],
                      peers[ORDER[p][k]])

    def rs_add(acc, got, part, k, p, w=None):
        start, n = part
        full = ORDER[p][:k]
        mine_ = cut(w, k, p, bits, full)
        there = cut(w, k, p, flipped_at(p, 5, k), full)

        def one(u):
            add = got[(u,) + got_at(w, p)] if k == 5 else acc[(u,) + there]
            acc[(u,) + mine_] = acc[(u,) + mine_] + add

        if k >= 2:
            @pl.loop(0, n)
            def _(i):
                one(start + i)
        else:
            for i in range(n):
                one(start + i)

    def rs_take(w, k, p):
        acc, got = bufs(w)

        def take():
            rs_copy(w, k, p).wait_recv()
            rs_add(acc, got, WAVES[w][p], k, p, w)

        when(rs_tests(w, k, p)[1], take)

    def rs(w, k):
        if k == 4:
            for p in range(6):
                when(rs_tests(w, 5, p)[0], rs_copy(w, 5, p).wait_send)
            for b in range(6):
                pl.semaphore_signal(credit.at[w, b], inc=1, device_id=peers[b],
                                    device_id_type=MESH)
        for p in range(6):
            if k == 4:
                rs_take(w, 5, p)
                pl.semaphore_wait(credit.at[w, ORDER[p][4]], 1)
            when(rs_tests(w, k, p)[0], rs_copy(w, k, p).start)

    def rs_fold(w):
        for p in range(6):
            rs_take(w, 4, p)

    GROUPS = (((u_buf, EARLY),), ((u_buf, LATE), (t_buf, TALLS)))

    def rs_small_copy(g, k, p, i):
        buf, parts = GROUPS[g][i]
        units = pl.ds(*parts[p])
        b = list(bits)
        b[ORDER[p][5]] = flipped[ORDER[p][5]]
        return remote(buf.at[(units,) + given(k, p)], buf.at[(units,) + slot(b, ORDER[p][:k])],
                      small_send.at[k, p, g + i], rs_small_recv.at[k, p, g + i],
                      peers[ORDER[p][k]])

    def rs_small(g, k):
        if k == 3:
            for b in range(6):
                pl.semaphore_signal(credit.at[5 + g, b], inc=1, device_id=peers[b],
                                    device_id_type=MESH)
        for i in range(len(GROUPS[g])):
            for p in range(6):
                if k == 3:
                    if i == 0:
                        pl.semaphore_wait(credit.at[5 + g, ORDER[p][3]], 1)
                else:
                    rs_small_copy(g, k + 1, p, i).wait_recv()
                    rs_add(GROUPS[g][i][0], None, GROUPS[g][i][1][p], k + 1, p)
                rs_small_copy(g, k, p, i).start()

    def rs_small_end(g):
        for i, (buf, parts) in enumerate(GROUPS[g]):
            for p in range(6):
                start, n = parts[p]
                units = pl.ds(start, n)
                rs_small_copy(g, 0, p, i).wait_recv()
                total = (buf[(units,) + slot(bits, ())].astype(F32)
                         + buf[(units,) + given(0, p, 5)].astype(F32))
                own_ref[pl.ds(start + i * UNITS, n)] = total
                if i == 0:
                    slab[units] = total.astype(BF)

    def rs_sent():
        for p in range(6):
            for w in range(5):
                when(rs_tests(w, 4, p)[0], rs_copy(w, 4, p).wait_send)
            for g, i in ((0, 0), (1, 0), (1, 1)):
                for k in range(4):
                    rs_small_copy(g, k, p, i).wait_send()

    def turned_bits(axis, j):
        b = list(bits)
        for i in ((0,), (1,), (0, 1))[j]:
            b[2 * axis + i] = flipped[2 * axis + i]
        return b

    def head_to(axis, j):
        return across_[axis] if j == 2 else peers[2 * axis + j]

    def head_full(r, stage):
        return [2 * ((r + i) % 3) + j for i in range(stage) for j in range(2)]

    def head_copy(stage, r, j):
        ref = u_buf.at[(pl.ds(*HEAD[r]),) + slot(bits, head_full(r, stage))]
        return remote(ref, ref, head_send.at[stage, r, j], ag_head_recv.at[stage, r, j],
                      head_to((r + stage) % 3, j))

    def ag_head(stage):
        for r in range(3):
            for j in range(3):
                if stage > 0:
                    head_copy(stage - 1, r, j).wait_recv()
            for j in range(3):
                head_copy(stage, r, j).start()

    def ag_head_done():
        for r in range(3):
            for j in range(3):
                head_copy(2, r, j).wait_recv()
        for r in range(3):
            for j in range(3):
                for stage in range(3):
                    head_copy(stage, r, j).wait_send()

    def head_rs_copy(stage, r, j):
        start, n = HEAD[r]
        axis = (r + stage) % 3
        src = u_buf.at[(pl.ds(start, n),) + slot(turned_bits(axis, j), head_full(r, stage))]
        dst = (h_got0, h_got1, h_got2)[stage].at[j, pl.ds(start - QKV, n)]
        return remote(src, dst, head_send.at[stage, r, j], rs_head_recv.at[stage, r, j],
                      head_to(axis, j))

    def head_sum(stage, r):
        start, n = HEAD[r]
        for j in range(3):
            head_rs_copy(stage, r, j).wait_recv()
        got = (h_got0, h_got1, h_got2)[stage]
        totals = []
        for i in range(n):
            at = (start + i,) + slot(bits, head_full(r, stage))
            total = u_buf[at].astype(F32)
            for j in range(3):
                total = total + got[j, start + i - QKV].astype(F32)
            if stage:
                u_buf[at] = total.astype(BF)
            else:
                own_ref[start + i] = total
                slab[start + i] = total.astype(BF)

    def rs_head(stage):
        for r in range(3):
            if stage < 2:
                head_sum(stage + 1, r)
            for j in range(3):
                head_rs_copy(stage, r, j).start()

    def rs_head_end():
        for r in range(3):
            head_sum(0, r)
        for r in range(3):
            for j in range(3):
                for stage in range(3):
                    head_rs_copy(stage, r, j).wait_send()

    def last_swap(i):
        at = pl.ds(0, QKV) if i == 0 else pl.ds(QKV, UNITS - QKV)
        return to_sibling(slab.at[at], sib_ref.at[at], 16 + i)

    mine = slot(bits, ())
    for c in range(7):
        cols = slice(128 * c, 128 * c + 128)
        for r in range(2):
            t_buf[(2 * c + r,) + mine] = w_down[16 * r:16 * r + 16, cols]
    for r in range(3):
        t_buf[(14 + r,) + mine] = last_rows[16 * r:16 * r + 16, :].astype(BF)
    fill(send_s, True)
    pl.semaphore_wait(barrier, 10)
    swap_pair = to_sibling(send_s, stage, 0)
    swap_pair.start()
    ag_small(0, 1)
    swap_seg = to_sibling(seg_own, seg_all.at[core], 1)
    swap_x = to_sibling(x_own, x_all.at[own], 2)
    swap_e = to_sibling(e_own, e_all.at[own], 3)
    for c in (swap_seg, swap_x, swap_e):
        c.start()
    fill(own_s, False)
    seg_all[core] = seg_own[...]

    def rows(s):
        return pl.ds(pl.multiple_of(s * 128, 128), 128)

    def unit(u):
        return u_buf[u].reshape(1024, 128)

    swap_pair.wait()
    u_buf[(slice(None),) + mine] = own_s[...] + stage[...]
    ag_head(0)
    ag_small(0, 0)
    ag_small(1, 1)
    ag_head(1)
    ag_small(1, 0)
    ag_small(2, 1)
    ag_head(2)
    for c in locals_:
        c.wait()
    for c in (swap_seg, swap_x, swap_e):
        c.wait()
    ag_small(3, 1)
    ag_small(2, 0)

    causal = (lax.broadcasted_iota(jnp.int32, (128, 128), 1)
              <= lax.broadcasted_iota(jnp.int32, (128, 128), 0))

    def allowed(s):
        line = seg_all[s // 2, pl.ds(s % 2, 1), :]
        across = jnp.broadcast_to(line, (128, 128))
        return jnp.logical_and(causal, across == across.T)

    for s in range(4):
        place = jnp.sum(allowed(s).astype(F32), axis=1, keepdims=True) - 1.0
        angle = place * freq[0:1, :]
        cosine[rows(s), :] = jnp.cos(angle)
        sine[rows(s), :] = jnp.sin(angle)
    ag_small_end(1)
    ag(DOWN, 4)
    ag_small(3, 0)
    ag_head_done()

    small = unit(49).T
    gain[...] = dot_t(small[64:80], spread[...])[0:8]
    hit = (lax.broadcasted_iota(jnp.int32, (1024, 640), 0) == brow[core, 0:1, :]).astype(BF)
    picked = dot(small[80:96], hit)
    choose = lax.broadcasted_iota(jnp.int32, (16, 640), 0) == brow[core, 1:2, :]
    bias[...] = jnp.broadcast_to(
        jnp.sum(jnp.where(choose, picked, 0.0), axis=0, keepdims=True), (8, 640))

    def inv_root(v):
        return lax.rsqrt(jnp.mean(v * v, axis=-1, keepdims=True) + EPSILON)

    @pl.loop(0, 4)
    def _(s):
        v = x_all[rows(s), :].astype(F32)
        a2s[rows(s), 0:896] = (v * inv_root(v) * gain[0:1, :]).astype(BF)

    def spread_rows(dst):
        for h in range(2):
            at = pl.ds(256 * h, 256)
            dst[at, :] = dot(a2s[at, 0:896], spread[...]).astype(BF)

    spread_rows(a1s)

    ag_small_end(0)
    ag(OUT, 4)
    ag(FFN, 4)
    lane = lax.broadcasted_iota(jnp.int32, (128, 640), 1)
    first = lane % 64 < 32
    turns = lane < 512

    def wide(ref, s):
        return jnp.concatenate([ref[rows(s), :]] * 5, axis=1)

    w_qkv = jnp.concatenate([unit(QKV + i) for i in range(5)], axis=1)
    da2[:, 0:640] = dot(a1s[...], w_qkv)
    for s in range(4):
        raw = da2[rows(s), 0:640] + bias[0:1, :]
        turned = jnp.where(first, -pltpu.roll(raw, 608, 1), pltpu.roll(raw, 32, 1))
        turned = raw * wide(cosine, s) + turned * wide(sine, s)
        qkv[rows(s), :] = jnp.where(turns, turned, raw).astype(BF)
    ag(OUT, 5)
    ag(DOWN, 5)

    def heads(v):
        return jnp.concatenate([v[:, 64 * h:64 * h + 64] for h in range(7)], axis=0)

    def unheads(v):
        return jnp.concatenate([v[128 * h:128 * h + 128, :] for h in range(7)], axis=1)

    def attend(s):
        q7 = heads(qkv[rows(s), 0:448])
        k = qkv[rows(s), 448:512]
        v = qkv[rows(s), 512:576]
        score = dot_t(q7, k) * 0.125
        ok = allowed(s)
        score = jnp.where(jnp.concatenate([ok] * 7, axis=0), score, NEG_FILL)
        e = jnp.exp(score - jnp.max(score, axis=-1, keepdims=True))
        soft = e / jnp.sum(e, axis=-1, keepdims=True)
        return q7, k, v, soft

    def w_out():
        return jnp.concatenate(
            [u_buf[OUT_UNITS[i], :, :, :, :, core].reshape(512, 128) for i in range(7)], axis=1)

    def y_swap(s):
        return to_sibling(ypart.at[rows(s)], yrec.at[rows(s)], 4 + s)

    def tick(now, t, *acts):
        @pl.when(now == t)
        def _():
            for f, a in acts:
                f(*a)

    @pl.loop(0, 4)
    def _(s):
        tick(s, 2, (ag, (FFN, 5)), (ag, (FFN + 1, 4)))
        _, _, v, soft = attend(s)
        a2s[rows(s), 0:448] = unheads(dot(soft.astype(BF), v)).astype(BF)

    ag_done(OUT)
    ag_small_sent()
    o_s[...] = dot(a2s[:, 0:448], spread_o[core]).astype(BF)
    for h in range(2):
        at = pl.ds(256 * h, 256)
        ypart[at, :] = dot(o_s[at, :], w_out())
        for s in (2 * h, 2 * h + 1):
            y_swap(s).start()

    ag_done(DOWN)

    def slab_place(s):
        z, x, y = s // 16, s // 4 % 4, s % 4
        b = []
        for v in (x, y, z):
            low, high = gray_bits(v)
            b += [low, high]
        return slot(b, ())

    @pl.loop(0, 8)
    def _(g):
        lines, ends = [], []
        for i in range(8):
            at = slab_place(g * 8 + i)
            for r in range(2):
                lines.append(jnp.concatenate(
                    [t_buf[(2 * c + r,) + at] for c in range(7)], axis=1))
            ends += [t_buf[(14 + r,) + at] for r in range(3)]
        ends = dot(pick_in[...], jnp.concatenate(ends, axis=0)).astype(BF)
        lines.append(jnp.concatenate([ends[48 * c:48 * c + 48] for c in range(7)], axis=1))
        block = jnp.concatenate(lines, axis=0)
        wd[pl.ds(pl.multiple_of(g * 304, 16), 304), :] = dot(pack[...], block).astype(BF)

    ag(FFN + 1, 5)
    ag(FFN + 2, 4)

    @pl.loop(0, 4)
    def _(s):
        y_swap(s).wait()
        v = x_all[rows(s), :].astype(F32) + (ypart[rows(s), :] + yrec[rows(s), :])
        y1[rows(s), :] = v
        a2s[rows(s), 0:896] = (v * inv_root(v) * gain[1:2, :]).astype(BF)
        ypart[rows(s), :] = jnp.zeros((128, 896), F32)
        da2[rows(s), :] = jnp.zeros((128, 1024), F32)

    spread_rows(a2s)
    a2st[...] = a2s[...].T

    def ffn(gates, ups, row, n):
        width = 128 * n
        w = jnp.concatenate([unit(i) for i in gates + ups], axis=1)
        both = dot(a2s[...], w)
        g, u = both[:, :width], both[:, width:]
        at = pl.ds(pl.multiple_of(row, 128), width)
        w_d = wd[at, :]
        dm = dot_t(e_all[...], w_d)
        sig = 1.0 / (1.0 + jnp.exp(-g))
        silu = g * sig
        m = (silu * u).astype(BF)
        dg = (dm * u * sig * (1.0 + g * (1.0 - sig))).astype(BF)
        du = (dm * silu).astype(BF)
        dgu = jnp.concatenate([dg, du], axis=1)
        ypart[...] += dot(m, w_d)
        da2[...] += dot_t(dgu, w)
        wd[at, :] = dot(m.T, e_all[...]).astype(BF)
        for part, places in ((dg, gates), (du, ups)):
            grads = dot(a2st[...], part).astype(BF)
            for i, place in enumerate(places):
                u_buf[place] = grads[:, 128 * i:128 * i + 128].reshape((2,) * 6 + (16, 128))

    ag_done(FFN)
    ffn([2], [25], 2304, 1)

    @pl.loop(0, 9)
    def _(i):
        tick(i, 2, (ag, (FFN + 2, 5)))
        tick(i, 3, (rs, (FFN, 5)), (ag_done, (FFN + 1,)))
        tick(i, 6, (rs, (FFN + 1, 5)), (ag_done, (FFN + 2,)))
        wave, q = i // 3, i % 3
        odd = (2 - q) // 2 * ((wave + 1) // 2)
        g = 8 * q + 2 * wave + odd
        u = 23 + 8 * q - q // 2 + 2 * wave + odd
        ffn([g, g + 1], [u, u + 1], i * 256, 2)

    rs(FFN, 4)
    rs(FFN + 2, 5)

    other = pl.ds(pl.multiple_of((1 - core) * 256, 256), 256)
    out_swap = to_sibling(ypart.at[other], mrec, 8)
    out_swap.start()

    def unspread(v):
        n = v.shape[0]
        high = v.astype(BF)
        low = (v - high.astype(F32)).astype(BF)
        both = dot_t(jnp.concatenate([high, low], axis=0), spread[...])
        return both[:n] + both[n:]

    def unspread_rows(h):
        at = pl.ds(256 * h, 256)
        yrec[at, :] = unspread(da2[at, :])

    def da_swap(s):
        return to_sibling(yrec.at[rows(s)], darec.at[rows(s)], 9 + s)

    for h in range(2):
        unspread_rows(h)
        for s in (2 * h, 2 * h + 1):
            da_swap(s).start()

    rs(FFN + 1, 4)

    @pl.loop(0, 8)
    def _(g):
        block = dot(unpack[...], wd[pl.ds(pl.multiple_of(g * 304, 16), 304), :]).astype(BF)
        ends = jnp.concatenate([block[256:304, 128 * c:128 * c + 128] for c in range(7)], axis=0)
        ends = dot(pick_out[...], ends).astype(BF)
        for i in range(8):
            at = slab_place(g * 8 + i)
            for r in range(2):
                for c in range(7):
                    t_buf[(2 * c + r,) + at] = block[32 * i + 16 * r:32 * i + 16 * r + 16,
                                                     128 * c:128 * c + 128]
            for r in range(3):
                t_buf[(14 + r,) + at] = ends[48 * i + 16 * r:48 * i + 16 * r + 16]

    rs(DOWN, 5)
    out_swap.wait()
    for s in range(2):
        at = pl.ds(pl.multiple_of(core * 256 + 128 * s, 128), 128)
        out_ref[pl.ds(128 * s, 128), :] = (
            y1[at, :] + (ypart[at, :] + mrec[pl.ds(128 * s, 128), :])).astype(BF)

    gain_grads = gain.at[pl.ds(2, 2)]
    gain_grads[...] = jnp.zeros((2, 896), F32)

    @pl.loop(0, 4)
    def _(s):
        da_swap(s).wait()
        da = yrec[rows(s), :] + darec[rows(s), :]
        v = y1[rows(s), :]
        r = inv_root(v)

        @pl.when(s // 2 == core)
        def _():
            gain[3:4, :] += jnp.sum(da * v * r, axis=0, keepdims=True)

        w = da * gain[1:2, :]
        dy = (e_all[rows(s), :].astype(F32) + r * w
              - v * (r * r * r) * jnp.mean(w * v, axis=-1, keepdims=True))
        darec[rows(s), :] = dy
        f = dy.astype(BF)
        a2s[rows(s), 0:896] = f

    rs(FFN + 2, 4)
    w_o = w_out()
    a2st[0:512, 0:448] = dot_t(dot_t(a2s[:, 0:896], w_o).astype(BF), spread_o[core]).astype(BF)

    o_grad = dot(o_s[...].T, a2s[:, 0:896]).astype(BF)
    for i in range(7):
        part = o_grad[:, 128 * i:128 * i + 128].reshape((2,) * 5 + (16, 128))
        u_buf[OUT_UNITS[i], :, :, :, :, core] = part
        u_buf[OUT_UNITS[i], :, :, :, :, 1 - core] = jnp.zeros_like(part)
    rs(OUT, 5)
    rs_fold(FFN)
    rs_fold(FFN + 1)
    rs_small(0, 3)

    bias[...] = jnp.zeros((8, 640), F32)

    @pl.loop(0, 4)
    def _(s):
        tick(s, 2, (rs, (DOWN, 4)))
        tick(s, 3, (rs, (OUT, 4)), (rs_fold, (FFN + 2,)))
        q7, k, v, soft = attend(s)
        do7 = heads(a2st[rows(s), 0:448])
        dp = dot_t(do7, v)
        ds_ = (soft * (dp - jnp.sum(soft * dp, axis=-1, keepdims=True))).astype(BF)
        dq = unheads(dot(ds_, k)) * 0.125
        dk = dot(ds_.T, q7) * 0.125
        dv = dot(soft.astype(BF).T, do7)
        raw = jnp.concatenate([dq, dk, dv, jnp.zeros((128, 64), F32)], axis=1)
        scaled = raw * wide(sine, s)
        turned = jnp.where(first, pltpu.roll(scaled, 608, 1), -pltpu.roll(scaled, 32, 1))
        grad = jnp.where(turns, raw * wide(cosine, s) + turned, raw).astype(BF)
        qkv[rows(s), :] = grad
        bias[0:1, :] += jnp.sum(grad.astype(F32), axis=0, keepdims=True)

    rs_small(0, 2)
    w_qkv = jnp.concatenate([unit(QKV + i) for i in range(5)], axis=1)
    da2[...] = dot_t(qkv[...], w_qkv)
    rs_fold(DOWN)
    rs_fold(OUT)
    rs_small(1, 3)
    for h in range(2):
        unspread_rows(h)
    a_swap = to_sibling(yrec.at[other], arec, 13)
    a_swap.start()
    rs_small(0, 1)
    a2st[...] = a1s[...].T
    for i in range(4):
        part = dot(a2st[...], qkv[:, 128 * i:128 * i + 128])
        u_buf[QKV + i] = part.astype(BF).reshape((2,) * 6 + (16, 128))
    rs_small(1, 2)
    a_swap.wait()
    for s in range(2):
        at = pl.ds(pl.multiple_of(core * 256 + 128 * s, 128), 128)
        da = yrec[at, :] + arec[pl.ds(128 * s, 128), :]
        v = x_all[at, :].astype(F32)
        r = inv_root(v)
        gain[2:3, :] += jnp.sum(da * v * r, axis=0, keepdims=True)
        w = da * gain[0:1, :]
        gtok_ref[pl.ds(128 * s, 128), :] = (
            darec[at, :] + r * w
            - v * (r * r * r) * jnp.mean(w * v, axis=-1, keepdims=True)).astype(BF)
    rs_small(0, 0)
    top = dot(jnp.concatenate([gain[2:4, :], jnp.zeros((14, 896), F32)], axis=0).astype(BF),
              spread[...])
    spot = jnp.where(choose, jnp.broadcast_to(bias[0:1, :], (16, 640)), 0.0).astype(BF)
    hit = (lax.broadcasted_iota(jnp.int32, (1024, 640), 0) == brow[core, 0:1, :]).astype(BF)
    low = dot_t(spot, hit)
    small = jnp.concatenate(
        [jnp.zeros((64, 1024), F32), top, low, jnp.zeros((32, 1024), F32)], axis=0).T
    part = dot(a2st[...], qkv[:, 512:640]) + small
    u_buf[49] = part.astype(BF).reshape((2,) * 6 + (16, 128))
    rs_head(2)
    rs_small(1, 1)
    rs_small_end(0)
    rs_head(1)
    rs_small(1, 0)
    rs_head(0)
    rs_small_end(1)
    last_swap(0).start()
    rs_head_end()
    last_swap(1).start()
    rs_sent()
    for i in range(2):
        last_swap(i).wait()


def layer(*arrays):
    dma = pltpu.SemaphoreType.DMA
    vm = pltpu.VMEM
    return pl.pallas_call(
        layer_kernel,
        out_shape=(
            jax.ShapeDtypeStruct((256, 896), BF),
            jax.ShapeDtypeStruct((256, 896), BF),
            jax.ShapeDtypeStruct((UNITS + TALL, 16, 128), F32),
            jax.ShapeDtypeStruct((UNITS, 16, 128), BF),
        ),
        in_specs=[pl.BlockSpec(memory_space=vm)] * 10 + [pl.BlockSpec(memory_space=pl.ANY)] * 6
        + [pl.BlockSpec(memory_space=vm)] * 4,
        out_specs=[pl.BlockSpec(memory_space=vm)] * 4,
        scratch_shapes=[
            vm((UNITS,) + (2,) * 6 + (16, 128), BF), vm((TALL,) + (2,) * 6 + (16, 128), BF),
            vm((QKV,) + (2,) * 5 + (16, 128), BF), vm((TALL,) + (2,) * 5 + (16, 128), BF),
            vm((2432, 896), BF), vm((512, 896), BF), vm((512, 896), BF), vm((2, 8, 128), F32),
            vm((UNITS, 16, 128), BF), vm((512, 1024), BF), vm((512, 1024), BF),
            vm((1024, 512), BF), vm((512, 640), BF), vm((512, 512), BF),
            vm((512, 896), F32), vm((512, 896), F32), vm((512, 896), F32), vm((512, 1024), F32),
            vm((512, 896), F32), vm((256, 896), F32), vm((256, 896), F32), vm((512, 128), F32), vm((512, 128), F32),
            vm((8, 896), F32), vm((8, 640), F32), vm((UNITS, 16, 128), BF),
            vm((8, RAW), F32), vm((48, 128), F32), vm((UNITS, 16, 128), BF),
            vm((UNITS, 16, 128), BF), vm((8, 128), F32), vm((896, 1024), BF), vm((2, 448, 512), BF),
            vm((304, 304), BF), vm((304, 304), BF),
            vm((3, 5, 16, 128), BF), vm((3, 5) + (2,) * 2 + (16, 128), BF),
            vm((3, 5) + (2,) * 4 + (16, 128), BF),
            dma((4, 6, 2)), dma((4, 6, 3)), dma((4, 6, 3)), dma((5, 2, 6)), dma((5, 2, 6)),
            dma((5, 2, 6)), dma((3, 3, 3)), dma((3, 3, 3)), dma((3, 3, 3)),
            pltpu.SemaphoreType.REGULAR((7, 6)),
            dma((21,)), dma((21,)), dma((6,)),
        ],
        compiler_params=pltpu.CompilerParams(collective_id=0, has_side_effects=True,
                                             vmem_limit_bytes=60 * 2**20),
    )(*arrays)


def finish_kernel(own, sib, out, tok, out_ref, tok_ref, q_ref, k_ref, v_ref, o_ref, g_ref, u_ref,
                  d_ref, gain_ref, bias_ref):
    out_ref[...] = out[...]
    tok_ref[...] = tok[...]
    for c in range(7):
        for r in range(2):
            d_ref[16 * r:16 * r + 16, 128 * c:128 * c + 128] = own[UNITS + 2 * c + r]
    ends = jnp.concatenate([own[UNITS + 14 + r] for r in range(3)], axis=0)
    for c in range(7):
        d_ref[32:38, 128 * c:128 * c + 128] = ends[6 * c:6 * c + 6]
    core = lax.axis_index("dp") % 2
    for c in range(2):
        @pl.when(core == c)
        def _():
            def mine(u):
                return own[u, 8 * c:8 * c + 8, :]

            def theirs(u):
                return sib[u].astype(F32)[8 * c:8 * c + 8]

            def half(plane, u, h):
                return (mine if plane == c else theirs)(u)[:, 64 * h:64 * h + 64]

            def put(ref, count, where):
                for n in range(count):
                    (p0, u0, h0), (p1, u1, h1) = where(2 * n), where(2 * n + 1)
                    if (p0, u0, h0, h1) == (p1, u1, 0, 1):
                        v = (mine if p0 == c else theirs)(u0)
                    else:
                        v = jnp.concatenate([half(p0, u0, h0), half(p1, u1, h1)], axis=1)
                    ref[:, 128 * n:128 * n + 128] = v[0:7]

            def hidden(table):
                def where(h):
                    t = h // 38 * 19 + h % 19
                    return h // 19 % 2, table[t // 2], t % 2
                return where

            put(g_ref, 38, hidden(GATE_UNITS))
            put(u_ref, 38, hidden(UP_UNITS))
            put(q_ref, 7, lambda h: (h // 7, QKV + h % 7 // 2, h % 7 % 2))
            put(k_ref, 1, lambda h: (h, QKV + 3, 1))
            put(v_ref, 1, lambda h: (h, QKV + 4, 0))
            for j, u in enumerate(OUT_UNITS):
                o_ref[:, 128 * j:128 * j + 128] = (mine(u) + theirs(u))[0:7]
            small = mine(QKV + 4) + theirs(QKV + 4)
            gain_ref[...] = small.T[64:66, 0:7]
            bias_ref[...] = small[0:1, 80:89]


def finish(own, sib, out, tok):
    vm = pl.BlockSpec(memory_space=pltpu.VMEM)
    shapes = [((256, 896), BF), ((256, 896), BF), ((7, 896), F32), ((7, 128), F32),
              ((7, 128), F32), ((7, 896), F32), ((7, 4864), F32), ((7, 4864), F32),
              ((38, 896), F32), ((2, 7), F32), ((1, 9), F32)]
    return pl.pallas_call(
        finish_kernel,
        out_shape=tuple(jax.ShapeDtypeStruct(s, d) for s, d in shapes),
        in_specs=[vm] * 4, out_specs=[vm] * 11,
    )(own, sib, out, tok)


def constants():
    slots = np.zeros(128, np.int32)
    for n in range(128):
        dp, fs = n // 32, n % 32
        x, y, z, core = fs // 4 % 4, fs % 4, (dp // 2) * 2 + fs // 16, dp % 2
        slots[n] = ((GRAY[x] * 4 + GRAY[y]) * 4 + GRAY[z]) * 2 + core
    spread = np.zeros((896, 1024), np.float32)
    for d in range(896):
        spread[d, slots[d // 7] * 8 + d % 7] = 1.0
    spread_o = np.zeros((2, 448, 512), np.float32)
    for c in range(2):
        part = spread[448 * c:448 * c + 448].reshape(448, 16, 2, 32)
        spread_o[c] = part[:, :, c].reshape(448, 512)
    unpack = np.zeros((304, 304), np.float32)
    pick_in = np.zeros((336, 384), np.float32)
    for a in range(8):
        for r in range(38):
            unpack[32 * a + r if r < 32 else 256 + 6 * a + r - 32, 38 * a + r] = 1.0
        for r in range(6):
            for c in range(7):
                pick_in[48 * c + 6 * a + r, 48 * a + 6 * c + r] = 1.0
    brow = np.full((2, 8, 640), -1, np.int32)
    for c in range(2):
        for i in range(576):
            if i < 448:
                nat = 448 * c + i
            elif i < 512:
                nat = 896 + 64 * c + i - 448
            else:
                nat = 1024 + 64 * c + i - 512
            brow[c, 0, i] = slots[nat // 9] * 8
            brow[c, 1, i] = nat % 9
    freq = THETA ** (-2.0 * (np.arange(128) % 32) / 64.0)
    freq = np.concatenate([freq[None], np.zeros((7, 128))]).astype(np.float32)
    return (jnp.asarray(spread, BF), jnp.asarray(spread_o, BF), jnp.asarray(unpack.T, BF),
            jnp.asarray(unpack, BF), jnp.asarray(pick_in, BF), jnp.asarray(pick_in.T, BF),
            jnp.asarray(brow), jnp.asarray(freq))


def shards(tokens, segments, w_query, w_key, w_value, w_out, w_gate, w_up, w_down, gains, biases,
           cotangent):
    out, tok, own, sib = layer(
        w_query, w_key, w_value, w_out, w_gate, w_up, w_down, gains.T, biases.reshape(1, 9),
        segments.reshape(2, 128), tokens.reshape(256, 896), cotangent.reshape(256, 896),
        *constants())
    out, tok, *grads, gain, bias = finish(own, sib, out, tok)
    return (out.reshape(tokens.shape), tok.reshape(tokens.shape), *grads, gain.T,
            bias.reshape(9))


def solution(mesh):
    row = P(AXES, None)
    batch = P(None, AXES, None, None)
    return jax.shard_map(
        shards, mesh=mesh,
        in_specs=(batch, P(None, AXES, None)) + (row,) * 8 + (P(AXES), batch),
        out_specs=(batch, batch) + (row,) * 8 + (P(AXES),),
        check_vma=False,
    )
```

```python
import functools

import jax
import jax.numpy as jnp
import numpy as np
from jax import lax
from jax.experimental import pallas as pl
from jax.experimental.pallas import tpu as pltpu
from jax.sharding import PartitionSpec as P

EPSILON = 1e-06
THETA = 1000000.0
NEG_FILL = -1e30
MESH = pl.DeviceIdType.MESH
AXES = ("dp", "fsdp")
BF = jnp.bfloat16
F32 = jnp.float32
GRAY = (0, 1, 3, 2)

BULK = ((0, 8), (8, 8), (16, 7), (23, 8), (31, 7), (38, 7))
TALLS = ((0, 3), (3, 3), (6, 3), (9, 3), (12, 3), (15, 2))
WAVES = (
    ((7, 1), (14, 2), (22, 1), (30, 1), (37, 1), (44, 1)),
    TALLS,
    ((0, 3), (8, 2), (16, 2), (23, 3), (31, 2), (38, 2)),
    ((3, 2), (10, 2), (18, 2), (26, 2), (33, 2), (40, 2)),
    ((5, 2), (12, 2), (20, 2), (28, 2), (35, 2), (42, 2)),
)
EARLY = ((0, 5), (8, 4), (16, 4), (23, 5), (31, 4), (38, 4))
LATE = ((5, 3), (12, 4), (20, 3), (28, 3), (35, 3), (42, 3))
OUT, DOWN, FFN = 0, 1, 2
OUT_UNITS = (7, 14, 15, 22, 30, 37, 44)
HEAD = ((45, 2), (47, 2), (49, 1))
UNITS, TALL, QKV = 50, 17, 45


def pair_units(starts, last):
    return tuple(starts[j % 6 // 2] + 2 * (j // 6) + j % 2 + (j > 5 and j % 6 < 2)
                 for j in range(18)) + (last,)


GATE_UNITS = pair_units((0, 8, 16), 2)
UP_UNITS = pair_units((23, 31, 38), 25)
GATE_AT, UP_AT, Q_AT, K_AT, V_AT, O_AT, S_AT, RAW = (
    0, 4864, 9728, 10624, 10752, 10880, 11776, 11904)
ORDER = tuple(
    tuple(2 * ((p % 3 + k // 2) % 3) + ((k % 2) ^ (p // 3)) for k in range(6)) for p in range(6)
)


def here():
    dp = lax.axis_index("dp")
    fs = lax.axis_index("fsdp")
    return (fs // 4) % 4, fs % 4, (dp // 2) * 2 + fs // 16, dp % 2


def device(x, y, z, core):
    return ((z // 2) * 2 + core, (z % 2) * 16 + x * 4 + y)


def gray_bits(v):
    high = v // 2
    low = (v % 2 + high) % 2
    return low, high


def flip(v, bit):
    if bit == 0:
        return v + 1 - 2 * (v % 2)
    return 3 - v


def partner(bit):
    x, y, z, core = here()
    axis, low = bit // 2, bit % 2
    place = [x, y, z]
    place[axis] = flip(place[axis], low)
    return device(*place, core)


def sibling():
    x, y, z, core = here()
    return device(x, y, z, 1 - core)


def my_bits():
    x, y, z, _ = here()
    bits = []
    for v in (x, y, z):
        low, high = gray_bits(v)
        bits += [low, high]
    return bits


DIMS = (1, 0, 3, 2, 5, 4)


def slot(bits, full):
    return tuple(slice(None) if b in full else bits[b] for b in DIMS)


def far(axis):
    x, y, z, core = here()
    place = [x, y, z]
    place[axis] = 3 - flip(place[axis], 0)
    return device(*place, core)


def dot(a, b):
    return lax.dot_general(a, b, (((1,), (0,)), ((), ())), preferred_element_type=F32)


def dot_t(a, b):
    return lax.dot_general(a, b, (((1,), (1,)), ((), ())), preferred_element_type=F32)


def layer_kernel(
    w_query, w_key, w_value, w_out_, w_gate, w_up, w_down, gains, biases, segments,
    x_own, e_own, spread_h, spread_o_h, pack_h, unpack_h, pick_in, pick_out, brow, freq,
    out_ref, gtok_ref, own_ref, sib_ref,
    u_buf, t_buf, u_got, t_got, wd, x_all, e_all, seg_all, stage, a1s, a2s, a2st, qkv, o_s,
    y1, ypart, yrec, da2, darec, mrec, arec, cosine, sine, gain, bias, slab,
    raw, last_rows, own_s, send_s, seg_own, spread, spread_o, pack, unpack,
    h_got0, h_got1, h_got2, ag_small_recv, rs_small_recv, small_send, ag_big_recv, rs_big_recv,
    big_send, ag_head_recv, rs_head_recv, head_send, credit, sib_send, sib_recv, loc_sem,
):
    _, _, _, core = here()
    bits = my_bits()
    flipped = [1 - b for b in bits]
    sib = sibling()
    peers = [partner(b) for b in range(6)]
    across_ = [far(a) for a in range(3)]

    barrier = pltpu.get_barrier_semaphore()
    for d in peers + across_ + [sib]:
        pl.semaphore_signal(barrier, inc=1, device_id=d, device_id_type=MESH)

    def to_sibling(src, dst, i):
        return pltpu.make_async_remote_copy(
            src_ref=src, dst_ref=dst, send_sem=sib_send.at[i], recv_sem=sib_recv.at[i],
            device_id=sib, device_id_type=MESH)

    own = pl.ds(pl.multiple_of(core * 256, 256), 256)
    locals_ = [
        pltpu.make_async_copy(a, b, loc_sem.at[i]) for i, (a, b) in enumerate((
            (x_own, x_all.at[own]), (e_own, e_all.at[own]), (spread_h, spread),
            (spread_o_h, spread_o), (pack_h, pack), (unpack_h, unpack)))]
    for c in locals_:
        c.start()

    raw[...] = jnp.zeros((8, RAW), F32)
    for ref, a in ((w_gate, GATE_AT), (w_up, UP_AT), (w_query, Q_AT), (w_key, K_AT),
                   (w_value, V_AT), (w_out_, O_AT)):
        raw[0:7, a:a + ref.shape[1]] = ref[...].astype(F32)
    last_rows[0:8, :] = jnp.zeros((8, 128), F32)
    last_rows[0:2, 0:7] = gains[...].astype(F32)
    raw[0:7, S_AT:S_AT + 2] = last_rows[0:8, :].T[0:7, 0:2]
    raw[0:1, S_AT + 16:S_AT + 25] = biases[...].astype(F32)
    seg_own[...] = jnp.zeros((8, 128), F32)
    seg_own[0:2, :] = segments[...].astype(F32)
    last_rows[...] = jnp.zeros((48, 128), F32)
    ends = w_down[32:38, :].astype(F32)
    for c in range(7):
        last_rows[6 * c:6 * c + 6, :] = ends[:, 128 * c:128 * c + 128]

    def lanes(first, second):
        if second == first + 64:
            return raw[:, first:first + 128]
        return jnp.concatenate([raw[:, first:first + 64], raw[:, second:second + 64]], axis=1)

    def hidden_at(base, c, h):
        return base + 1216 * (2 * (h // 19) + c) + 64 * (h % 19)

    def head_at(c, h):
        return (Q_AT + 448 * c + 64 * h, K_AT + 64 * c, V_AT + 64 * c, S_AT)[max(0, h - 6)]

    def units_of(c):
        for table, base in ((GATE_UNITS, GATE_AT), (UP_UNITS, UP_AT)):
            for j, place in enumerate(table):
                yield place, lanes(hidden_at(base, c, 2 * j), hidden_at(base, c, 2 * j + 1))
        for j in range(5):
            yield QKV + j, lanes(head_at(c, 2 * j), head_at(c, 2 * j + 1))
        for j, place in enumerate(OUT_UNITS):
            yield place, raw[:, O_AT + 128 * j:O_AT + 128 * j + 128]

    def fill(dst, other):
        for c in range(2):
            @pl.when(core == c)
            def _():
                zero = jnp.zeros((8, 128), F32)
                for place, v in units_of(1 - c if other else c):
                    tile = jnp.concatenate([zero, v] if c else [v, zero], axis=0)
                    dst[place] = tile.astype(BF)

    def remote(src, dst, send, recv, to):
        return pltpu.make_async_remote_copy(
            src_ref=src, dst_ref=dst, send_sem=send, recv_sem=recv, device_id=to,
            device_id_type=MESH)

    BOTH = ((u_buf, BULK), (t_buf, TALLS))

    def bufs(w):
        return (t_buf, t_got) if w == DOWN else (u_buf, u_got)

    def sent(buf, parts, k, sem):
        count = sum(n for _, n in parts)
        ref = buf.at[(pl.ds(0, count),) + slot(bits, ORDER[0][:k])]
        remote(ref, ref, sem, sem, peers[0]).wait_send()

    def small_copy(k, p, i):
        buf, parts = BOTH[i]
        ref = buf.at[(pl.ds(*parts[p]),) + slot(bits, ORDER[p][:k])]
        return remote(ref, ref, small_send.at[k, 2 * i], ag_small_recv.at[k, p, i],
                      peers[ORDER[p][k]])

    def ag_small(k, i):
        for p in range(6):
            if k > 0:
                small_copy(k - 1, p, i).wait_recv()
            small_copy(k, p, i).start()

    def ag_small_end(i):
        for p in range(6):
            small_copy(3, p, i).wait_recv()

    def ag_small_sent():
        for i in range(2):
            buf, parts = BOTH[i]
            for k in range(4):
                sent(buf, parts, k, small_send.at[k, 2 * i])

    is_mine = bits[5] == core

    def when(test, f):
        if test is None:
            f()
        else:
            pl.when(test)(f)

    def open_bit(w, k, p):
        return ORDER[p].index(5) - k if w == OUT else None

    def ag_tests(w, k, p):
        at = open_bit(w, k, p)
        if at is None or at < 0:
            return None, None
        return is_mine, (jnp.logical_not(is_mine) if at == 0 else is_mine)

    def rs_tests(w, k, p):
        send, take = ag_tests(w, k, p)
        return take, send

    def cut(w, k, p, b, full):
        if w == OUT and open_bit(w, k, p) < 0:
            b, full = list(b), [i for i in full if i != 5]
            b[5] = core
        return slot(b, full)

    def ag_copy(w, k, p):
        order = ORDER[p]
        ref = bufs(w)[0].at[(pl.ds(*WAVES[w][p]),) + cut(w, k, p, bits, order[:k])]
        return remote(ref, ref, big_send.at[w, k - 4, p], ag_big_recv.at[w, k - 4, p],
                      peers[order[k]])

    def ag(w, k):
        for p in range(6):
            if k == 5:
                when(ag_tests(w, 4, p)[1], ag_copy(w, 4, p).wait_recv)
            when(ag_tests(w, k, p)[0], ag_copy(w, k, p).start)

    def ag_done(w):
        for p in range(6):
            when(ag_tests(w, 5, p)[1], ag_copy(w, 5, p).wait_recv)
        for p in range(6):
            for k in (4, 5):
                when(ag_tests(w, k, p)[0], ag_copy(w, k, p).wait_send)

    def given(k, p, *more):
        b = list(bits)
        for j in (k,) + more:
            b[ORDER[p][j]] = flipped[ORDER[p][j]]
        return slot(b, ORDER[p][:k])

    def flipped_at(p, *steps):
        b = list(bits)
        for j in steps:
            b[ORDER[p][j]] = flipped[ORDER[p][j]]
        return b

    def got_at(w, p):
        if w == OUT and ORDER[p][5] != 5:
            return tuple(core if b == 5 else slice(None) for b in DIMS if b != ORDER[p][5])
        return ()

    def rs_copy(w, k, p):
        acc, got = bufs(w)
        units = pl.ds(*WAVES[w][p])
        full = ORDER[p][:k]
        src = acc.at[(units,) + cut(w, k, p, flipped_at(p, k), full)]
        if k == 5:
            dst = got.at[(units,) + got_at(w, p)]
        else:
            dst = acc.at[(units,) + cut(w, k, p, flipped_at(p, 5), full)]
        return remote(src, dst, big_send.at[w, k - 4, p], rs_big_recv.at[w, k - 4, p],
                      peers[ORDER[p][k]])

    def rs_add(acc, got, part, k, p, w=None):
        start, n = part
        full = ORDER[p][:k]
        mine_ = cut(w, k, p, bits, full)
        there = cut(w, k, p, flipped_at(p, 5, k), full)

        def one(u):
            add = got[(u,) + got_at(w, p)] if k == 5 else acc[(u,) + there]
            acc[(u,) + mine_] = acc[(u,) + mine_] + add

        if k >= 2:
            @pl.loop(0, n)
            def _(i):
                one(start + i)
        else:
            for i in range(n):
                one(start + i)

    def rs_take(w, k, p):
        acc, got = bufs(w)

        def take():
            rs_copy(w, k, p).wait_recv()
            rs_add(acc, got, WAVES[w][p], k, p, w)

        when(rs_tests(w, k, p)[1], take)

    def rs(w, k):
        if k == 4:
            for p in range(6):
                when(rs_tests(w, 5, p)[0], rs_copy(w, 5, p).wait_send)
            for b in range(6):
                pl.semaphore_signal(credit.at[w, b], inc=1, device_id=peers[b],
                                    device_id_type=MESH)
        for p in range(6):
            if k == 4:
                rs_take(w, 5, p)
                pl.semaphore_wait(credit.at[w, ORDER[p][4]], 1)
            when(rs_tests(w, k, p)[0], rs_copy(w, k, p).start)

    def rs_fold(w):
        for p in range(6):
            rs_take(w, 4, p)

    GROUPS = (((u_buf, EARLY),), ((u_buf, LATE), (t_buf, TALLS)))

    def rs_small_copy(g, k, p, i):
        buf, parts = GROUPS[g][i]
        units = pl.ds(*parts[p])
        b = list(bits)
        b[ORDER[p][5]] = flipped[ORDER[p][5]]
        return remote(buf.at[(units,) + given(k, p)], buf.at[(units,) + slot(b, ORDER[p][:k])],
                      small_send.at[k, g + i], rs_small_recv.at[k, p, g + i],
                      peers[ORDER[p][k]])

    def rs_small(g, k):
        if k == 3:
            for b in range(6):
                pl.semaphore_signal(credit.at[5 + g, b], inc=1, device_id=peers[b],
                                    device_id_type=MESH)
        for i in range(len(GROUPS[g])):
            for p in range(6):
                if k == 3:
                    if i == 0:
                        pl.semaphore_wait(credit.at[5 + g, ORDER[p][3]], 1)
                else:
                    rs_small_copy(g, k + 1, p, i).wait_recv()
                    rs_add(GROUPS[g][i][0], None, GROUPS[g][i][1][p], k + 1, p)
                rs_small_copy(g, k, p, i).start()

    def rs_small_end(g):
        for i, (buf, parts) in enumerate(GROUPS[g]):
            for p in range(6):
                start, n = parts[p]
                units = pl.ds(start, n)
                rs_small_copy(g, 0, p, i).wait_recv()
                total = (buf[(units,) + slot(bits, ())].astype(F32)
                         + buf[(units,) + given(0, p, 5)].astype(F32))
                own_ref[pl.ds(start + i * UNITS, n)] = total
                if i == 0:
                    slab[units] = total.astype(BF)

    def rs_sent():
        for p in range(6):
            for w in range(5):
                when(rs_tests(w, 4, p)[0], rs_copy(w, 4, p).wait_send)
        for g, i in ((0, 0), (1, 0), (1, 1)):
            for k in range(4):
                sent(*GROUPS[g][i], k, small_send.at[k, g + i])

    def turned_bits(axis, j):
        b = list(bits)
        for i in ((0,), (1,), (0, 1))[j]:
            b[2 * axis + i] = flipped[2 * axis + i]
        return b

    def head_to(axis, j):
        return across_[axis] if j == 2 else peers[2 * axis + j]

    def head_full(r, stage):
        return [2 * ((r + i) % 3) + j for i in range(stage) for j in range(2)]

    def head_copy(stage, r, j):
        ref = u_buf.at[(pl.ds(*HEAD[r]),) + slot(bits, head_full(r, stage))]
        return remote(ref, ref, head_send.at[stage], ag_head_recv.at[stage, r, j],
                      head_to((r + stage) % 3, j))

    def head_sent():
        for stage in range(3):
            ref = u_buf.at[(pl.ds(0, 15),) + slot(bits, head_full(0, stage))]
            remote(ref, ref, head_send.at[stage], head_send.at[stage], peers[0]).wait_send()

    def ag_head(stage):
        for r in range(3):
            for j in range(3):
                if stage > 0:
                    head_copy(stage - 1, r, j).wait_recv()
            for j in range(3):
                head_copy(stage, r, j).start()

    def ag_head_done():
        for r in range(3):
            for j in range(3):
                head_copy(2, r, j).wait_recv()
        head_sent()

    def head_rs_copy(stage, r, j):
        start, n = HEAD[r]
        axis = (r + stage) % 3
        src = u_buf.at[(pl.ds(start, n),) + slot(turned_bits(axis, j), head_full(r, stage))]
        dst = (h_got0, h_got1, h_got2)[stage].at[j, pl.ds(start - QKV, n)]
        return remote(src, dst, head_send.at[stage], rs_head_recv.at[stage, r, j],
                      head_to(axis, j))

    def head_sum(stage, r):
        start, n = HEAD[r]
        for j in range(3):
            head_rs_copy(stage, r, j).wait_recv()
        got = (h_got0, h_got1, h_got2)[stage]
        totals = []
        for i in range(n):
            at = (start + i,) + slot(bits, head_full(r, stage))
            total = u_buf[at].astype(F32)
            for j in range(3):
                total = total + got[j, start + i - QKV].astype(F32)
            if stage:
                u_buf[at] = total.astype(BF)
            else:
                own_ref[start + i] = total
                slab[start + i] = total.astype(BF)

    def rs_head(stage):
        for r in range(3):
            if stage < 2:
                head_sum(stage + 1, r)
            for j in range(3):
                head_rs_copy(stage, r, j).start()

    def rs_head_end():
        for r in range(3):
            head_sum(0, r)
        head_sent()

    def last_swap(i):
        at = pl.ds(0, QKV) if i == 0 else pl.ds(QKV, UNITS - QKV)
        return to_sibling(slab.at[at], sib_ref.at[at], 16 + i)

    mine = slot(bits, ())
    for c in range(7):
        cols = slice(128 * c, 128 * c + 128)
        for r in range(2):
            t_buf[(2 * c + r,) + mine] = w_down[16 * r:16 * r + 16, cols]
    for r in range(3):
        t_buf[(14 + r,) + mine] = last_rows[16 * r:16 * r + 16, :].astype(BF)
    fill(send_s, True)
    pl.semaphore_wait(barrier, 10)
    swap_pair = to_sibling(send_s, stage, 0)
    swap_pair.start()
    ag_small(0, 1)
    swap_seg = to_sibling(seg_own, seg_all.at[core], 1)
    swap_x = to_sibling(x_own, x_all.at[own], 2)
    swap_e = to_sibling(e_own, e_all.at[own], 3)
    for c in (swap_seg, swap_x, swap_e):
        c.start()
    fill(own_s, False)
    seg_all[core] = seg_own[...]

    def rows(s):
        return pl.ds(pl.multiple_of(s * 128, 128), 128)

    def unit(u):
        return u_buf[u].reshape(1024, 128)

    swap_pair.wait()
    u_buf[(slice(None),) + mine] = own_s[...] + stage[...]
    ag_head(0)
    ag_small(0, 0)
    ag_small(1, 1)
    ag_head(1)
    ag_small(1, 0)
    ag_small(2, 1)
    ag_head(2)
    for c in locals_:
        c.wait()
    for c in (swap_seg, swap_x, swap_e):
        c.wait()
    ag_small(3, 1)
    ag_small(2, 0)

    causal = (lax.broadcasted_iota(jnp.int32, (128, 128), 1)
              <= lax.broadcasted_iota(jnp.int32, (128, 128), 0))

    def allowed(s):
        line = seg_all[s // 2, pl.ds(s % 2, 1), :]
        across = jnp.broadcast_to(line, (128, 128))
        return jnp.logical_and(causal, across == across.T)

    for s in range(4):
        place = jnp.sum(allowed(s).astype(F32), axis=1, keepdims=True) - 1.0
        angle = place * freq[0:1, :]
        cosine[rows(s), :] = jnp.cos(angle)
        sine[rows(s), :] = jnp.sin(angle)
    ag_small_end(1)
    ag(DOWN, 4)
    ag_small(3, 0)
    ag_head_done()

    small = unit(49).T
    gain[...] = dot_t(small[64:80], spread[...])[0:8]
    hit = (lax.broadcasted_iota(jnp.int32, (1024, 640), 0) == brow[core, 0:1, :]).astype(BF)
    picked = dot(small[80:96], hit)
    choose = lax.broadcasted_iota(jnp.int32, (16, 640), 0) == brow[core, 1:2, :]
    bias[...] = jnp.broadcast_to(
        jnp.sum(jnp.where(choose, picked, 0.0), axis=0, keepdims=True), (8, 640))

    def inv_root(v):
        return lax.rsqrt(jnp.mean(v * v, axis=-1, keepdims=True) + EPSILON)

    @pl.loop(0, 4)
    def _(s):
        v = x_all[rows(s), :].astype(F32)
        a2s[rows(s), 0:896] = (v * inv_root(v) * gain[0:1, :]).astype(BF)

    def spread_rows(dst):
        for h in range(2):
            at = pl.ds(256 * h, 256)
            dst[at, :] = dot(a2s[at, 0:896], spread[...]).astype(BF)

    spread_rows(a1s)

    ag_small_end(0)
    ag(OUT, 4)
    ag(FFN, 4)
    lane = lax.broadcasted_iota(jnp.int32, (128, 640), 1)
    first = lane % 64 < 32
    turns = lane < 512

    def wide(ref, s):
        return jnp.concatenate([ref[rows(s), :]] * 5, axis=1)

    w_qkv = jnp.concatenate([unit(QKV + i) for i in range(5)], axis=1)
    da2[:, 0:640] = dot(a1s[...], w_qkv)
    for s in range(4):
        raw = da2[rows(s), 0:640] + bias[0:1, :]
        turned = jnp.where(first, -pltpu.roll(raw, 608, 1), pltpu.roll(raw, 32, 1))
        turned = raw * wide(cosine, s) + turned * wide(sine, s)
        qkv[rows(s), :] = jnp.where(turns, turned, raw).astype(BF)
    ag(OUT, 5)
    ag(DOWN, 5)

    def heads(v):
        return jnp.concatenate([v[:, 64 * h:64 * h + 64] for h in range(7)], axis=0)

    def unheads(v):
        return jnp.concatenate([v[128 * h:128 * h + 128, :] for h in range(7)], axis=1)

    def attend(s):
        q7 = heads(qkv[rows(s), 0:448])
        k = qkv[rows(s), 448:512]
        v = qkv[rows(s), 512:576]
        score = dot_t(q7, k) * 0.125
        ok = allowed(s)
        score = jnp.where(jnp.concatenate([ok] * 7, axis=0), score, NEG_FILL)
        e = jnp.exp(score - jnp.max(score, axis=-1, keepdims=True))
        soft = e / jnp.sum(e, axis=-1, keepdims=True)
        return q7, k, v, soft

    def w_out():
        return jnp.concatenate(
            [u_buf[OUT_UNITS[i], :, :, :, :, core].reshape(512, 128) for i in range(7)], axis=1)

    def y_swap(s):
        return to_sibling(ypart.at[rows(s)], yrec.at[rows(s)], 4 + s)

    def tick(now, t, *acts):
        @pl.when(now == t)
        def _():
            for f, a in acts:
                f(*a)

    @pl.loop(0, 4)
    def _(s):
        tick(s, 2, (ag, (FFN, 5)), (ag, (FFN + 1, 4)))
        _, _, v, soft = attend(s)
        a2s[rows(s), 0:448] = unheads(dot(soft.astype(BF), v)).astype(BF)

    ag_done(OUT)
    ag_small_sent()
    o_s[...] = dot(a2s[:, 0:448], spread_o[core]).astype(BF)
    for h in range(2):
        at = pl.ds(256 * h, 256)
        ypart[at, :] = dot(o_s[at, :], w_out())
        for s in (2 * h, 2 * h + 1):
            y_swap(s).start()

    ag_done(DOWN)

    def slab_place(s):
        z, x, y = s // 16, s // 4 % 4, s % 4
        b = []
        for v in (x, y, z):
            low, high = gray_bits(v)
            b += [low, high]
        return slot(b, ())

    @pl.loop(0, 8)
    def _(g):
        lines, ends = [], []
        for i in range(8):
            at = slab_place(g * 8 + i)
            for r in range(2):
                lines.append(jnp.concatenate(
                    [t_buf[(2 * c + r,) + at] for c in range(7)], axis=1))
            ends += [t_buf[(14 + r,) + at] for r in range(3)]
        ends = dot(pick_in[...], jnp.concatenate(ends, axis=0)).astype(BF)
        lines.append(jnp.concatenate([ends[48 * c:48 * c + 48] for c in range(7)], axis=1))
        block = jnp.concatenate(lines, axis=0)
        wd[pl.ds(pl.multiple_of(g * 304, 16), 304), :] = dot(pack[...], block).astype(BF)

    ag(FFN + 1, 5)
    ag(FFN + 2, 4)

    @pl.loop(0, 4)
    def _(s):
        y_swap(s).wait()
        v = x_all[rows(s), :].astype(F32) + (ypart[rows(s), :] + yrec[rows(s), :])
        y1[rows(s), :] = v
        a2s[rows(s), 0:896] = (v * inv_root(v) * gain[1:2, :]).astype(BF)
        ypart[rows(s), :] = jnp.zeros((128, 896), F32)
        da2[rows(s), :] = jnp.zeros((128, 1024), F32)

    spread_rows(a2s)
    a2st[...] = a2s[...].T

    def ffn(gates, ups, row, n):
        width = 128 * n
        w = jnp.concatenate([unit(i) for i in gates + ups], axis=1)
        both = dot(a2s[...], w)
        g, u = both[:, :width], both[:, width:]
        at = pl.ds(pl.multiple_of(row, 128), width)
        w_d = wd[at, :]
        dm = dot_t(e_all[...], w_d)
        sig = 1.0 / (1.0 + jnp.exp(-g))
        silu = g * sig
        m = (silu * u).astype(BF)
        dg = (dm * u * sig * (1.0 + g * (1.0 - sig))).astype(BF)
        du = (dm * silu).astype(BF)
        dgu = jnp.concatenate([dg, du], axis=1)
        ypart[...] += dot(m, w_d)
        da2[...] += dot_t(dgu, w)
        wd[at, :] = dot(m.T, e_all[...]).astype(BF)
        for part, places in ((dg, gates), (du, ups)):
            grads = dot(a2st[...], part).astype(BF)
            for i, place in enumerate(places):
                u_buf[place] = grads[:, 128 * i:128 * i + 128].reshape((2,) * 6 + (16, 128))

    ag_done(FFN)
    ffn([2], [25], 2304, 1)

    @pl.loop(0, 9)
    def _(i):
        tick(i, 2, (ag, (FFN + 2, 5)))
        tick(i, 3, (rs, (FFN, 5)), (ag_done, (FFN + 1,)))
        tick(i, 6, (rs, (FFN + 1, 5)), (ag_done, (FFN + 2,)))
        wave, q = i // 3, i % 3
        odd = (2 - q) // 2 * ((wave + 1) // 2)
        g = 8 * q + 2 * wave + odd
        u = 23 + 8 * q - q // 2 + 2 * wave + odd
        ffn([g, g + 1], [u, u + 1], i * 256, 2)

    rs(FFN, 4)
    rs(FFN + 2, 5)

    other = pl.ds(pl.multiple_of((1 - core) * 256, 256), 256)
    out_swap = to_sibling(ypart.at[other], mrec, 8)
    out_swap.start()

    def unspread(v):
        n = v.shape[0]
        high = v.astype(BF)
        low = (v - high.astype(F32)).astype(BF)
        both = dot_t(jnp.concatenate([high, low], axis=0), spread[...])
        return both[:n] + both[n:]

    def unspread_rows(h):
        at = pl.ds(256 * h, 256)
        yrec[at, :] = unspread(da2[at, :])

    def da_swap(s):
        return to_sibling(yrec.at[rows(s)], darec.at[rows(s)], 9 + s)

    for h in range(2):
        unspread_rows(h)
        for s in (2 * h, 2 * h + 1):
            da_swap(s).start()

    rs(FFN + 1, 4)

    @pl.loop(0, 8)
    def _(g):
        block = dot(unpack[...], wd[pl.ds(pl.multiple_of(g * 304, 16), 304), :]).astype(BF)
        ends = jnp.concatenate([block[256:304, 128 * c:128 * c + 128] for c in range(7)], axis=0)
        ends = dot(pick_out[...], ends).astype(BF)
        for i in range(8):
            at = slab_place(g * 8 + i)
            for r in range(2):
                for c in range(7):
                    t_buf[(2 * c + r,) + at] = block[32 * i + 16 * r:32 * i + 16 * r + 16,
                                                     128 * c:128 * c + 128]
            for r in range(3):
                t_buf[(14 + r,) + at] = ends[48 * i + 16 * r:48 * i + 16 * r + 16]

    rs(DOWN, 5)
    out_swap.wait()
    for s in range(2):
        at = pl.ds(pl.multiple_of(core * 256 + 128 * s, 128), 128)
        out_ref[pl.ds(128 * s, 128), :] = (
            y1[at, :] + (ypart[at, :] + mrec[pl.ds(128 * s, 128), :])).astype(BF)

    gain_grads = gain.at[pl.ds(2, 2)]
    gain_grads[...] = jnp.zeros((2, 896), F32)

    @pl.loop(0, 4)
    def _(s):
        da_swap(s).wait()
        da = yrec[rows(s), :] + darec[rows(s), :]
        v = y1[rows(s), :]
        r = inv_root(v)

        @pl.when(s // 2 == core)
        def _():
            gain[3:4, :] += jnp.sum(da * v * r, axis=0, keepdims=True)

        w = da * gain[1:2, :]
        dy = (e_all[rows(s), :].astype(F32) + r * w
              - v * (r * r * r) * jnp.mean(w * v, axis=-1, keepdims=True))
        darec[rows(s), :] = dy
        f = dy.astype(BF)
        a2s[rows(s), 0:896] = f

    rs(FFN + 2, 4)
    w_o = w_out()
    a2st[0:512, 0:448] = dot_t(dot_t(a2s[:, 0:896], w_o).astype(BF), spread_o[core]).astype(BF)

    o_grad = dot(o_s[...].T, a2s[:, 0:896]).astype(BF)
    for i in range(7):
        part = o_grad[:, 128 * i:128 * i + 128].reshape((2,) * 5 + (16, 128))
        u_buf[OUT_UNITS[i], :, :, :, :, core] = part
        u_buf[OUT_UNITS[i], :, :, :, :, 1 - core] = jnp.zeros_like(part)
    rs(OUT, 5)
    rs_fold(FFN)
    rs_fold(FFN + 1)
    rs_small(0, 3)

    bias[...] = jnp.zeros((8, 640), F32)

    @pl.loop(0, 4)
    def _(s):
        tick(s, 2, (rs, (DOWN, 4)))
        tick(s, 3, (rs, (OUT, 4)), (rs_fold, (FFN + 2,)))
        q7, k, v, soft = attend(s)
        do7 = heads(a2st[rows(s), 0:448])
        dp = dot_t(do7, v)
        ds_ = (soft * (dp - jnp.sum(soft * dp, axis=-1, keepdims=True))).astype(BF)
        dq = unheads(dot(ds_, k)) * 0.125
        dk = dot(ds_.T, q7) * 0.125
        dv = dot(soft.astype(BF).T, do7)
        raw = jnp.concatenate([dq, dk, dv, jnp.zeros((128, 64), F32)], axis=1)
        scaled = raw * wide(sine, s)
        turned = jnp.where(first, pltpu.roll(scaled, 608, 1), -pltpu.roll(scaled, 32, 1))
        grad = jnp.where(turns, raw * wide(cosine, s) + turned, raw).astype(BF)
        qkv[rows(s), :] = grad
        bias[0:1, :] += jnp.sum(grad.astype(F32), axis=0, keepdims=True)

    rs_small(0, 2)
    w_qkv = jnp.concatenate([unit(QKV + i) for i in range(5)], axis=1)
    da2[...] = dot_t(qkv[...], w_qkv)
    rs_fold(DOWN)
    rs_fold(OUT)
    rs_small(1, 3)
    for h in range(2):
        unspread_rows(h)
    a_swap = to_sibling(yrec.at[other], arec, 13)
    a_swap.start()
    rs_small(0, 1)
    a2st[...] = a1s[...].T
    for i in range(4):
        part = dot(a2st[...], qkv[:, 128 * i:128 * i + 128])
        u_buf[QKV + i] = part.astype(BF).reshape((2,) * 6 + (16, 128))
    rs_small(1, 2)
    a_swap.wait()
    for s in range(2):
        at = pl.ds(pl.multiple_of(core * 256 + 128 * s, 128), 128)
        da = yrec[at, :] + arec[pl.ds(128 * s, 128), :]
        v = x_all[at, :].astype(F32)
        r = inv_root(v)
        gain[2:3, :] += jnp.sum(da * v * r, axis=0, keepdims=True)
        w = da * gain[0:1, :]
        gtok_ref[pl.ds(128 * s, 128), :] = (
            darec[at, :] + r * w
            - v * (r * r * r) * jnp.mean(w * v, axis=-1, keepdims=True)).astype(BF)
    rs_small(0, 0)
    top = dot(jnp.concatenate([gain[2:4, :], jnp.zeros((14, 896), F32)], axis=0).astype(BF),
              spread[...])
    spot = jnp.where(choose, jnp.broadcast_to(bias[0:1, :], (16, 640)), 0.0).astype(BF)
    hit = (lax.broadcasted_iota(jnp.int32, (1024, 640), 0) == brow[core, 0:1, :]).astype(BF)
    low = dot_t(spot, hit)
    small = jnp.concatenate(
        [jnp.zeros((64, 1024), F32), top, low, jnp.zeros((32, 1024), F32)], axis=0).T
    part = dot(a2st[...], qkv[:, 512:640]) + small
    u_buf[49] = part.astype(BF).reshape((2,) * 6 + (16, 128))
    rs_head(2)
    rs_small(1, 1)
    rs_small_end(0)
    rs_head(1)
    rs_small(1, 0)
    rs_head(0)
    rs_small_end(1)
    last_swap(0).start()
    rs_head_end()
    last_swap(1).start()
    rs_sent()
    for i in range(2):
        last_swap(i).wait()


def layer(*arrays):
    dma = pltpu.SemaphoreType.DMA
    vm = pltpu.VMEM
    return pl.pallas_call(
        layer_kernel,
        out_shape=(
            jax.ShapeDtypeStruct((256, 896), BF),
            jax.ShapeDtypeStruct((256, 896), BF),
            jax.ShapeDtypeStruct((UNITS + TALL, 16, 128), F32),
            jax.ShapeDtypeStruct((UNITS, 16, 128), BF),
        ),
        in_specs=[pl.BlockSpec(memory_space=vm)] * 10 + [pl.BlockSpec(memory_space=pl.ANY)] * 6
        + [pl.BlockSpec(memory_space=vm)] * 4,
        out_specs=[pl.BlockSpec(memory_space=vm)] * 4,
        scratch_shapes=[
            vm((UNITS,) + (2,) * 6 + (16, 128), BF), vm((TALL,) + (2,) * 6 + (16, 128), BF),
            vm((QKV,) + (2,) * 5 + (16, 128), BF), vm((TALL,) + (2,) * 5 + (16, 128), BF),
            vm((2432, 896), BF), vm((512, 896), BF), vm((512, 896), BF), vm((2, 8, 128), F32),
            vm((UNITS, 16, 128), BF), vm((512, 1024), BF), vm((512, 1024), BF),
            vm((1024, 512), BF), vm((512, 640), BF), vm((512, 512), BF),
            vm((512, 896), F32), vm((512, 896), F32), vm((512, 896), F32), vm((512, 1024), F32),
            vm((512, 896), F32), vm((256, 896), F32), vm((256, 896), F32), vm((512, 128), F32), vm((512, 128), F32),
            vm((8, 896), F32), vm((8, 640), F32), vm((UNITS, 16, 128), BF),
            vm((8, RAW), F32), vm((48, 128), F32), vm((UNITS, 16, 128), BF),
            vm((UNITS, 16, 128), BF), vm((8, 128), F32), vm((896, 1024), BF), vm((2, 448, 512), BF),
            vm((304, 304), BF), vm((304, 304), BF),
            vm((3, 5, 16, 128), BF), vm((3, 5) + (2,) * 2 + (16, 128), BF),
            vm((3, 5) + (2,) * 4 + (16, 128), BF),
            dma((4, 6, 2)), dma((4, 6, 3)), dma((4, 3)), dma((5, 2, 6)), dma((5, 2, 6)),
            dma((5, 2, 6)), dma((3, 3, 3)), dma((3, 3, 3)), dma((3,)),
            pltpu.SemaphoreType.REGULAR((7, 6)),
            dma((21,)), dma((21,)), dma((6,)),
        ],
        compiler_params=pltpu.CompilerParams(collective_id=0, has_side_effects=True,
                                             vmem_limit_bytes=60 * 2**20),
    )(*arrays)


def finish_kernel(own, sib, out, tok, out_ref, tok_ref, q_ref, k_ref, v_ref, o_ref, g_ref, u_ref,
                  d_ref, gain_ref, bias_ref):
    out_ref[...] = out[...]
    tok_ref[...] = tok[...]
    for c in range(7):
        for r in range(2):
            d_ref[16 * r:16 * r + 16, 128 * c:128 * c + 128] = own[UNITS + 2 * c + r]
    ends = jnp.concatenate([own[UNITS + 14 + r] for r in range(3)], axis=0)
    for c in range(7):
        d_ref[32:38, 128 * c:128 * c + 128] = ends[6 * c:6 * c + 6]
    core = lax.axis_index("dp") % 2
    for c in range(2):
        @pl.when(core == c)
        def _():
            def mine(u):
                return own[u, 8 * c:8 * c + 8, :]

            def theirs(u):
                return sib[u].astype(F32)[8 * c:8 * c + 8]

            def half(plane, u, h):
                return (mine if plane == c else theirs)(u)[:, 64 * h:64 * h + 64]

            def put(ref, count, where):
                for n in range(count):
                    (p0, u0, h0), (p1, u1, h1) = where(2 * n), where(2 * n + 1)
                    if (p0, u0, h0, h1) == (p1, u1, 0, 1):
                        v = (mine if p0 == c else theirs)(u0)
                    else:
                        v = jnp.concatenate([half(p0, u0, h0), half(p1, u1, h1)], axis=1)
                    ref[:, 128 * n:128 * n + 128] = v[0:7]

            def hidden(table):
                def where(h):
                    t = h // 38 * 19 + h % 19
                    return h // 19 % 2, table[t // 2], t % 2
                return where

            put(g_ref, 38, hidden(GATE_UNITS))
            put(u_ref, 38, hidden(UP_UNITS))
            put(q_ref, 7, lambda h: (h // 7, QKV + h % 7 // 2, h % 7 % 2))
            put(k_ref, 1, lambda h: (h, QKV + 3, 1))
            put(v_ref, 1, lambda h: (h, QKV + 4, 0))
            for j, u in enumerate(OUT_UNITS):
                o_ref[:, 128 * j:128 * j + 128] = (mine(u) + theirs(u))[0:7]
            small = mine(QKV + 4) + theirs(QKV + 4)
            gain_ref[...] = small.T[64:66, 0:7]
            bias_ref[...] = small[0:1, 80:89]


def finish(own, sib, out, tok):
    vm = pl.BlockSpec(memory_space=pltpu.VMEM)
    shapes = [((256, 896), BF), ((256, 896), BF), ((7, 896), F32), ((7, 128), F32),
              ((7, 128), F32), ((7, 896), F32), ((7, 4864), F32), ((7, 4864), F32),
              ((38, 896), F32), ((2, 7), F32), ((1, 9), F32)]
    return pl.pallas_call(
        finish_kernel,
        out_shape=tuple(jax.ShapeDtypeStruct(s, d) for s, d in shapes),
        in_specs=[vm] * 4, out_specs=[vm] * 11,
    )(own, sib, out, tok)


def constants():
    slots = np.zeros(128, np.int32)
    for n in range(128):
        dp, fs = n // 32, n % 32
        x, y, z, core = fs // 4 % 4, fs % 4, (dp // 2) * 2 + fs // 16, dp % 2
        slots[n] = ((GRAY[x] * 4 + GRAY[y]) * 4 + GRAY[z]) * 2 + core
    spread = np.zeros((896, 1024), np.float32)
    for d in range(896):
        spread[d, slots[d // 7] * 8 + d % 7] = 1.0
    spread_o = np.zeros((2, 448, 512), np.float32)
    for c in range(2):
        part = spread[448 * c:448 * c + 448].reshape(448, 16, 2, 32)
        spread_o[c] = part[:, :, c].reshape(448, 512)
    unpack = np.zeros((304, 304), np.float32)
    pick_in = np.zeros((336, 384), np.float32)
    for a in range(8):
        for r in range(38):
            unpack[32 * a + r if r < 32 else 256 + 6 * a + r - 32, 38 * a + r] = 1.0
        for r in range(6):
            for c in range(7):
                pick_in[48 * c + 6 * a + r, 48 * a + 6 * c + r] = 1.0
    brow = np.full((2, 8, 640), -1, np.int32)
    for c in range(2):
        for i in range(576):
            if i < 448:
                nat = 448 * c + i
            elif i < 512:
                nat = 896 + 64 * c + i - 448
            else:
                nat = 1024 + 64 * c + i - 512
            brow[c, 0, i] = slots[nat // 9] * 8
            brow[c, 1, i] = nat % 9
    freq = THETA ** (-2.0 * (np.arange(128) % 32) / 64.0)
    freq = np.concatenate([freq[None], np.zeros((7, 128))]).astype(np.float32)
    return (jnp.asarray(spread, BF), jnp.asarray(spread_o, BF), jnp.asarray(unpack.T, BF),
            jnp.asarray(unpack, BF), jnp.asarray(pick_in, BF), jnp.asarray(pick_in.T, BF),
            jnp.asarray(brow), jnp.asarray(freq))


def shards(tokens, segments, w_query, w_key, w_value, w_out, w_gate, w_up, w_down, gains, biases,
           cotangent):
    out, tok, own, sib = layer(
        w_query, w_key, w_value, w_out, w_gate, w_up, w_down, gains.T, biases.reshape(1, 9),
        segments.reshape(2, 128), tokens.reshape(256, 896), cotangent.reshape(256, 896),
        *constants())
    out, tok, *grads, gain, bias = finish(own, sib, out, tok)
    return (out.reshape(tokens.shape), tok.reshape(tokens.shape), *grads, gain.T,
            bias.reshape(9))


def solution(mesh):
    row = P(AXES, None)
    batch = P(None, AXES, None, None)
    return jax.shard_map(
        shards, mesh=mesh,
        in_specs=(batch, P(None, AXES, None)) + (row,) * 8 + (P(AXES), batch),
        out_specs=(batch, batch) + (row,) * 8 + (P(AXES),),
        check_vma=False,
    )
```

```python
import functools

import jax
import jax.numpy as jnp
import numpy as np
from jax import lax
from jax.experimental import pallas as pl
from jax.experimental.pallas import tpu as pltpu
from jax.sharding import PartitionSpec as P

EPSILON = 1e-06
THETA = 1000000.0
NEG_FILL = -1e30
MESH = pl.DeviceIdType.MESH
AXES = ("dp", "fsdp")
BF = jnp.bfloat16
F32 = jnp.float32
GRAY = (0, 1, 3, 2)

BULK = ((0, 8), (8, 8), (16, 7), (23, 8), (31, 7), (38, 7))
TALLS = ((0, 2), (2, 3), (5, 3), (8, 3), (11, 3), (14, 3))
WAVES = (
    ((7, 1), (14, 2), (22, 1), (30, 1), (37, 1), (44, 1)),
    TALLS,
    ((0, 3), (8, 2), (16, 2), (23, 3), (31, 2), (38, 2)),
    ((3, 2), (10, 2), (18, 2), (26, 2), (33, 2), (40, 2)),
    ((5, 2), (12, 2), (20, 2), (28, 2), (35, 2), (42, 2)),
)
EARLY = ((0, 5), (8, 4), (16, 4), (23, 5), (31, 4), (38, 4))
LATE = ((5, 3), (12, 4), (20, 3), (28, 3), (35, 3), (42, 3))
OUT, DOWN, FFN = 0, 1, 2
OUT_UNITS = (7, 14, 15, 22, 30, 37, 44)
HEAD = ((45, 2), (47, 2), (49, 1))
UNITS, TALL, QKV = 50, 17, 45


def pair_units(starts, last):
    return tuple(starts[j % 6 // 2] + 2 * (j // 6) + j % 2 + (j > 5 and j % 6 < 2)
                 for j in range(18)) + (last,)


GATE_UNITS = pair_units((0, 8, 16), 2)
UP_UNITS = pair_units((23, 31, 38), 25)
GATE_AT, UP_AT, Q_AT, K_AT, V_AT, O_AT, S_AT, RAW = (
    0, 4864, 9728, 10624, 10752, 10880, 11776, 11904)
ORDER = tuple(
    tuple(2 * ((p % 3 + k // 2) % 3) + ((k % 2) ^ (p // 3)) for k in range(6)) for p in range(6)
)


def here():
    dp = lax.axis_index("dp")
    fs = lax.axis_index("fsdp")
    return (fs // 4) % 4, fs % 4, (dp // 2) * 2 + fs // 16, dp % 2


def device(x, y, z, core):
    return ((z // 2) * 2 + core, (z % 2) * 16 + x * 4 + y)


def gray_bits(v):
    high = v // 2
    low = (v % 2 + high) % 2
    return low, high


def flip(v, bit):
    if bit == 0:
        return v + 1 - 2 * (v % 2)
    return 3 - v


def partner(bit):
    x, y, z, core = here()
    axis, low = bit // 2, bit % 2
    place = [x, y, z]
    place[axis] = flip(place[axis], low)
    return device(*place, core)


def sibling():
    x, y, z, core = here()
    return device(x, y, z, 1 - core)


def my_bits():
    x, y, z, _ = here()
    bits = []
    for v in (x, y, z):
        low, high = gray_bits(v)
        bits += [low, high]
    return bits


DIMS = (1, 0, 3, 2, 5, 4)


def slot(bits, full):
    return tuple(slice(None) if b in full else bits[b] for b in DIMS)


def far(axis):
    x, y, z, core = here()
    place = [x, y, z]
    place[axis] = 3 - flip(place[axis], 0)
    return device(*place, core)


def dot(a, b):
    return lax.dot_general(a, b, (((1,), (0,)), ((), ())), preferred_element_type=F32)


def dot_t(a, b):
    return lax.dot_general(a, b, (((1,), (1,)), ((), ())), preferred_element_type=F32)


def layer_kernel(
    w_query, w_key, w_value, w_out_, w_gate, w_up, w_down, gains, biases, segments,
    x_own, e_own, spread_h, spread_o_h, pack_h, unpack_h, pick_in, pick_out, brow, freq,
    out_ref, gtok_ref, own_ref, sib_ref,
    u_buf, t_buf, u_got, t_got, wd, x_all, e_all, seg_all, stage, a1s, a2s, a2st, qkv, o_s,
    y1, ypart, yrec, da2, darec, mrec, arec, cosine, sine, gain, bias, slab,
    raw, last_rows, own_s, send_s, seg_own, spread, spread_o, pack, unpack,
    h_got0, h_got1, h_got2, ag_small_recv, rs_small_recv, small_send, ag_big_recv, rs_big_recv,
    big_send, ag_head_recv, rs_head_recv, head_send, credit, sib_send, sib_recv, loc_sem,
):
    _, _, _, core = here()
    bits = my_bits()
    flipped = [1 - b for b in bits]
    sib = sibling()
    peers = [partner(b) for b in range(6)]
    across_ = [far(a) for a in range(3)]

    barrier = pltpu.get_barrier_semaphore()
    for d in peers + across_ + [sib]:
        pl.semaphore_signal(barrier, inc=1, device_id=d, device_id_type=MESH)

    def to_sibling(src, dst, i):
        return pltpu.make_async_remote_copy(
            src_ref=src, dst_ref=dst, send_sem=sib_send.at[i], recv_sem=sib_recv.at[i],
            device_id=sib, device_id_type=MESH)

    own = pl.ds(pl.multiple_of(core * 256, 256), 256)
    locals_ = [
        pltpu.make_async_copy(a, b, loc_sem.at[i]) for i, (a, b) in enumerate((
            (x_own, x_all.at[own]), (e_own, e_all.at[own]), (spread_h, spread),
            (spread_o_h, spread_o), (pack_h, pack), (unpack_h, unpack)))]
    for c in locals_:
        c.start()

    raw[...] = jnp.zeros((8, RAW), F32)
    for ref, a in ((w_gate, GATE_AT), (w_up, UP_AT), (w_query, Q_AT), (w_key, K_AT),
                   (w_value, V_AT), (w_out_, O_AT)):
        raw[0:7, a:a + ref.shape[1]] = ref[...].astype(F32)
    last_rows[0:8, :] = jnp.zeros((8, 128), F32)
    last_rows[0:2, 0:7] = gains[...].astype(F32)
    raw[0:7, S_AT:S_AT + 2] = last_rows[0:8, :].T[0:7, 0:2]
    raw[0:1, S_AT + 16:S_AT + 25] = biases[...].astype(F32)
    seg_own[...] = jnp.zeros((8, 128), F32)
    seg_own[0:2, :] = segments[...].astype(F32)
    last_rows[...] = jnp.zeros((48, 128), F32)
    ends = w_down[32:38, :].astype(F32)
    for c in range(7):
        last_rows[6 * c:6 * c + 6, :] = ends[:, 128 * c:128 * c + 128]

    def lanes(first, second):
        if second == first + 64:
            return raw[:, first:first + 128]
        return jnp.concatenate([raw[:, first:first + 64], raw[:, second:second + 64]], axis=1)

    def hidden_at(base, c, h):
        return base + 1216 * (2 * (h // 19) + c) + 64 * (h % 19)

    def head_at(c, h):
        return (Q_AT + 448 * c + 64 * h, K_AT + 64 * c, V_AT + 64 * c, S_AT)[max(0, h - 6)]

    def units_of(c):
        for table, base in ((GATE_UNITS, GATE_AT), (UP_UNITS, UP_AT)):
            for j, place in enumerate(table):
                yield place, lanes(hidden_at(base, c, 2 * j), hidden_at(base, c, 2 * j + 1))
        for j in range(5):
            yield QKV + j, lanes(head_at(c, 2 * j), head_at(c, 2 * j + 1))
        for j, place in enumerate(OUT_UNITS):
            yield place, raw[:, O_AT + 128 * j:O_AT + 128 * j + 128]

    def fill(dst, other):
        for c in range(2):
            @pl.when(core == c)
            def _():
                zero = jnp.zeros((8, 128), F32)
                for place, v in units_of(1 - c if other else c):
                    tile = jnp.concatenate([zero, v] if c else [v, zero], axis=0)
                    dst[place] = tile.astype(BF)

    def remote(src, dst, send, recv, to):
        return pltpu.make_async_remote_copy(
            src_ref=src, dst_ref=dst, send_sem=send, recv_sem=recv, device_id=to,
            device_id_type=MESH)

    BOTH = ((u_buf, BULK), (t_buf, TALLS))

    def bufs(w):
        return (t_buf, t_got) if w == DOWN else (u_buf, u_got)

    def sent(buf, parts, k, sem):
        count = sum(n for _, n in parts)
        ref = buf.at[(pl.ds(0, count),) + slot(bits, ORDER[0][:k])]
        remote(ref, ref, sem, sem, peers[0]).wait_send()

    def small_copy(k, p, i):
        buf, parts = BOTH[i]
        ref = buf.at[(pl.ds(*parts[p]),) + slot(bits, ORDER[p][:k])]
        return remote(ref, ref, small_send.at[k, 2 * i], ag_small_recv.at[k, p, i],
                      peers[ORDER[p][k]])

    def ag_small(k, i):
        for p in range(6):
            if k > 0:
                small_copy(k - 1, p, i).wait_recv()
            small_copy(k, p, i).start()

    def ag_small_end(i):
        for p in range(6):
            small_copy(3, p, i).wait_recv()

    def ag_small_sent():
        for i in range(2):
            buf, parts = BOTH[i]
            for k in range(4):
                sent(buf, parts, k, small_send.at[k, 2 * i])

    is_mine = bits[5] == core

    def when(test, f):
        if test is None:
            f()
        else:
            pl.when(test)(f)

    def open_bit(w, k, p):
        return ORDER[p].index(5) - k if w == OUT else None

    def ag_tests(w, k, p):
        at = open_bit(w, k, p)
        if at is None or at < 0:
            return None, None
        return is_mine, (jnp.logical_not(is_mine) if at == 0 else is_mine)

    def rs_tests(w, k, p):
        send, take = ag_tests(w, k, p)
        return take, send

    def cut(w, k, p, b, full):
        if w == OUT and open_bit(w, k, p) < 0:
            b, full = list(b), [i for i in full if i != 5]
            b[5] = core
        return slot(b, full)

    def ag_copy(w, k, p):
        order = ORDER[p]
        ref = bufs(w)[0].at[(pl.ds(*WAVES[w][p]),) + cut(w, k, p, bits, order[:k])]
        return remote(ref, ref, big_send.at[w, k - 4, p], ag_big_recv.at[w, k - 4, p],
                      peers[order[k]])

    def ag(w, k):
        for p in range(6):
            if k == 5:
                when(ag_tests(w, 4, p)[1], ag_copy(w, 4, p).wait_recv)
            when(ag_tests(w, k, p)[0], ag_copy(w, k, p).start)

    def ag_done(w):
        for p in range(6):
            when(ag_tests(w, 5, p)[1], ag_copy(w, 5, p).wait_recv)
        for p in range(6):
            for k in (4, 5):
                when(ag_tests(w, k, p)[0], ag_copy(w, k, p).wait_send)

    def given(k, p, *more):
        b = list(bits)
        for j in (k,) + more:
            b[ORDER[p][j]] = flipped[ORDER[p][j]]
        return slot(b, ORDER[p][:k])

    def flipped_at(p, *steps):
        b = list(bits)
        for j in steps:
            b[ORDER[p][j]] = flipped[ORDER[p][j]]
        return b

    def got_at(w, p):
        if w == OUT and ORDER[p][5] != 5:
            return tuple(core if b == 5 else slice(None) for b in DIMS if b != ORDER[p][5])
        return ()

    def rs_copy(w, k, p):
        acc, got = bufs(w)
        units = pl.ds(*WAVES[w][p])
        full = ORDER[p][:k]
        src = acc.at[(units,) + cut(w, k, p, flipped_at(p, k), full)]
        if k == 5:
            dst = got.at[(units,) + got_at(w, p)]
        else:
            dst = acc.at[(units,) + cut(w, k, p, flipped_at(p, 5), full)]
        return remote(src, dst, big_send.at[w, k - 4, p], rs_big_recv.at[w, k - 4, p],
                      peers[ORDER[p][k]])

    def rs_add(acc, got, part, k, p, w=None):
        start, n = part
        full = ORDER[p][:k]
        mine_ = cut(w, k, p, bits, full)
        there = cut(w, k, p, flipped_at(p, 5, k), full)

        def one(u):
            add = got[(u,) + got_at(w, p)] if k == 5 else acc[(u,) + there]
            acc[(u,) + mine_] = acc[(u,) + mine_] + add

        if k >= 2:
            @pl.loop(0, n)
            def _(i):
                one(start + i)
        else:
            for i in range(n):
                one(start + i)

    def rs_take(w, k, p):
        acc, got = bufs(w)

        def take():
            rs_copy(w, k, p).wait_recv()
            rs_add(acc, got, WAVES[w][p], k, p, w)

        when(rs_tests(w, k, p)[1], take)

    def rs(w, k):
        if k == 4:
            for p in range(6):
                when(rs_tests(w, 5, p)[0], rs_copy(w, 5, p).wait_send)
            for b in range(6):
                pl.semaphore_signal(credit.at[w, b], inc=1, device_id=peers[b],
                                    device_id_type=MESH)
        for p in range(6):
            if k == 4:
                rs_take(w, 5, p)
                pl.semaphore_wait(credit.at[w, ORDER[p][4]], 1)
            when(rs_tests(w, k, p)[0], rs_copy(w, k, p).start)

    def rs_fold(w):
        for p in range(6):
            rs_take(w, 4, p)

    GROUPS = (((u_buf, EARLY),), ((u_buf, LATE), (t_buf, TALLS)))

    def rs_small_copy(g, k, p, i):
        buf, parts = GROUPS[g][i]
        units = pl.ds(*parts[p])
        b = list(bits)
        b[ORDER[p][5]] = flipped[ORDER[p][5]]
        return remote(buf.at[(units,) + given(k, p)], buf.at[(units,) + slot(b, ORDER[p][:k])],
                      small_send.at[k, g + i], rs_small_recv.at[k, p, g + i],
                      peers[ORDER[p][k]])

    def rs_small(g, k):
        if k == 3:
            for b in range(6):
                pl.semaphore_signal(credit.at[5 + g, b], inc=1, device_id=peers[b],
                                    device_id_type=MESH)
        for i in range(len(GROUPS[g])):
            for p in range(6):
                if k == 3:
                    if i == 0:
                        pl.semaphore_wait(credit.at[5 + g, ORDER[p][3]], 1)
                else:
                    rs_small_copy(g, k + 1, p, i).wait_recv()
                    rs_add(GROUPS[g][i][0], None, GROUPS[g][i][1][p], k + 1, p)
                rs_small_copy(g, k, p, i).start()

    def rs_small_end(g):
        for i, (buf, parts) in enumerate(GROUPS[g]):
            for p in range(6):
                start, n = parts[p]
                units = pl.ds(start, n)
                rs_small_copy(g, 0, p, i).wait_recv()
                total = (buf[(units,) + slot(bits, ())].astype(F32)
                         + buf[(units,) + given(0, p, 5)].astype(F32))
                own_ref[pl.ds(start + i * UNITS, n)] = total
                if i == 0:
                    slab[units] = total.astype(BF)

    def rs_sent():
        for p in range(6):
            for w in range(5):
                when(rs_tests(w, 4, p)[0], rs_copy(w, 4, p).wait_send)
        for g, i in ((0, 0), (1, 0), (1, 1)):
            for k in range(4):
                sent(*GROUPS[g][i], k, small_send.at[k, g + i])

    def turned_bits(axis, j):
        b = list(bits)
        for i in ((0,), (1,), (0, 1))[j]:
            b[2 * axis + i] = flipped[2 * axis + i]
        return b

    def head_to(axis, j):
        return across_[axis] if j == 2 else peers[2 * axis + j]

    def head_full(r, stage):
        return [2 * ((r + i) % 3) + j for i in range(stage) for j in range(2)]

    def head_copy(stage, r, j):
        ref = u_buf.at[(pl.ds(*HEAD[r]),) + slot(bits, head_full(r, stage))]
        return remote(ref, ref, head_send.at[stage], ag_head_recv.at[stage, r, j],
                      head_to((r + stage) % 3, j))

    def head_sent():
        for stage in range(3):
            ref = u_buf.at[(pl.ds(0, 15),) + slot(bits, head_full(0, stage))]
            remote(ref, ref, head_send.at[stage], head_send.at[stage], peers[0]).wait_send()

    def ag_head(stage):
        for r in range(3):
            for j in range(3):
                if stage > 0:
                    head_copy(stage - 1, r, j).wait_recv()
            for j in range(3):
                head_copy(stage, r, j).start()

    def ag_head_done():
        for r in range(3):
            for j in range(3):
                head_copy(2, r, j).wait_recv()
        head_sent()

    def head_rs_copy(stage, r, j):
        start, n = HEAD[r]
        axis = (r + stage) % 3
        src = u_buf.at[(pl.ds(start, n),) + slot(turned_bits(axis, j), head_full(r, stage))]
        dst = (h_got0, h_got1, h_got2)[stage].at[j, pl.ds(start - QKV, n)]
        return remote(src, dst, head_send.at[stage], rs_head_recv.at[stage, r, j],
                      head_to(axis, j))

    def head_sum(stage, r):
        start, n = HEAD[r]
        for j in range(3):
            head_rs_copy(stage, r, j).wait_recv()
        got = (h_got0, h_got1, h_got2)[stage]
        totals = []
        for i in range(n):
            at = (start + i,) + slot(bits, head_full(r, stage))
            total = u_buf[at].astype(F32)
            for j in range(3):
                total = total + got[j, start + i - QKV].astype(F32)
            if stage:
                u_buf[at] = total.astype(BF)
            else:
                own_ref[start + i] = total
                slab[start + i] = total.astype(BF)

    def rs_head(stage):
        for r in range(3):
            if stage < 2:
                head_sum(stage + 1, r)
            for j in range(3):
                head_rs_copy(stage, r, j).start()

    def rs_head_end():
        for r in range(3):
            head_sum(0, r)
        head_sent()

    def last_swap(i):
        at = pl.ds(0, QKV) if i == 0 else pl.ds(QKV, UNITS - QKV)
        return to_sibling(slab.at[at], sib_ref.at[at], 16 + i)

    mine = slot(bits, ())
    for c in range(7):
        cols = slice(128 * c, 128 * c + 128)
        for r in range(2):
            t_buf[(2 * c + r,) + mine] = w_down[16 * r:16 * r + 16, cols]
    for r in range(3):
        t_buf[(14 + r,) + mine] = last_rows[16 * r:16 * r + 16, :].astype(BF)
    fill(send_s, True)
    pl.semaphore_wait(barrier, 10)
    swap_pair = to_sibling(send_s, stage, 0)
    swap_pair.start()
    ag_small(0, 1)
    swap_seg = to_sibling(seg_own, seg_all.at[core], 1)
    swap_x = to_sibling(x_own, x_all.at[own], 2)
    swap_e = to_sibling(e_own, e_all.at[own], 3)
    for c in (swap_seg, swap_x, swap_e):
        c.start()
    fill(own_s, False)
    seg_all[core] = seg_own[...]

    def rows(s):
        return pl.ds(pl.multiple_of(s * 128, 128), 128)

    def unit(u):
        return u_buf[u].reshape(1024, 128)

    swap_pair.wait()
    u_buf[(slice(None),) + mine] = own_s[...] + stage[...]
    ag_head(0)
    ag_small(0, 0)
    ag_small(1, 1)
    ag_head(1)
    ag_small(1, 0)
    ag_small(2, 1)
    ag_head(2)
    for c in locals_:
        c.wait()
    for c in (swap_seg, swap_x, swap_e):
        c.wait()
    ag_small(3, 1)
    ag_small(2, 0)

    causal = (lax.broadcasted_iota(jnp.int32, (128, 128), 1)
              <= lax.broadcasted_iota(jnp.int32, (128, 128), 0))

    def allowed(s):
        line = seg_all[s // 2, pl.ds(s % 2, 1), :]
        across = jnp.broadcast_to(line, (128, 128))
        return jnp.logical_and(causal, across == across.T)

    for s in range(4):
        place = jnp.sum(allowed(s).astype(F32), axis=1, keepdims=True) - 1.0
        angle = place * freq[0:1, :]
        cosine[rows(s), :] = jnp.cos(angle)
        sine[rows(s), :] = jnp.sin(angle)
    ag_small_end(1)
    ag(DOWN, 4)
    ag_small(3, 0)
    ag_head_done()

    small = unit(49).T
    gain[...] = dot_t(small[64:80], spread[...])[0:8]
    hit = (lax.broadcasted_iota(jnp.int32, (1024, 640), 0) == brow[core, 0:1, :]).astype(BF)
    picked = dot(small[80:96], hit)
    choose = lax.broadcasted_iota(jnp.int32, (16, 640), 0) == brow[core, 1:2, :]
    bias[...] = jnp.broadcast_to(
        jnp.sum(jnp.where(choose, picked, 0.0), axis=0, keepdims=True), (8, 640))

    def inv_root(v):
        return lax.rsqrt(jnp.mean(v * v, axis=-1, keepdims=True) + EPSILON)

    @pl.loop(0, 4)
    def _(s):
        v = x_all[rows(s), :].astype(F32)
        a2s[rows(s), 0:896] = (v * inv_root(v) * gain[0:1, :]).astype(BF)

    def spread_rows(dst):
        for h in range(2):
            at = pl.ds(256 * h, 256)
            dst[at, :] = dot(a2s[at, 0:896], spread[...]).astype(BF)

    spread_rows(a1s)

    ag_small_end(0)
    ag(OUT, 4)
    ag(FFN, 4)
    lane = lax.broadcasted_iota(jnp.int32, (128, 640), 1)
    first = lane % 64 < 32
    turns = lane < 512

    def wide(ref, s):
        return jnp.concatenate([ref[rows(s), :]] * 5, axis=1)

    w_qkv = jnp.concatenate([unit(QKV + i) for i in range(5)], axis=1)
    da2[:, 0:640] = dot(a1s[...], w_qkv)
    for s in range(4):
        raw = da2[rows(s), 0:640] + bias[0:1, :]
        turned = jnp.where(first, -pltpu.roll(raw, 608, 1), pltpu.roll(raw, 32, 1))
        turned = raw * wide(cosine, s) + turned * wide(sine, s)
        qkv[rows(s), :] = jnp.where(turns, turned, raw).astype(BF)
    ag(OUT, 5)
    ag(DOWN, 5)

    def heads(v):
        return jnp.concatenate([v[:, 64 * h:64 * h + 64] for h in range(7)], axis=0)

    def unheads(v):
        return jnp.concatenate([v[128 * h:128 * h + 128, :] for h in range(7)], axis=1)

    def attend(s):
        q7 = heads(qkv[rows(s), 0:448])
        k = qkv[rows(s), 448:512]
        v = qkv[rows(s), 512:576]
        score = dot_t(q7, k) * 0.125
        ok = allowed(s)
        score = jnp.where(jnp.concatenate([ok] * 7, axis=0), score, NEG_FILL)
        e = jnp.exp(score - jnp.max(score, axis=-1, keepdims=True))
        soft = e / jnp.sum(e, axis=-1, keepdims=True)
        return q7, k, v, soft

    def w_out():
        return jnp.concatenate(
            [u_buf[OUT_UNITS[i], :, :, :, :, core].reshape(512, 128) for i in range(7)], axis=1)

    def y_swap(s):
        return to_sibling(ypart.at[rows(s)], yrec.at[rows(s)], 4 + s)

    def tick(now, t, *acts):
        @pl.when(now == t)
        def _():
            for f, a in acts:
                f(*a)

    @pl.loop(0, 4)
    def _(s):
        tick(s, 2, (ag, (FFN, 5)), (ag, (FFN + 1, 4)))
        _, _, v, soft = attend(s)
        a2s[rows(s), 0:448] = unheads(dot(soft.astype(BF), v)).astype(BF)

    ag_done(OUT)
    ag_small_sent()
    o_s[...] = dot(a2s[:, 0:448], spread_o[core]).astype(BF)
    for h in range(2):
        at = pl.ds(256 * h, 256)
        ypart[at, :] = dot(o_s[at, :], w_out())
        for s in (2 * h, 2 * h + 1):
            y_swap(s).start()

    ag_done(DOWN)

    def slab_place(s):
        z, x, y = s // 16, s // 4 % 4, s % 4
        b = []
        for v in (x, y, z):
            low, high = gray_bits(v)
            b += [low, high]
        return slot(b, ())

    @pl.loop(0, 8)
    def _(g):
        lines, ends = [], []
        for i in range(8):
            at = slab_place(g * 8 + i)
            for r in range(2):
                lines.append(jnp.concatenate(
                    [t_buf[(2 * c + r,) + at] for c in range(7)], axis=1))
            ends += [t_buf[(14 + r,) + at] for r in range(3)]
        ends = dot(pick_in[...], jnp.concatenate(ends, axis=0)).astype(BF)
        lines.append(jnp.concatenate([ends[48 * c:48 * c + 48] for c in range(7)], axis=1))
        block = jnp.concatenate(lines, axis=0)
        wd[pl.ds(pl.multiple_of(g * 304, 16), 304), :] = dot(pack[...], block).astype(BF)

    ag(FFN + 1, 5)
    ag(FFN + 2, 4)

    @pl.loop(0, 4)
    def _(s):
        y_swap(s).wait()
        v = x_all[rows(s), :].astype(F32) + (ypart[rows(s), :] + yrec[rows(s), :])
        y1[rows(s), :] = v
        a2s[rows(s), 0:896] = (v * inv_root(v) * gain[1:2, :]).astype(BF)
        ypart[rows(s), :] = jnp.zeros((128, 896), F32)
        da2[rows(s), :] = jnp.zeros((128, 1024), F32)

    spread_rows(a2s)
    a2st[...] = a2s[...].T

    def ffn(gates, ups, row, n):
        width = 128 * n
        w = jnp.concatenate([unit(i) for i in gates + ups], axis=1)
        both = dot(a2s[...], w)
        g, u = both[:, :width], both[:, width:]
        at = pl.ds(pl.multiple_of(row, 128), width)
        w_d = wd[at, :]
        dm = dot_t(e_all[...], w_d)
        sig = 1.0 / (1.0 + jnp.exp(-g))
        silu = g * sig
        m = (silu * u).astype(BF)
        dg = (dm * u * sig * (1.0 + g * (1.0 - sig))).astype(BF)
        du = (dm * silu).astype(BF)
        dgu = jnp.concatenate([dg, du], axis=1)
        ypart[...] += dot(m, w_d)
        da2[...] += dot_t(dgu, w)
        wd[at, :] = dot(m.T, e_all[...]).astype(BF)
        for part, places in ((dg, gates), (du, ups)):
            grads = dot(a2st[...], part).astype(BF)
            for i, place in enumerate(places):
                u_buf[place] = grads[:, 128 * i:128 * i + 128].reshape((2,) * 6 + (16, 128))

    ag_done(FFN)
    ffn([2], [25], 2304, 1)

    @pl.loop(0, 9)
    def _(i):
        tick(i, 2, (ag, (FFN + 2, 5)))
        tick(i, 3, (rs, (FFN, 5)), (ag_done, (FFN + 1,)))
        tick(i, 6, (rs, (FFN + 1, 5)), (ag_done, (FFN + 2,)))
        wave, q = i // 3, i % 3
        odd = (2 - q) // 2 * ((wave + 1) // 2)
        g = 8 * q + 2 * wave + odd
        u = 23 + 8 * q - q // 2 + 2 * wave + odd
        ffn([g, g + 1], [u, u + 1], i * 256, 2)

    rs(FFN, 4)
    rs(FFN + 2, 5)

    other = pl.ds(pl.multiple_of((1 - core) * 256, 256), 256)
    out_swap = to_sibling(ypart.at[other], mrec, 8)
    out_swap.start()

    def unspread(v):
        n = v.shape[0]
        high = v.astype(BF)
        low = (v - high.astype(F32)).astype(BF)
        both = dot_t(jnp.concatenate([high, low], axis=0), spread[...])
        return both[:n] + both[n:]

    def unspread_rows(h):
        at = pl.ds(256 * h, 256)
        yrec[at, :] = unspread(da2[at, :])

    def da_swap(s):
        return to_sibling(yrec.at[rows(s)], darec.at[rows(s)], 9 + s)

    for h in range(2):
        unspread_rows(h)
        for s in (2 * h, 2 * h + 1):
            da_swap(s).start()

    rs(FFN + 1, 4)

    @pl.loop(0, 8)
    def _(g):
        block = dot(unpack[...], wd[pl.ds(pl.multiple_of(g * 304, 16), 304), :]).astype(BF)
        ends = jnp.concatenate([block[256:304, 128 * c:128 * c + 128] for c in range(7)], axis=0)
        ends = dot(pick_out[...], ends).astype(BF)
        for i in range(8):
            at = slab_place(g * 8 + i)
            for r in range(2):
                for c in range(7):
                    t_buf[(2 * c + r,) + at] = block[32 * i + 16 * r:32 * i + 16 * r + 16,
                                                     128 * c:128 * c + 128]
            for r in range(3):
                t_buf[(14 + r,) + at] = ends[48 * i + 16 * r:48 * i + 16 * r + 16]

    rs(DOWN, 5)
    out_swap.wait()
    for s in range(2):
        at = pl.ds(pl.multiple_of(core * 256 + 128 * s, 128), 128)
        out_ref[pl.ds(128 * s, 128), :] = (
            y1[at, :] + (ypart[at, :] + mrec[pl.ds(128 * s, 128), :])).astype(BF)

    gain_grads = gain.at[pl.ds(2, 2)]
    gain_grads[...] = jnp.zeros((2, 896), F32)

    @pl.loop(0, 4)
    def _(s):
        da_swap(s).wait()
        da = yrec[rows(s), :] + darec[rows(s), :]
        v = y1[rows(s), :]
        r = inv_root(v)

        @pl.when(s // 2 == core)
        def _():
            gain[3:4, :] += jnp.sum(da * v * r, axis=0, keepdims=True)

        w = da * gain[1:2, :]
        dy = (e_all[rows(s), :].astype(F32) + r * w
              - v * (r * r * r) * jnp.mean(w * v, axis=-1, keepdims=True))
        darec[rows(s), :] = dy
        f = dy.astype(BF)
        a2s[rows(s), 0:896] = f

    rs(FFN + 2, 4)
    w_o = w_out()
    a2st[0:512, 0:448] = dot_t(dot_t(a2s[:, 0:896], w_o).astype(BF), spread_o[core]).astype(BF)

    o_grad = dot(o_s[...].T, a2s[:, 0:896]).astype(BF)
    for i in range(7):
        part = o_grad[:, 128 * i:128 * i + 128].reshape((2,) * 5 + (16, 128))
        u_buf[OUT_UNITS[i], :, :, :, :, core] = part
        u_buf[OUT_UNITS[i], :, :, :, :, 1 - core] = jnp.zeros_like(part)
    rs(OUT, 5)
    rs_fold(FFN)
    rs_fold(FFN + 1)
    rs_small(0, 3)

    bias[...] = jnp.zeros((8, 640), F32)

    @pl.loop(0, 4)
    def _(s):
        tick(s, 2, (rs, (DOWN, 4)))
        tick(s, 3, (rs, (OUT, 4)), (rs_fold, (FFN + 2,)))
        q7, k, v, soft = attend(s)
        do7 = heads(a2st[rows(s), 0:448])
        dp = dot_t(do7, v)
        ds_ = (soft * (dp - jnp.sum(soft * dp, axis=-1, keepdims=True))).astype(BF)
        dq = unheads(dot(ds_, k)) * 0.125
        dk = dot(ds_.T, q7) * 0.125
        dv = dot(soft.astype(BF).T, do7)
        raw = jnp.concatenate([dq, dk, dv, jnp.zeros((128, 64), F32)], axis=1)
        scaled = raw * wide(sine, s)
        turned = jnp.where(first, pltpu.roll(scaled, 608, 1), -pltpu.roll(scaled, 32, 1))
        grad = jnp.where(turns, raw * wide(cosine, s) + turned, raw).astype(BF)
        qkv[rows(s), :] = grad
        bias[0:1, :] += jnp.sum(grad.astype(F32), axis=0, keepdims=True)

    rs_small(0, 2)
    w_qkv = jnp.concatenate([unit(QKV + i) for i in range(5)], axis=1)
    da2[...] = dot_t(qkv[...], w_qkv)
    rs_fold(DOWN)
    rs_fold(OUT)
    rs_small(1, 3)
    for h in range(2):
        unspread_rows(h)
    a_swap = to_sibling(yrec.at[other], arec, 13)
    a_swap.start()
    rs_small(0, 1)
    a2st[...] = a1s[...].T
    for i in range(4):
        part = dot(a2st[...], qkv[:, 128 * i:128 * i + 128])
        u_buf[QKV + i] = part.astype(BF).reshape((2,) * 6 + (16, 128))
    rs_small(1, 2)
    a_swap.wait()
    for s in range(2):
        at = pl.ds(pl.multiple_of(core * 256 + 128 * s, 128), 128)
        da = yrec[at, :] + arec[pl.ds(128 * s, 128), :]
        v = x_all[at, :].astype(F32)
        r = inv_root(v)
        gain[2:3, :] += jnp.sum(da * v * r, axis=0, keepdims=True)
        w = da * gain[0:1, :]
        gtok_ref[pl.ds(128 * s, 128), :] = (
            darec[at, :] + r * w
            - v * (r * r * r) * jnp.mean(w * v, axis=-1, keepdims=True)).astype(BF)
    rs_small(0, 0)
    top = dot(jnp.concatenate([gain[2:4, :], jnp.zeros((14, 896), F32)], axis=0).astype(BF),
              spread[...])
    spot = jnp.where(choose, jnp.broadcast_to(bias[0:1, :], (16, 640)), 0.0).astype(BF)
    hit = (lax.broadcasted_iota(jnp.int32, (1024, 640), 0) == brow[core, 0:1, :]).astype(BF)
    low = dot_t(spot, hit)
    small = jnp.concatenate(
        [jnp.zeros((64, 1024), F32), top, low, jnp.zeros((32, 1024), F32)], axis=0).T
    part = dot(a2st[...], qkv[:, 512:640]) + small
    u_buf[49] = part.astype(BF).reshape((2,) * 6 + (16, 128))
    rs_head(2)
    rs_small(1, 1)
    rs_small_end(0)
    rs_head(1)
    rs_small(1, 0)
    rs_head(0)
    rs_small_end(1)
    last_swap(0).start()
    rs_head_end()
    last_swap(1).start()
    rs_sent()
    for i in range(2):
        last_swap(i).wait()


def layer(*arrays):
    dma = pltpu.SemaphoreType.DMA
    vm = pltpu.VMEM
    return pl.pallas_call(
        layer_kernel,
        out_shape=(
            jax.ShapeDtypeStruct((256, 896), BF),
            jax.ShapeDtypeStruct((256, 896), BF),
            jax.ShapeDtypeStruct((UNITS + TALL, 16, 128), F32),
            jax.ShapeDtypeStruct((UNITS, 16, 128), BF),
        ),
        in_specs=[pl.BlockSpec(memory_space=vm)] * 10 + [pl.BlockSpec(memory_space=pl.ANY)] * 6
        + [pl.BlockSpec(memory_space=vm)] * 4,
        out_specs=[pl.BlockSpec(memory_space=vm)] * 4,
        scratch_shapes=[
            vm((UNITS,) + (2,) * 6 + (16, 128), BF), vm((TALL,) + (2,) * 6 + (16, 128), BF),
            vm((QKV,) + (2,) * 5 + (16, 128), BF), vm((TALL,) + (2,) * 5 + (16, 128), BF),
            vm((2432, 896), BF), vm((512, 896), BF), vm((512, 896), BF), vm((2, 8, 128), F32),
            vm((UNITS, 16, 128), BF), vm((512, 1024), BF), vm((512, 1024), BF),
            vm((1024, 512), BF), vm((512, 640), BF), vm((512, 512), BF),
            vm((512, 896), F32), vm((512, 896), F32), vm((512, 896), F32), vm((512, 1024), F32),
            vm((512, 896), F32), vm((256, 896), F32), vm((256, 896), F32), vm((512, 128), F32), vm((512, 128), F32),
            vm((8, 896), F32), vm((8, 640), F32), vm((UNITS, 16, 128), BF),
            vm((8, RAW), F32), vm((48, 128), F32), vm((UNITS, 16, 128), BF),
            vm((UNITS, 16, 128), BF), vm((8, 128), F32), vm((896, 1024), BF), vm((2, 448, 512), BF),
            vm((304, 304), BF), vm((304, 304), BF),
            vm((3, 5, 16, 128), BF), vm((3, 5) + (2,) * 2 + (16, 128), BF),
            vm((3, 5) + (2,) * 4 + (16, 128), BF),
            dma((4, 6, 2)), dma((4, 6, 3)), dma((4, 3)), dma((5, 2, 6)), dma((5, 2, 6)),
            dma((5, 2, 6)), dma((3, 3, 3)), dma((3, 3, 3)), dma((3,)),
            pltpu.SemaphoreType.REGULAR((7, 6)),
            dma((21,)), dma((21,)), dma((6,)),
        ],
        compiler_params=pltpu.CompilerParams(collective_id=0, has_side_effects=True,
                                             vmem_limit_bytes=60 * 2**20),
    )(*arrays)


def finish_kernel(own, sib, out, tok, out_ref, tok_ref, q_ref, k_ref, v_ref, o_ref, g_ref, u_ref,
                  d_ref, gain_ref, bias_ref):
    out_ref[...] = out[...]
    tok_ref[...] = tok[...]
    for c in range(7):
        for r in range(2):
            d_ref[16 * r:16 * r + 16, 128 * c:128 * c + 128] = own[UNITS + 2 * c + r]
    ends = jnp.concatenate([own[UNITS + 14 + r] for r in range(3)], axis=0)
    for c in range(7):
        d_ref[32:38, 128 * c:128 * c + 128] = ends[6 * c:6 * c + 6]
    core = lax.axis_index("dp") % 2
    for c in range(2):
        @pl.when(core == c)
        def _():
            def mine(u):
                return own[u, 8 * c:8 * c + 8, :]

            def theirs(u):
                return sib[u].astype(F32)[8 * c:8 * c + 8]

            def half(plane, u, h):
                return (mine if plane == c else theirs)(u)[:, 64 * h:64 * h + 64]

            def put(ref, count, where):
                for n in range(count):
                    (p0, u0, h0), (p1, u1, h1) = where(2 * n), where(2 * n + 1)
                    if (p0, u0, h0, h1) == (p1, u1, 0, 1):
                        v = (mine if p0 == c else theirs)(u0)
                    else:
                        v = jnp.concatenate([half(p0, u0, h0), half(p1, u1, h1)], axis=1)
                    ref[:, 128 * n:128 * n + 128] = v[0:7]

            def hidden(table):
                def where(h):
                    t = h // 38 * 19 + h % 19
                    return h // 19 % 2, table[t // 2], t % 2
                return where

            put(g_ref, 38, hidden(GATE_UNITS))
            put(u_ref, 38, hidden(UP_UNITS))
            put(q_ref, 7, lambda h: (h // 7, QKV + h % 7 // 2, h % 7 % 2))
            put(k_ref, 1, lambda h: (h, QKV + 3, 1))
            put(v_ref, 1, lambda h: (h, QKV + 4, 0))
            for j, u in enumerate(OUT_UNITS):
                o_ref[:, 128 * j:128 * j + 128] = (mine(u) + theirs(u))[0:7]
            small = mine(QKV + 4) + theirs(QKV + 4)
            gain_ref[...] = small.T[64:66, 0:7]
            bias_ref[...] = small[0:1, 80:89]


def finish(own, sib, out, tok):
    vm = pl.BlockSpec(memory_space=pltpu.VMEM)
    shapes = [((256, 896), BF), ((256, 896), BF), ((7, 896), F32), ((7, 128), F32),
              ((7, 128), F32), ((7, 896), F32), ((7, 4864), F32), ((7, 4864), F32),
              ((38, 896), F32), ((2, 7), F32), ((1, 9), F32)]
    return pl.pallas_call(
        finish_kernel,
        out_shape=tuple(jax.ShapeDtypeStruct(s, d) for s, d in shapes),
        in_specs=[vm] * 4, out_specs=[vm] * 11,
    )(own, sib, out, tok)


def constants():
    slots = np.zeros(128, np.int32)
    for n in range(128):
        dp, fs = n // 32, n % 32
        x, y, z, core = fs // 4 % 4, fs % 4, (dp // 2) * 2 + fs // 16, dp % 2
        slots[n] = ((GRAY[x] * 4 + GRAY[y]) * 4 + GRAY[z]) * 2 + core
    spread = np.zeros((896, 1024), np.float32)
    for d in range(896):
        spread[d, slots[d // 7] * 8 + d % 7] = 1.0
    spread_o = np.zeros((2, 448, 512), np.float32)
    for c in range(2):
        part = spread[448 * c:448 * c + 448].reshape(448, 16, 2, 32)
        spread_o[c] = part[:, :, c].reshape(448, 512)
    unpack = np.zeros((304, 304), np.float32)
    pick_in = np.zeros((336, 384), np.float32)
    for a in range(8):
        for r in range(38):
            unpack[32 * a + r if r < 32 else 256 + 6 * a + r - 32, 38 * a + r] = 1.0
        for r in range(6):
            for c in range(7):
                pick_in[48 * c + 6 * a + r, 48 * a + 6 * c + r] = 1.0
    brow = np.full((2, 8, 640), -1, np.int32)
    for c in range(2):
        for i in range(576):
            if i < 448:
                nat = 448 * c + i
            elif i < 512:
                nat = 896 + 64 * c + i - 448
            else:
                nat = 1024 + 64 * c + i - 512
            brow[c, 0, i] = slots[nat // 9] * 8
            brow[c, 1, i] = nat % 9
    freq = THETA ** (-2.0 * (np.arange(128) % 32) / 64.0)
    freq = np.concatenate([freq[None], np.zeros((7, 128))]).astype(np.float32)
    return (jnp.asarray(spread, BF), jnp.asarray(spread_o, BF), jnp.asarray(unpack.T, BF),
            jnp.asarray(unpack, BF), jnp.asarray(pick_in, BF), jnp.asarray(pick_in.T, BF),
            jnp.asarray(brow), jnp.asarray(freq))


def shards(tokens, segments, w_query, w_key, w_value, w_out, w_gate, w_up, w_down, gains, biases,
           cotangent):
    out, tok, own, sib = layer(
        w_query, w_key, w_value, w_out, w_gate, w_up, w_down, gains.T, biases.reshape(1, 9),
        segments.reshape(2, 128), tokens.reshape(256, 896), cotangent.reshape(256, 896),
        *constants())
    out, tok, *grads, gain, bias = finish(own, sib, out, tok)
    return (out.reshape(tokens.shape), tok.reshape(tokens.shape), *grads, gain.T,
            bias.reshape(9))


def solution(mesh):
    row = P(AXES, None)
    batch = P(None, AXES, None, None)
    return jax.shard_map(
        shards, mesh=mesh,
        in_specs=(batch, P(None, AXES, None)) + (row,) * 8 + (P(AXES), batch),
        out_specs=(batch, batch) + (row,) * 8 + (P(AXES),),
        check_vma=False,
    )
```
